32 devices in a mesh: wide: 8 (over y, x, core), narrow: 4 (over z).
Axes of the slice: x: 2, y: 2, z: 4, core: 2. Of those that a mesh axis runs over, the one named last changes fastest.
Arguments:
- tokens: bfloat16 [49152, 512], P(('wide', 'narrow')), may hold values from -20 to 20
- segment: int32 [49152], P(('wide', 'narrow')), may hold values from 0 to 1535, as said below
- w_query: bfloat16 [512, 512], P(('wide', 'narrow')), may hold values from -0.25 to 0.25
- w_key: bfloat16 [512, 512], P(('wide', 'narrow')), may hold values from -0.25 to 0.25
- w_value: bfloat16 [512, 512], P(('wide', 'narrow')), may hold values from -0.25 to 0.25
- w_output: bfloat16 [512, 512], P(('wide', 'narrow')), may hold values from -1 to 1
- gate_attn: bfloat16 [512, 512], P(('wide', 'narrow')), may hold values from -0.25 to 0.25
- gate_ffn: bfloat16 [512, 512], P(('wide', 'narrow')), may hold values from -0.25 to 0.25
- w_in: bfloat16 [512, 2048], P(('wide', 'narrow')), may hold values from -0.25 to 0.25
- w_out: bfloat16 [2048, 512], P(('wide', 'narrow')), may hold values from -0.125 to 0.125
- norm_attn: bfloat16 [512], P(('wide', 'narrow')), may hold values from 0.5 to 1.5
- norm_ffn: bfloat16 [512], P(('wide', 'narrow')), may hold values from 0.5 to 1.5
- bias_attn: bfloat16 [512], P(('wide', 'narrow')), may hold values from -3 to 3
- bias_ffn: bfloat16 [512], P(('wide', 'narrow')), may hold values from -3 to 3
- out_grad: bfloat16 [49152, 512], P(('wide', 'narrow')), may hold values from -6 to 6
Outputs:
- result: bfloat16 [49152, 512], P(('wide', 'narrow'))
- token_grad: float32 [49152, 512], P(('wide', 'narrow'))
- grad_query: float32 [512, 512], P(('wide', 'narrow'))
- grad_key: float32 [512, 512], P(('wide', 'narrow'))
- grad_value: float32 [512, 512], P(('wide', 'narrow'))
- grad_output: float32 [512, 512], P(('wide', 'narrow'))
- grad_gate_attn: float32 [512, 512], P(('wide', 'narrow'))
- grad_gate_ffn: float32 [512, 512], P(('wide', 'narrow'))
- grad_in: float32 [512, 2048], P(('wide', 'narrow'))
- grad_out: float32 [2048, 512], P(('wide', 'narrow'))
- grad_norm_attn: float32 [512], P(('wide', 'narrow'))
- grad_norm_ffn: float32 [512], P(('wide', 'narrow'))
- grad_bias_attn: float32 [512], P(('wide', 'narrow'))
- grad_bias_ffn: float32 [512], P(('wide', 'narrow'))
- gate_stats: float32 [4, 512], replicated
The draws below stay inside these ranges and needn't reach their ends.
Inputs may be any that keep to these rules, and one draw needn't show every extreme that they name: `segment`: each token's number is the position, within its device's 1536 tokens, of the first token of its sequence; tokens with one number form one sequence of consecutive tokens; no sequence crosses a device; short sequences have at most 128 tokens, and some devices (at least one in every draw, which ones drawn) hold one sequence of exactly 1024 tokens, the longest.
All inputs are finite; a program needn't handle non-finite values.
Results may differ from the reference program's by a relative error of at most 0.015.
Values may be sent and summed in bfloat16 or wider, within the bound.
No kernel may reach another device: no remote copies, remote signals or barrier semaphores. Data moves between devices by JAX's collectives and lax.ppermute only.
A program may use at most 384 MiB of HBM per device.

```python
import jax
import jax.numpy as jnp
from jax import lax

HEADS = 8
HEAD_DIM = 64
D = 512
FF = 2048
TOK_DEV = 1536
SHORT_MOST = 128
LONGEST = 1024
TOKENS = 49152
N_WIDE = 8
N_NARROW = 4


def draw_tokens(key, part):
    key = jax.random.fold_in(key, 23)
    device_count = N_WIDE * N_NARROW
    noise_key, course_key = jax.random.split(key, 2)
    course = jnp.clip(jax.random.normal(course_key, (D,), jnp.float32), -2.5, 2.5)
    ramp = jnp.arange(device_count, dtype=jnp.float32) / max(device_count - 1, 1)
    noise = jnp.clip(jax.random.normal(noise_key, (TOKENS, D), jnp.float32), -4.0, 4.0)
    strength = 1.0 + 3.0 * ramp
    per_row = jnp.repeat(strength, TOK_DEV)
    values = noise + per_row[:, None] * course[None, :]
    return values.astype(jnp.bfloat16)


def draw_segment(key, part):
    key = jax.random.fold_in(key, 11)
    device_count = N_WIDE * N_NARROW
    holder_key, picker_key, start_key, cutter_key = jax.random.split(key, 4)
    holder = jax.random.randint(holder_key, (device_count,), 0, 2)
    chosen = jax.random.randint(picker_key, (), 0, device_count)
    device_ids = jnp.arange(device_count)
    holder = jnp.maximum(holder, (device_ids == chosen).astype(jnp.int32))
    spared = (chosen + 1) % device_count
    holder = holder * (device_ids != spared).astype(jnp.int32)
    starts = jax.random.randint(start_key, (device_count,), 0, TOK_DEV - LONGEST + 1)
    cutter = jax.random.randint(cutter_key, (device_count, TOK_DEV), 0, SHORT_MOST) == 0
    places = jnp.arange(TOK_DEV)[None, :]
    begins = starts[:, None]
    holding = holder[:, None] == 1
    inside = holding & (places >= begins) & (places < begins + LONGEST)
    border = (places % SHORT_MOST == 0) | cutter
    bounds = jnp.where(inside, places == begins, border)
    bounds = bounds | holding & (places == begins + LONGEST)
    bounds = bounds | jnp.logical_not(holding) & (places == TOK_DEV - 1)
    bounds = bounds | (places == 0)
    marked = jnp.where(bounds, jnp.broadcast_to(places, bounds.shape), 0).astype(jnp.int32)
    segment_ids = lax.cummax(marked, axis=1)
    return segment_ids.reshape(device_count * TOK_DEV).astype(jnp.int32)


def level_of(key, dims, shards, low, high):
    level, own = 1.0, jax.random.fold_in(key, 6)
    for axis_at, parts in shards:
        heights = jnp.exp(jax.random.uniform(jax.random.fold_in(own, axis_at), (parts,), jnp.float32, low / len(shards), high / len(shards)))
        level = level * jnp.repeat(heights, dims[axis_at] // parts).reshape([-1 if axis == axis_at else 1 for axis in range(len(dims))])
    return level


def bell_draw(stream_key, dims, scale, limit, shards=(), held_as=jnp.bfloat16):
    result = jax.random.normal(stream_key, dims, jnp.float32) * scale
    if len(shards) > 0:
        result = level_of(stream_key, dims, shards, -0.22, 0.18) * result
    return jnp.clip(result, min=-limit, max=limit).astype(held_as)


def setup_inputs(seed: int = 0) -> dict:
    seeds = jax.random.split(jax.random.key(seed), 16)
    return {
        "tokens": draw_tokens(jax.random.fold_in(seeds[15], 71), 0),
        "segment": draw_segment(jax.random.fold_in(seeds[15], 71), 0),
        "w_query": bell_draw(seeds[2], (D, D), D ** -0.5, 0.25, ((0, 32),)),
        "w_key": bell_draw(seeds[3], (D, D), D ** -0.5, 0.25, ((0, 32),)),
        "w_value": bell_draw(seeds[4], (D, D), D ** -0.5, 0.25, ((0, 32),)),
        "w_output": bell_draw(seeds[5], (D, D), (D // 16) ** -0.5, 1.0, ((0, 32),)),
        "gate_attn": bell_draw(seeds[6], (D, D), D ** -0.5, 0.25, ((0, 32),)),
        "gate_ffn": bell_draw(seeds[7], (D, D), D ** -0.5, 0.25, ((0, 32),)),
        "w_in": bell_draw(seeds[8], (D, FF), D ** -0.5, 0.25, ((0, 32),)),
        "w_out": bell_draw(seeds[9], (FF, D), FF ** -0.5, 0.125, ((0, 32),)),
        "norm_attn": jnp.clip(1.0 + 0.1 * jax.random.normal(seeds[10], (D,), jnp.float32), 0.5, 1.5).astype(jnp.bfloat16),
        "norm_ffn": jnp.clip(1.0 + 0.1 * jax.random.normal(seeds[11], (D,), jnp.float32), 0.5, 1.5).astype(jnp.bfloat16),
        "bias_attn": bell_draw(seeds[12], (D,), 0.5, 3.0, ((0, 32),)),
        "bias_ffn": bell_draw(seeds[13], (D,), 0.5, 3.0, ((0, 32),)),
        "out_grad": bell_draw(seeds[14], (TOKENS, D), 1.0, 6.0, ((0, 32),)),
    }


EPSILON = 1e-05
MASKED = -1000000000.0

@jax.custom_vjp
def low(v):
    return lax.optimization_barrier(v.astype(jnp.bfloat16)).astype(jnp.float32)

@jax.custom_vjp
def low_back(v):
    return v

def low_keep(v):
    return (low(v), None)

def low_pass(kept, grad):
    return (grad,)

def back_keep(v):
    return (v, None)

def back_low(kept, grad):
    return (low(grad),)
low.defvjp(low_keep, low_pass)
low_back.defvjp(back_keep, back_low)

def matmul(left, right):
    return jnp.dot(left, right, precision=lax.Precision.HIGHEST)

def layer_norm(values, gain):
    center = lax.optimization_barrier(jnp.mean(values, axis=-1, keepdims=True))
    offset = values - center
    spread = lax.optimization_barrier(jnp.mean(offset * offset, axis=-1, keepdims=True))
    return offset * lax.rsqrt(spread + EPSILON) * gain

def attend_block(queries, keys, values, seg_query, seg_key, start):
    count = queries.shape[0]
    scaled = jnp.einsum('qhd,khd->hqk', queries, keys, precision=lax.Precision.HIGHEST) * HEAD_DIM ** (-0.5)
    scores = low_back(scaled)
    query_place = start + jnp.arange(count, dtype=jnp.int32)
    key_place = jnp.arange(keys.shape[0], dtype=jnp.int32)
    allowed = (query_place[:, None] >= key_place[None, :]) & (seg_query[:, None] == seg_key[None, :])
    scores = jnp.where(allowed[None], scores, MASKED)
    weights = low(jax.nn.softmax(scores, axis=-1))
    return jnp.einsum('hqk,khd->qhd', weights, values, precision=lax.Precision.HIGHEST)

def device_layer(params, inputs, segment):
    w_query, w_key, w_value, w_output, gate_attn, gate_ffn, w_in, w_out, norm_attn, norm_ffn, bias_attn, bias_ffn = params
    length = inputs.shape[0]
    normed = low(layer_norm(inputs, norm_attn))

    def project(weight):
        return low(low_back(matmul(normed, weight))).reshape(length, HEADS, HEAD_DIM)
    queries = project(w_query)
    keys = project(w_key)
    values = project(w_value)
    half_rows = length // 2
    query_blocks = queries.reshape(2, half_rows, HEADS, HEAD_DIM)
    segment_blocks = segment.reshape(2, half_rows)
    starts = jnp.arange(2, dtype=jnp.int32) * half_rows

    def one_block(item):
        return jax.checkpoint(attend_block)(item[0], keys, values, item[1], segment, item[2])
    mixed = lax.map(one_block, (query_blocks, segment_blocks, starts)).reshape(length, HEADS * HEAD_DIM)
    mixed = low(low_back(mixed))
    branch = low_back(matmul(mixed, w_output))
    gate_one = jax.nn.sigmoid(low_back(matmul(normed, gate_attn)) + bias_attn)
    middle = inputs + gate_one * branch
    second = low(layer_norm(middle, norm_ffn))
    gate_two = jax.nn.sigmoid(low_back(matmul(second, gate_ffn)) + bias_ffn)
    inner = low_back(matmul(second, w_in))
    hidden = low(jax.nn.gelu(inner, approximate=True))
    feed = low_back(matmul(hidden, w_out))
    output = middle + gate_two * feed
    moments = jnp.stack([lax.optimization_barrier(jnp.sum(gate_one, axis=0)), lax.optimization_barrier(jnp.sum(gate_one * gate_one, axis=0)), lax.optimization_barrier(jnp.sum(gate_two, axis=0)), lax.optimization_barrier(jnp.sum(gate_two * gate_two, axis=0))])
    return (output, moments)

def reference(tokens, segment, w_query, w_key, w_value, w_output, gate_attn, gate_ffn, w_in, w_out, norm_attn, norm_ffn, bias_attn, bias_ffn, out_grad):
    params = tuple((item.astype(jnp.float32) for item in (w_query, w_key, w_value, w_output, gate_attn, gate_ffn, w_in, w_out, norm_attn, norm_ffn, bias_attn, bias_ffn)))
    device_count = N_WIDE * N_NARROW
    inputs = tokens.astype(jnp.float32).reshape(device_count, TOK_DEV, D)
    segments = segment.reshape(device_count, TOK_DEV)
    cotangents = out_grad.astype(jnp.float32).reshape(device_count, TOK_DEV, D)

    def step(carry, item):
        grads, moments = carry
        rows_in, rows_seg, rows_cot = item
        output, pull, part = jax.vjp(lambda p, v: device_layer(p, v, rows_seg), params, rows_in, has_aux=True)
        grad_params, grad_rows = pull(rows_cot)
        grads = jax.tree.map(jnp.add, grads, grad_params)
        return ((grads, moments + part), (output.astype(jnp.bfloat16), grad_rows))
    start_carry = (jax.tree.map(jnp.zeros_like, params), jnp.zeros((4, D), jnp.float32))
    (grads, moments), (outputs, grad_inputs) = lax.scan(step, start_carry, (inputs, segments, cotangents))
    mean_one = moments[0] / TOKENS
    mean_two = moments[2] / TOKENS
    gate_stats = jnp.stack([mean_one, moments[1] / TOKENS - mean_one * mean_one, mean_two, moments[3] / TOKENS - mean_two * mean_two])
    return (outputs.reshape(TOKENS, D), grad_inputs.reshape(TOKENS, D), grads[0], grads[1], grads[2], grads[3], grads[4], grads[5], grads[6], grads[7], grads[8], grads[9], grads[10], grads[11], gate_stats)
```

```python
from functools import partial

import jax
import jax.numpy as jnp
from jax import lax
from jax.experimental import pallas as pl
from jax.experimental.pallas import tpu as pltpu
from jax.sharding import PartitionSpec as P

HEADS = 8
HEAD_DIM = 64
EPSILON = 1e-05
MASKED = -1000000000.0
AXES = ("wide", "narrow")
BF = jnp.bfloat16
F32 = jnp.float32
MIB = 1 << 20
VMEM = 60 * MIB
BLOCK = 256
ROWS = 16
BLOCKS = 32
FIRST = 1536 + 128
REST = 5632
SUMS = 384


def dot(left, right):
    return jnp.dot(left, right, preferred_element_type=F32)


def dot_t(left, right):
    return lax.dot_general(left, right, (((1,), (1,)), ((), ())), preferred_element_type=F32)


def t_dot(left, right):
    return lax.dot_general(left, right, (((0,), (0,)), ((), ())), preferred_element_type=F32)


def row_mean(values):
    return jnp.mean(values, axis=-1, keepdims=True)


def normalise(values):
    offset = values - row_mean(values)
    scale = lax.rsqrt(row_mean(offset * offset) + EPSILON)
    return offset * scale, scale


def sigmoid(values):
    return 1.0 / (1.0 + jnp.exp(-values))


def project_kernel(
    order, tokens, *refs
):
    pieces, refs = refs[:8], refs[8:]
    normed, normed_t, query, key, value, key_t, value_t, weights, small, held, sem = refs
    step = pl.program_id(0)

    @pl.when(step == 0)
    def _():
        for at in range(BLOCKS):
            place = pl.multiple_of(order[at] * ROWS, ROWS)
            pltpu.make_async_copy(
                pieces[at // 4].at[pl.ds(at % 4 * ROWS, ROWS)], held.at[pl.ds(place, ROWS)], sem
            ).start()

    unit, _ = normalise(tokens[...].astype(F32))

    @pl.when(step == 0)
    def _():
        pltpu.make_async_copy(held, held, sem).wait()
        total = jnp.zeros((ROWS, 128), F32)
        for at in range(BLOCKS):
            total = total + held[pl.ds(at * ROWS, ROWS), 1536:FIRST].astype(F32)
        for vector in range(4):
            for part in range(4):
                small[vector : vector + 1, part * 128 : (part + 1) * 128] = total[
                    vector * 4 + part : vector * 4 + part + 1
                ]
        weights[...] = held[:, :1536]

    low = (unit * small[0:1, :]).astype(BF)
    normed[...] = low
    normed_t[...] = low.T
    query[...] = (dot(low, held[:, :512]).astype(BF).astype(F32) * HEAD_DIM**-0.5).astype(BF)
    keys = dot(low, held[:, 512:1024]).astype(BF)
    key[...] = keys
    key_t[...] = keys.T
    values = dot(low, held[:, 1024:1536]).astype(BF)
    value[...] = values
    value_t[...] = values.T


def project(order, tokens, pieces):
    length, width = tokens.shape
    tile = 512
    by_rows = pl.BlockSpec((tile, width), lambda i: (i, 0))
    by_columns = pl.BlockSpec((width, tile), lambda i: (0, i))
    whole = lambda *shape: pl.BlockSpec(shape, lambda i: (0,) * len(shape))
    rows = jax.ShapeDtypeStruct((length, width), BF)
    columns = jax.ShapeDtypeStruct((width, length), BF)
    return pl.pallas_call(
        project_kernel,
        grid=(length // tile,),
        in_specs=[
            pl.BlockSpec(memory_space=pltpu.SMEM),
            by_rows,
        ] + [pl.BlockSpec(memory_space=pl.ANY)] * 8,
        out_specs=[
            by_rows, by_columns, by_rows, by_rows, by_rows, by_columns, by_columns,
            whole(width, 1536), whole(4, width),
        ],
        out_shape=[
            rows, columns, rows, rows, rows, columns, columns,
            jax.ShapeDtypeStruct((width, 1536), BF),
            jax.ShapeDtypeStruct((4, width), F32),
        ],
        scratch_shapes=[pltpu.VMEM((width, FIRST), BF), pltpu.SemaphoreType.DMA],
        compiler_params=pltpu.CompilerParams(vmem_limit_bytes=VMEM),
        cost_estimate=pl.CostEstimate(
            flops=6 * length * width * width, bytes_accessed=12 * MIB, transcendentals=length
        ),
        name="project",
    )(order, tokens, *pieces)


def bias_of(segment_row, key_block, query_block):
    key_at = key_block * BLOCK + lax.broadcasted_iota(jnp.int32, (BLOCK, BLOCK), 0)
    query_at = query_block * BLOCK + lax.broadcasted_iota(jnp.int32, (BLOCK, BLOCK), 1)
    return jnp.where((key_at >= segment_row) & (key_at <= query_at), 0.0, MASKED)


def keep_head(pair, head):
    lane = lax.broadcasted_iota(jnp.int32, pair.shape, 1)
    own = (lane >= HEAD_DIM) if head % 2 else (lane < HEAD_DIM)
    return jnp.where(own, pair, jnp.zeros_like(pair))


def attend_kernel(
    segment, segment_row, query, key, value_t, mixed, log_total, masked_query, peak, total, mix
):
    step = pl.program_id(0)
    for head in range(HEADS):
        pair = pl.ds(head // 2 * 128, 128)
        masked_query[head] = keep_head(query[:, pair], head)
    peak[...] = jnp.full(peak.shape, -1e30, F32)
    total[...] = jnp.zeros(total.shape, F32)
    mix[...] = jnp.zeros(mix.shape, F32)
    seen = segment_row[...]

    def visit(block, _):
        bias = bias_of(seen, block, step)
        rows = pl.ds(pl.multiple_of(block * BLOCK, BLOCK), BLOCK)
        heads = range(HEADS)
        pair = lambda head: pl.ds(head // 2 * 128, 128)
        own = lambda head: pl.ds(head * HEAD_DIM, HEAD_DIM)
        scores = [dot_t(key[rows, pair(h)], masked_query[h]) + bias for h in heads]
        old = [peak[h : h + 1, :] for h in heads]
        new = [jnp.maximum(o, jnp.max(s, axis=0, keepdims=True)) for o, s in zip(old, scores)]
        power = [jnp.exp(s - n) for s, n in zip(scores, new)]
        fade = [jnp.exp(o - n) for o, n in zip(old, new)]
        added = [jnp.sum(p, axis=0, keepdims=True) for p in power]
        high = [p.astype(BF) for p in power]
        rest = [(p - x.astype(F32)).astype(BF) for p, x in zip(power, high)]
        mixes = [
            mix[own(h), :] * fade[h] + dot(value_t[own(h), rows], high[h]) + dot(value_t[own(h), rows], rest[h])
            for h in heads
        ]
        for h in heads:
            peak[h : h + 1, :] = new[h]
            total[h : h + 1, :] = total[h : h + 1, :] * fade[h] + added[h]
            mix[own(h), :] = mixes[h]
        return 0

    first = lax.div(segment[step * BLOCK], BLOCK)
    lax.fori_loop(first, step + 1, visit, 0)
    log_total[...] = peak[...] + jnp.log(total[...])
    for head in range(HEADS):
        own = pl.ds(head * HEAD_DIM, HEAD_DIM)
        mix[own, :] = mix[own, :] / total[head : head + 1, :]
    mixed[...] = mix[...].T


def attend(segment, segment_row, query, key, value_t):
    length, width = query.shape
    whole = lambda *shape: pl.BlockSpec(shape, lambda i, s: (0,) * len(shape))
    return pl.pallas_call(
        attend_kernel,
        grid_spec=pltpu.PrefetchScalarGridSpec(
            num_scalar_prefetch=1,
            grid=(length // BLOCK,),
            in_specs=[
                pl.BlockSpec((1, BLOCK), lambda i, s: (0, i)),
                pl.BlockSpec((BLOCK, width), lambda i, s: (i, 0)),
                whole(length, width),
                whole(width, length),
            ],
            out_specs=[
                pl.BlockSpec((BLOCK, width), lambda i, s: (i, 0)),
                pl.BlockSpec((HEADS, BLOCK), lambda i, s: (0, i)),
            ],
            scratch_shapes=[
                pltpu.VMEM((HEADS, BLOCK, 128), BF),
                pltpu.VMEM((HEADS, BLOCK), F32),
                pltpu.VMEM((HEADS, BLOCK), F32),
                pltpu.VMEM((width, BLOCK), F32),
            ],
        ),
        out_shape=[
            jax.ShapeDtypeStruct((length, width), F32),
            jax.ShapeDtypeStruct((HEADS, length), F32),
        ],
        compiler_params=pltpu.CompilerParams(vmem_limit_bytes=VMEM),
        cost_estimate=pl.CostEstimate(
            flops=16 * length * length * width // 2, bytes_accessed=6 * MIB, transcendentals=8 * length * length // 2
        ),
        name="attend",
    )(segment, segment_row, query, key, value_t)


def attend_back_kernel(
    me, segment, segment_row, query, key, value, key_t, grad_mixed, log_total, inner_sum, normed_t, _after,
    grad_query, grad_key, grad_value, send, keep,
    masked_query, masked_grad, query_sum, key_sum, value_sum, whole_query, staged, sems,
    *, heads,
):
    step = pl.program_id(0)
    last = pl.num_programs(0) - 1
    width = heads * HEAD_DIM

    @pl.when(step == 0)
    def _():
        key_sum[...] = jnp.zeros(key_sum.shape, F32)
        value_sum[...] = jnp.zeros(value_sum.shape, F32)

    for head in range(heads):
        pair = pl.ds(head // 2 * 128, 128)
        masked_query[head] = keep_head(query[:, pair], head)
        masked_grad[head] = keep_head(grad_mixed[:, pair], head)
    query_sum[...] = jnp.zeros(query_sum.shape, F32)
    seen = segment_row[...]

    def visit(block, _):
        bias = bias_of(seen, block, step)
        rows = pl.ds(pl.multiple_of(block * BLOCK, BLOCK), BLOCK)
        every = range(heads)
        pair = lambda head: pl.ds(head // 2 * 128, 128)
        own = lambda head: pl.ds(head * HEAD_DIM, HEAD_DIM)
        scores = [dot_t(key[rows, pair(h)], masked_query[h]) for h in every]
        grad_probs = [dot_t(value[rows, pair(h)], masked_grad[h]) for h in every]
        probs = [jnp.exp((s + bias) - log_total[0, h : h + 1, :]) for h, s in enumerate(scores)]
        grad_scores = [
            (p * (g - inner_sum[0, h : h + 1, :])).astype(BF)
            for h, (p, g) in enumerate(zip(probs, grad_probs))
        ]
        to_value = [dot(p.astype(BF), masked_grad[h]) for h, p in enumerate(probs)]
        to_key = [dot(g, masked_query[h]) for h, g in enumerate(grad_scores)]
        to_query = [dot(key_t[own(h), rows], g) for h, g in enumerate(grad_scores)]
        for h in range(0, heads, 2):
            value_sum[rows, pair(h)] += to_value[h] + to_value[h + 1]
            key_sum[rows, pair(h)] += to_key[h] + to_key[h + 1]
        for h in every:
            query_sum[own(h), :] += to_query[h]
        return 0

    first = lax.div(segment[step * BLOCK], BLOCK)
    lax.fori_loop(first, step + 1, visit, 0)
    finished = (query_sum[...].T * HEAD_DIM**-0.5).astype(BF)
    grad_query[...] = finished
    whole_query[pl.ds(pl.multiple_of(step * BLOCK, BLOCK), BLOCK), :] = finished

    @pl.when(step == last)
    def _():
        low_key = key_sum[...].astype(BF)
        low_value = value_sum[...].astype(BF)
        grad_key[...] = low_key
        grad_value[...] = low_value
        staged[:, :width] = dot(normed_t[...], whole_query[...]).astype(BF)
        staged[:, width : 2 * width] = dot(normed_t[...], low_key).astype(BF)
        staged[:, 2 * width :] = dot(normed_t[...], low_value).astype(BF)
        hand_out(me[0], [(staged, 1, 0)], send, keep, sems)


def device_at(me, half, at):
    plane, line = at // 4, at % 4
    return jnp.bitwise_xor(me, (plane * 2 + half) * 4 + line)


def hand_out(me, parts, send, keep, sems):
    for half, target in enumerate((keep, send)):
        for at in range(BLOCKS // 2):
            owner = device_at(me, half, at)
            for source, groups, column in parts:
                wide = source.shape[1]
                if groups == 0:
                    pltpu.make_async_copy(
                        source, target.at[at, :, pl.ds(column, wide)], sems.at[half]
                    ).start()
                for group in range(groups):
                    place = pl.multiple_of(owner * (ROWS * groups) + group * ROWS, ROWS)
                    pltpu.make_async_copy(
                        source.at[pl.ds(place, ROWS)],
                        target.at[at, :, pl.ds(column + group * wide, wide)],
                        sems.at[half],
                    ).start()
    for half, target in enumerate((keep, send)):
        pltpu.make_async_copy(target, target, sems.at[half]).wait()


def attend_back(
    me, segment, segment_row, query, key, value, key_t, grad_mixed, log_total, inner_sum, normed_t,
    after, group, heads,
):
    length, full = query.shape
    width = heads * HEAD_DIM
    groups = HEADS // heads
    by_rows = pl.BlockSpec((BLOCK, width), lambda i, m, s: (i, group))
    columns = pl.BlockSpec((length, width), lambda i, m, s: (0, group))
    per_head = pl.BlockSpec((1, heads, BLOCK), lambda i, m, s: (group, 0, i))
    flat = jax.ShapeDtypeStruct((length, width), BF)
    packet = jax.ShapeDtypeStruct((BLOCKS // 2, ROWS, 3 * width), BF)
    return pl.pallas_call(
        partial(attend_back_kernel, heads=heads),
        grid_spec=pltpu.PrefetchScalarGridSpec(
            num_scalar_prefetch=2,
            grid=(length // BLOCK,),
            in_specs=[
                pl.BlockSpec((1, BLOCK), lambda i, m, s: (0, i)),
                by_rows,
                columns,
                columns,
                pl.BlockSpec((width, length), lambda i, m, s: (group, 0)),
                by_rows,
                per_head,
                per_head,
                pl.BlockSpec((full, length), lambda i, m, s: (0, 0)),
                pl.BlockSpec(memory_space=pl.ANY),
            ],
            out_specs=[
                pl.BlockSpec((BLOCK, width), lambda i, m, s: (i, 0)),
                pl.BlockSpec((length, width), lambda i, m, s: (0, 0)),
                pl.BlockSpec((length, width), lambda i, m, s: (0, 0)),
                pl.BlockSpec(memory_space=pl.ANY),
                pl.BlockSpec(memory_space=pl.ANY),
            ],
            scratch_shapes=[
                pltpu.VMEM((heads, BLOCK, 128), BF),
                pltpu.VMEM((heads, BLOCK, 128), BF),
                pltpu.VMEM((width, BLOCK), F32),
                pltpu.VMEM((length, width), F32),
                pltpu.VMEM((length, width), F32),
                pltpu.VMEM((length, width), BF),
                pltpu.VMEM((full, 3 * width), BF),
                pltpu.SemaphoreType.DMA((2,)),
            ],
        ),
        out_shape=[flat, flat, flat, packet, packet],
        compiler_params=pltpu.CompilerParams(vmem_limit_bytes=VMEM),
        cost_estimate=pl.CostEstimate(
            flops=40 * length * length * width // 2, bytes_accessed=8 * MIB, transcendentals=heads * length * length // 2
        ),
        name=f"attend_back_{group}",
    )(
        me, segment, segment_row, query, key, value, key_t, grad_mixed,
        log_total.reshape(groups, heads, length), inner_sum.reshape(groups, heads, length), normed_t, after,
    )


def feed_kernel(
    me, order, tokens, normed, mixed, out_grad, small, *refs
):
    pieces, refs = refs[:8], refs[8:]
    result, grad_middle, zeta_one_low, grad_mixed, inner_sum, gate_attn_out, send, keep, *refs = refs
    held, held_out, sum_held, sum_out, staged, staged_out, hidden, slope, sums, sums_tile, sems = refs
    step = pl.program_id(0)
    last = pl.num_programs(0) - 1
    features = tokens.shape[1]
    chunks = held_out.shape[0] // features
    straight = 3 * features + chunks * features

    @pl.when(step == 0)
    def _():
        for at in range(BLOCKS):
            source = pieces[at // 4].at[pl.ds(at % 4 * ROWS, ROWS)]
            place = pl.multiple_of(order[at] * ROWS, ROWS)
            pltpu.make_async_copy(
                source.at[:, pl.ds(0, straight)], held.at[pl.ds(place, ROWS)], sems.at[0]
            ).start()
            for group in range(4):
                pltpu.make_async_copy(
                    source.at[:, pl.ds(straight + group * features, features)],
                    held_out.at[pl.ds(place * 4 + group * ROWS, ROWS)],
                    sems.at[1],
                ).start()
        sums[...] = jnp.zeros(sums.shape, F32)
        sum_held[...] = jnp.zeros(sum_held.shape, F32)
        sum_out[...] = jnp.zeros(sum_out.shape, F32)
        pltpu.make_async_copy(held, held, sems.at[0]).wait()
        pltpu.make_async_copy(held_out, held_out, sems.at[1]).wait()
        gate_attn_out[...] = held[:, features : 2 * features]

    w_output = held.at[:, pl.ds(0, features)]
    gate_attn = held.at[:, pl.ds(features, features)]
    gate_ffn = held.at[:, pl.ds(2 * features, features)]
    gain, bias_one, bias_two = small[1:2, :], small[2:3, :], small[3:4, :]

    exact = mixed[...]
    mix = exact.astype(BF)
    branch = dot(mix, w_output[...])
    gate_one = sigmoid(dot(normed[...], gate_attn[...]) + bias_one)
    middle = tokens[...].astype(F32) + gate_one * branch
    unit, scale = normalise(middle)
    second = (unit * gain).astype(BF)
    gate_two = sigmoid(dot(second, gate_ffn[...]) + bias_two)

    feed = jnp.zeros(middle.shape, F32)
    for chunk in range(chunks):
        at = pl.ds(chunk * features, features)
        inner = dot(second, held[:, pl.ds((3 + chunk) * features, features)])
        root = (2.0 / jnp.pi) ** 0.5
        square = inner * inner
        turn = jnp.tanh(inner * (root + (root * 0.044715) * square))
        rise = 0.5 + 0.5 * turn
        value = inner * rise
        slope[:, at] = rise + value * (1.0 - turn) * (root + (3.0 * root * 0.044715) * square)
        low = value.astype(BF)
        hidden[:, at] = low
        feed = feed + dot(low, held_out[at, :])
    result[...] = (middle + gate_two * feed).astype(BF)

    grad = out_grad[...].astype(F32)
    grad_feed = (grad * gate_two).astype(BF)
    zeta_two = grad * feed * gate_two * (1.0 - gate_two)
    zeta_two_low = zeta_two.astype(BF)
    grad_second = dot_t(zeta_two_low, gate_ffn[...])
    sum_held[:, pl.ds(2 * features, features)] += t_dot(second, zeta_two_low)
    for chunk in range(chunks):
        at = pl.ds(chunk * features, features)
        columns = pl.ds((3 + chunk) * features, features)
        grad_hidden = dot_t(grad_feed, held_out[at, :])
        grad_inner = (slope[:, at] * grad_hidden).astype(BF)
        sum_out[at, :] += t_dot(hidden[:, at], grad_feed)
        sum_held[:, columns] += t_dot(second, grad_inner)
        grad_second = grad_second + dot_t(grad_inner, held[:, columns])

    grad_unit = grad_second * gain
    grad_mid = grad + scale * (
        grad_unit - row_mean(grad_unit) - unit * row_mean(grad_unit * unit)
    )
    grad_middle[...] = grad_mid
    grad_branch = (grad_mid * gate_one).astype(BF)
    zeta_one = grad_mid * branch * gate_one * (1.0 - gate_one)
    low_one = zeta_one.astype(BF)
    zeta_one_low[...] = low_one
    sum_held[:, pl.ds(0, features)] += t_dot(mix, grad_branch)
    sum_held[:, pl.ds(features, features)] += t_dot(normed[...], low_one)
    back = dot_t(grad_branch, w_output[...]).astype(BF)
    grad_mixed[...] = back
    product = back.astype(F32) * exact
    high = product.astype(BF)
    rest = (product - high.astype(F32)).astype(BF)
    head_of = lax.broadcasted_iota(jnp.int32, (HEADS, features), 1) // HEAD_DIM
    own = (head_of == lax.broadcasted_iota(jnp.int32, (HEADS, features), 0)).astype(BF)
    inner_sum[...] = dot_t(own, high) + dot_t(own, rest)

    total = lambda v: jnp.sum(v, axis=0, keepdims=True)
    sums[0:1, :] += total(gate_one)
    sums[1:2, :] += total(gate_one * gate_one)
    sums[2:3, :] += total(gate_two)
    sums[3:4, :] += total(gate_two * gate_two)
    sums[4:5, :] += total(zeta_one)
    sums[5:6, :] += total(zeta_two)

    @pl.when(step == last)
    def _():
        staged[...] = sum_held[...].astype(BF)
        staged_out[...] = sum_out[...].astype(BF)
        write_sums(sums[...], sums_tile)
        hand_out(me[0], [(staged, 1, 0), (staged_out, 4, straight), (sums_tile, 0, REST)], send, keep, sems)


def write_sums(sums, tile):
    high = sums[0:6].astype(BF)
    low = (sums[0:6] - high.astype(F32)).astype(BF)
    rows = jnp.concatenate([high.astype(F32), low.astype(F32)], axis=0)
    spill = [
        jnp.concatenate([rows[3 * r + k : 3 * r + k + 1, SUMS:] for k in range(3)], axis=1)
        for r in range(4)
    ]
    tile[...] = jnp.concatenate([rows[:, :SUMS]] + spill, axis=0).astype(BF)


def read_sums(tile):
    tile = tile.astype(F32)
    spill = jnp.concatenate(
        [tile[12 + r : 13 + r, k * 128 : (k + 1) * 128] for r in range(4) for k in range(3)], axis=0
    )
    rows = jnp.concatenate([tile[:12], spill], axis=1)
    return rows[0:6] + rows[6:12]


def feed_forward(me, order, tokens, normed, mixed, out_grad, small, pieces):
    length, width = tokens.shape
    hidden = REST - 3 * width
    hidden = hidden // 2
    tile = 512
    by_rows = pl.BlockSpec((tile, width), lambda i: (i, 0))
    anywhere = pl.BlockSpec(memory_space=pl.ANY)
    rows = jax.ShapeDtypeStruct((length, width), BF)
    half = jax.ShapeDtypeStruct((BLOCKS // 2, ROWS, REST + SUMS), BF)
    straight = 3 * width + hidden
    return pl.pallas_call(
        feed_kernel,
        grid=(length // tile,),
        in_specs=[
            pl.BlockSpec(memory_space=pltpu.SMEM),
            pl.BlockSpec(memory_space=pltpu.SMEM),
            by_rows, by_rows, by_rows, by_rows,
            pl.BlockSpec((4, width), lambda i: (0, 0)),
        ] + [anywhere] * 8,
        out_specs=[
            by_rows, by_rows, by_rows, by_rows,
            pl.BlockSpec((HEADS, tile), lambda i: (0, i)),
            pl.BlockSpec((width, width), lambda i: (0, 0)),
            anywhere, anywhere,
        ],
        out_shape=[
            rows,
            jax.ShapeDtypeStruct((length, width), F32),
            rows,
            rows,
            jax.ShapeDtypeStruct((HEADS, length), F32),
            jax.ShapeDtypeStruct((width, width), BF),
            half,
            half,
        ],
        scratch_shapes=[
            pltpu.VMEM((width, straight), BF),
            pltpu.VMEM((hidden, width), BF),
            pltpu.VMEM((width, straight), F32),
            pltpu.VMEM((hidden, width), F32),
            pltpu.VMEM((width, straight), BF),
            pltpu.VMEM((hidden, width), BF),
            pltpu.VMEM((tile, hidden), BF),
            pltpu.VMEM((tile, hidden), F32),
            pltpu.VMEM((8, width), F32),
            pltpu.VMEM((ROWS, SUMS), BF),
            pltpu.SemaphoreType.DMA((2,)),
        ],
        compiler_params=pltpu.CompilerParams(vmem_limit_bytes=VMEM),
        cost_estimate=pl.CostEstimate(
            flops=6 * length * width * (3 * width + 2 * hidden), bytes_accessed=24 * MIB, transcendentals=length * hidden
        ),
        name="feed_forward",
    )(me, order, tokens, normed, mixed, out_grad, small, *pieces)


def finish_kernel(tokens, zeta_one_low, grad_middle, weights, gate_attn, small, *refs):
    *grads, _after, token_grad = refs
    groups = len(grads) // 3
    width = tokens.shape[1]
    part = width // groups
    total = dot_t(zeta_one_low[...], gate_attn[...])
    for at, grad in enumerate(grads):
        which, group = at % 3, at // 3
        columns = pl.ds(which * width + group * part, part)
        total = total + dot_t(grad[...], weights[:, columns])
    unit, scale = normalise(tokens[...].astype(F32))
    grad_unit = total * small[0:1, :]
    token_grad[...] = grad_middle[...] + scale * (
        grad_unit - row_mean(grad_unit) - unit * row_mean(grad_unit * unit)
    )


def finish(tokens, zeta_one_low, grad_middle, weights, gate_attn, small, grads, after):
    length, width = tokens.shape
    tile = 512
    by_rows = pl.BlockSpec((tile, width), lambda i: (i, 0))
    return pl.pallas_call(
        finish_kernel,
        grid=(length // tile,),
        in_specs=[
            by_rows, by_rows, by_rows,
            pl.BlockSpec((width, 3 * width), lambda i: (0, 0)),
            pl.BlockSpec((width, width), lambda i: (0, 0)),
            pl.BlockSpec((4, width), lambda i: (0, 0)),
        ] + [pl.BlockSpec((tile, g.shape[1]), lambda i: (i, 0)) for g in grads]
        + [pl.BlockSpec(memory_space=pl.ANY)],
        out_specs=by_rows,
        out_shape=jax.ShapeDtypeStruct((length, width), F32),
        compiler_params=pltpu.CompilerParams(vmem_limit_bytes=VMEM),
        cost_estimate=pl.CostEstimate(
            flops=8 * length * width * width, bytes_accessed=16 * MIB, transcendentals=length
        ),
        name="finish",
    )(tokens, zeta_one_low, grad_middle, weights, gate_attn, small, *grads, after)


def row_sum(weight, grad):
    return jnp.sum(weight.astype(F32) * grad, axis=1, keepdims=True)


def close_kernel(
    query, key, value, gate_attn, gate_ffn, w_in, *refs
):
    *parts, _after, grad_query, grad_key, grad_value, grad_output, grad_gate_attn, grad_gate_ffn, grad_in, grad_out, norms, summed = refs
    width = query.shape[1]
    wide = w_in.shape[1]
    add = lambda four, columns: sum(p[:, columns].astype(F32) for p in four)
    late, early = parts[:4], parts[4:]
    total = jnp.zeros((ROWS, 1), F32)
    for k, (weight, out) in enumerate(((query, grad_query), (key, grad_key), (value, grad_value))):
        grad = add(late, pl.ds(k * width, width))
        out[...] = grad
        total = total + row_sum(weight[...], grad)
    grad_output[...] = add(early, pl.ds(0, width))
    grad = add(early, pl.ds(width, width))
    grad_gate_attn[...] = grad
    total = total + row_sum(gate_attn[...], grad)
    grad = add(early, pl.ds(2 * width, width))
    grad_gate_ffn[...] = grad
    other = row_sum(gate_ffn[...], grad)
    grad = add(early, pl.ds(3 * width, wide))
    grad_in[...] = grad
    other = other + row_sum(w_in[...], grad)
    for group in range(4):
        grad_out[pl.ds(group * ROWS, ROWS), :] = add(early, pl.ds(3 * width + wide + group * width, width))
    lane = lax.broadcasted_iota(jnp.int32, (ROWS, 128), 1)
    norms[...] = jnp.where(lane == 0, total, jnp.where(lane == 1, other, 0.0))
    gathered = sum(read_sums(p[:, pl.ds(REST, SUMS)]) for p in early)
    summed[...] = jnp.concatenate([gathered, jnp.zeros((2, width), F32)], axis=0)


def close(query, key, value, gate_attn, gate_ffn, w_in, late, early, after):
    width, wide = query.shape[1], w_in.shape[1]
    vmem = pl.BlockSpec(memory_space=pltpu.VMEM)
    square = jax.ShapeDtypeStruct((ROWS, width), F32)
    return pl.pallas_call(
        close_kernel,
        in_specs=[vmem] * 14 + [pl.BlockSpec(memory_space=pl.ANY)],
        out_shape=[square] * 6 + [
            jax.ShapeDtypeStruct((ROWS, wide), F32),
            jax.ShapeDtypeStruct((4 * ROWS, width), F32),
            jax.ShapeDtypeStruct((ROWS, 128), F32),
            jax.ShapeDtypeStruct((8, width), F32),
        ],
        compiler_params=pltpu.CompilerParams(vmem_limit_bytes=VMEM),
        name="close",
    )(query, key, value, gate_attn, gate_ffn, w_in, *late, *early, after)


def swap(values, axis, bits):
    count = lax.axis_size(axis)
    return lax.ppermute(values, axis, [(i, i ^ bits) for i in range(count)])


def gather_pieces(values):
    line = jnp.concatenate([values] + [swap(values, "narrow", k) for k in (1, 2, 3)])
    return [line] + [swap(line, "wide", 2 * k) for k in (1, 2, 3)]


def both_cores(near):
    return list(near) + [swap(piece, "wide", 1) for piece in near]


def hold_kernel(*refs):
    pass


def hold(arrays, *after):
    count = len(arrays)
    anywhere = pl.BlockSpec(memory_space=pl.ANY)
    return pl.pallas_call(
        hold_kernel,
        in_specs=[anywhere] * (count + len(after)),
        out_specs=[anywhere] * count,
        out_shape=[jax.ShapeDtypeStruct(a.shape, a.dtype) for a in arrays],
        input_output_aliases={k: k for k in range(count)},
        name="hold",
    )(*arrays, *after)


def add_kernel(*refs, terms, each, sums):
    sources, targets = refs[:terms], refs[terms + 1 :]
    columns = targets[0].shape[-1]
    main = columns - SUMS if sums else columns
    for at, target in enumerate(targets):
        for block in range(each):
            index = at * each + block
            total = sources[0][index, :, :main].astype(F32)
            for source in sources[1:]:
                total = total + source[index, :, :main].astype(F32)
            target[block, :, :main] = total.astype(BF)
    if sums:
        gathered = sum(read_sums(source[0, :, main:]) for source in sources)
        write_sums(gathered, targets[0].at[0, :, pl.ds(main, SUMS)])
        tile = targets[0][0, :, main:]
        for target in targets:
            for block in range(each):
                target[block, :, main:] = tile


def add_split(arrays, sums, after):
    blocks, _, columns = arrays[0].shape
    each = blocks // 4
    vmem = pl.BlockSpec(memory_space=pltpu.VMEM)
    return pl.pallas_call(
        partial(add_kernel, terms=len(arrays), each=each, sums=sums),
        in_specs=[vmem] * len(arrays) + [pl.BlockSpec(memory_space=pl.ANY)],
        out_specs=[vmem] * 4,
        out_shape=[jax.ShapeDtypeStruct((each, ROWS, columns), BF)] * 4,
        compiler_params=pltpu.CompilerParams(vmem_limit_bytes=VMEM),
        name="add_split",
    )(*arrays, after)


def add_core(send, keep, sums, after):
    return add_split([keep, swap(send, "wide", 1)], sums, after)


def swap_plane(plane):
    return [swap(plane[k], "wide", 2 * k) for k in (1, 2, 3)]


def along_line(line):
    return [line[0][0]] + [swap(line[k], "narrow", k)[0] for k in (1, 2, 3)]


def natural(send, keep):
    columns = keep.shape[-1]
    halves = jnp.stack([keep, send]).reshape(2, 4, 4, ROWS, columns)
    return halves.transpose(1, 0, 2, 3, 4).reshape(BLOCKS * ROWS, columns)


def pack_kernel(device, vectors, *refs):
    *shards, first, rest = refs
    own = vectors.shape[1]
    column, row = lax.rem(device[0] * own, 128), lax.div(device[0] * own, 128)
    at = 0
    for shard in shards[:3]:
        first[:, at : at + shard.shape[1]] = shard[...]
        at += shard.shape[1]
    values = vectors[...].astype(F32)
    wide = pltpu.roll(jnp.concatenate([values, jnp.zeros((4, 128 - own), F32)], axis=1), column, 1)
    place = lax.broadcasted_iota(jnp.int32, (ROWS, 128), 0)
    tile = jnp.zeros((ROWS, 128), F32)
    for vector in range(4):
        tile = jnp.where(place == vector * 4 + row, wide[vector : vector + 1], tile)
    first[:, at:] = tile.astype(BF)
    at = 0
    for shard in shards[3:7]:
        rest[:, at : at + shard.shape[1]] = shard[...]
        at += shard.shape[1]
    tall = shards[7]
    for group in range(4):
        wide = tall.shape[1]
        rest[:, at : at + wide] = tall[group * ROWS : (group + 1) * ROWS]
        at += wide


def pack(device, vectors, *shards):
    return pl.pallas_call(
        pack_kernel,
        in_specs=[pl.BlockSpec(memory_space=pltpu.SMEM)]
        + [pl.BlockSpec(memory_space=pltpu.VMEM)] * (1 + len(shards)),
        out_shape=[
            jax.ShapeDtypeStruct((ROWS, FIRST), BF),
            jax.ShapeDtypeStruct((ROWS, REST), BF),
        ],
        compiler_params=pltpu.CompilerParams(vmem_limit_bytes=VMEM),
        name="pack",
    )(device, vectors, *shards)


def per_device(
    tokens, segment, w_query, w_key, w_value, w_output, gate_attn, gate_ffn, w_in, w_out,
    norm_attn, norm_ffn, bias_attn, bias_ffn, out_grad,
):
    wide, narrow = lax.axis_size("wide"), lax.axis_size("narrow")
    devices = wide * narrow
    length, width = tokens.shape
    hidden = w_in.shape[1]
    own_rows = w_query.shape[0]
    device = lax.axis_index("wide") * narrow + lax.axis_index("narrow")
    direct = wide == 8 and narrow == 4 and own_rows == ROWS
    vectors = (norm_attn, norm_ffn, bias_attn, bias_ffn)

    def gather(values):
        return lax.all_gather(values, AXES, axis=0, tiled=True)

    if direct:
        me = device.astype(jnp.int32).reshape(1)
        first, rest = pack(
            me, jnp.stack(vectors), w_query, w_key, w_value, w_output, gate_attn, gate_ffn, w_in, w_out
        )
        pieces = both_cores(gather_pieces(first))
        rest_near = gather_pieces(rest)
        order = jnp.concatenate(
            [
                jnp.bitwise_xor(device, (jnp.arange(16) // 4 * 2 + half) * 4 + jnp.arange(16) % 4)
                for half in range(2)
            ]
        ).astype(jnp.int32)
    else:
        full = gather(jnp.stack(vectors, axis=1))
        tile = jnp.zeros((BLOCKS, ROWS, 128), BF).at[0].set(full.T.reshape(ROWS, 128))
        first = jnp.concatenate(
            [gather(w_query), gather(w_key), gather(w_value), tile.reshape(BLOCKS * ROWS, 128)], axis=1
        )
        out_blocks = gather(w_out).reshape(BLOCKS, 4, ROWS, width).transpose(0, 2, 1, 3)
        packet = jnp.concatenate(
            [gather(w_output), gather(gate_attn), gather(gate_ffn), gather(w_in),
             out_blocks.reshape(BLOCKS * ROWS, 4 * width)], axis=1
        )
        pieces = [first[k * 64 : (k + 1) * 64] for k in range(8)]
        rest_pieces = [packet[k * 64 : (k + 1) * 64] for k in range(8)]
        me = jnp.zeros((1,), jnp.int32)
        order = jnp.arange(BLOCKS, dtype=jnp.int32)

    segment_row = segment.reshape(1, length)
    normed, normed_t, query, key, value, key_t, value_t, weights, small = project(order, tokens, pieces)
    mixed, log_total = attend(segment, segment_row, query, key, value_t)
    if direct:
        rest_pieces = both_cores(rest_near[:1] + list(hold(rest_near[1:], mixed)))
    result, grad_middle, zeta_one_low, grad_mixed, inner_sum, whole_gate, send, keep = feed_forward(
        me, order, tokens, normed, mixed, out_grad, small, rest_pieces
    )
    plane = add_core(send, keep, True, me) if direct else [me]
    *grads, late_send, late_keep = attend_back(
        me, segment, segment_row, query, key, value, key_t, grad_mixed, log_total, inner_sum,
        normed_t, plane[0], 0, HEADS,
    )
    if direct:
        received = swap_plane(plane)
        (late_send,) = hold([late_send], *received)
        line = add_split([plane[0]] + received, True, late_send)
        late_plane = add_core(late_send, late_keep, False, line[0])
    else:
        late_plane = [me]
    token_grad = finish(
        tokens, zeta_one_low, grad_middle, weights, whole_gate, small, grads, late_plane[0]
    )

    straight = 3 * width + hidden
    if direct:
        early = along_line(line)
        late = along_line(add_split([late_plane[0]] + swap_plane(late_plane), False, token_grad))
        *owned, norms, summed = close(
            w_query, w_key, w_value, gate_attn, gate_ffn, w_in, late, early, token_grad
        )
        norm_one, norm_two = norms[:, 0], norms[:, 1]
    else:

        def scatter(values):
            return lax.psum_scatter(values, AXES, scatter_dimension=0, tiled=True)

        tile = keep[0, :, REST:].astype(F32)
        spill = tile[12:].reshape(12, 128)
        rows = jnp.concatenate([tile[:12], spill], axis=1)
        own_sums = rows[:6] + rows[6:]
        whole = natural(send, keep)[:, :REST].astype(F32)
        out_whole = whole[:, straight:].reshape(BLOCKS, ROWS, 4, width).transpose(0, 2, 1, 3)
        first = scatter(natural(late_send, late_keep).astype(F32))
        second = scatter(whole[:, :straight])
        owned = [first[:, k * width : (k + 1) * width] for k in range(3)]
        owned += [second[:, k * width : (k + 1) * width] for k in range(3)]
        owned += [second[:, 3 * width :], scatter(out_whole.reshape(hidden, width))]
        shards = (w_query, w_key, w_value, gate_attn)
        norm_one = sum(row_sum(w, g)[:, 0] for w, g in zip(shards, owned[:3] + owned[4:5]))
        norm_two = (row_sum(gate_ffn, owned[5]) + row_sum(w_in, owned[6]))[:, 0]
        summed = lax.psum(own_sums, AXES)

    grad_norm_attn = norm_one / norm_attn.astype(F32)
    grad_norm_ffn = norm_two / norm_ffn.astype(F32)
    counted = length * devices
    mean_one = summed[0] / counted
    mean_two = summed[2] / counted
    gate_stats = jnp.stack(
        [
            mean_one,
            summed[1] / counted - mean_one * mean_one,
            mean_two,
            summed[3] / counted - mean_two * mean_two,
        ]
    )
    own = lax.dynamic_slice(summed, (4, device * own_rows), (2, own_rows))
    return (result, token_grad, *owned, grad_norm_attn, grad_norm_ffn, own[0], own[1], gate_stats)


def solution(mesh):
    rows = P(AXES, None)
    flat = P(AXES)
    in_specs = (rows, flat) + (rows,) * 8 + (flat,) * 4 + (rows,)
    out_specs = (rows,) * 10 + (flat,) * 4 + (P(),)
    return jax.shard_map(
        per_device, mesh=mesh, in_specs=in_specs, out_specs=out_specs, check_vma=False
    )
```

```python
from functools import partial

import jax
import jax.numpy as jnp
from jax import lax
from jax.experimental import pallas as pl
from jax.experimental.pallas import tpu as pltpu
from jax.sharding import PartitionSpec as P

HEADS = 8
HEAD_DIM = 64
EPSILON = 1e-05
MASKED = -1000000000.0
AXES = ("wide", "narrow")
BF = jnp.bfloat16
F32 = jnp.float32
MIB = 1 << 20
VMEM = 60 * MIB
ANYWHERE = pl.BlockSpec(memory_space=pl.ANY)
BLOCK = 256
ROWS = 16
BLOCKS = 32
FIRST = 1536 + 128
TILES = 11
PARTS = 1


def dot(left, right):
    return jnp.dot(left, right, preferred_element_type=F32)


def dot_t(left, right):
    return lax.dot_general(left, right, (((1,), (1,)), ((), ())), preferred_element_type=F32)


def t_dot(left, right):
    return lax.dot_general(left, right, (((0,), (0,)), ((), ())), preferred_element_type=F32)


def row_mean(values):
    return jnp.mean(values, axis=-1, keepdims=True)


def normalise(values):
    offset = values - row_mean(values)
    scale = lax.rsqrt(row_mean(offset * offset) + EPSILON)
    return offset * scale, scale


def sigmoid(values):
    return 1.0 / (1.0 + jnp.exp(-values))


def project_kernel(
    order, tokens, *refs
):
    pieces, refs = refs[:8], refs[8:]
    normed, normed_t, query, key, value, key_t, value_t, weights, small, held, sem = refs
    step = pl.program_id(0)

    @pl.when(step == 0)
    def _():
        for at in range(BLOCKS):
            place = pl.multiple_of(order[at] * ROWS, ROWS)
            pltpu.make_async_copy(
                pieces[at // 4].at[pl.ds(at % 4 * ROWS, ROWS)], held.at[pl.ds(place, ROWS)], sem
            ).start()

    unit, _ = normalise(tokens[...].astype(F32))

    @pl.when(step == 0)
    def _():
        pltpu.make_async_copy(held, held, sem).wait()
        total = jnp.zeros((ROWS, 128), F32)
        for at in range(BLOCKS):
            total = total + held[pl.ds(at * ROWS, ROWS), 1536:FIRST].astype(F32)
        for vector in range(4):
            for part in range(4):
                small[vector : vector + 1, part * 128 : (part + 1) * 128] = total[
                    vector * 4 + part : vector * 4 + part + 1
                ]
        weights[...] = held[:, :1536]

    low = (unit * small[0:1, :]).astype(BF)
    normed[...] = low
    normed_t[...] = low.T
    query[...] = (dot(low, held[:, :512]).astype(BF).astype(F32) * HEAD_DIM**-0.5).astype(BF)
    keys = dot(low, held[:, 512:1024]).astype(BF)
    key[...] = keys
    key_t[...] = keys.T
    values = dot(low, held[:, 1024:1536]).astype(BF)
    value[...] = values
    value_t[...] = values.T


def project(order, tokens, pieces):
    length, width = tokens.shape
    tile = 512
    by_rows = pl.BlockSpec((tile, width), lambda i: (i, 0))
    by_columns = pl.BlockSpec((width, tile), lambda i: (0, i))
    whole = lambda *shape: pl.BlockSpec(shape, lambda i: (0,) * len(shape))
    rows = jax.ShapeDtypeStruct((length, width), BF)
    columns = jax.ShapeDtypeStruct((width, length), BF)
    return pl.pallas_call(
        project_kernel,
        grid=(length // tile,),
        in_specs=[
            pl.BlockSpec(memory_space=pltpu.SMEM),
            by_rows,
        ] + [pl.BlockSpec(memory_space=pl.ANY)] * 8,
        out_specs=[
            by_rows, by_columns, by_rows, by_rows, by_rows, by_columns, by_columns,
            whole(width, 1536), whole(4, width),
        ],
        out_shape=[
            rows, columns, rows, rows, rows, columns, columns,
            jax.ShapeDtypeStruct((width, 1536), BF),
            jax.ShapeDtypeStruct((4, width), F32),
        ],
        scratch_shapes=[pltpu.VMEM((width, FIRST), BF), pltpu.SemaphoreType.DMA],
        compiler_params=pltpu.CompilerParams(vmem_limit_bytes=VMEM),
        cost_estimate=pl.CostEstimate(
            flops=6 * length * width * width, bytes_accessed=12 * MIB, transcendentals=length
        ),
        name="project",
    )(order, tokens, *pieces)


def bias_of(segment_row, key_block, query_block):
    key_at = key_block * BLOCK + lax.broadcasted_iota(jnp.int32, (BLOCK, BLOCK), 0)
    query_at = query_block * BLOCK + lax.broadcasted_iota(jnp.int32, (BLOCK, BLOCK), 1)
    return jnp.where((key_at >= segment_row) & (key_at <= query_at), 0.0, MASKED)


def keep_heads(source, target):
    for head in range(target.shape[0]):
        target[head, :, pl.ds(head % 2 * HEAD_DIM, HEAD_DIM)] = source[:, pl.ds(head * HEAD_DIM, HEAD_DIM)]


def attend_kernel(
    segment, segment_row, query_in, key_in, value_t_in, mixed_out, log_total,
    query, key, value_t, mixed, masked_query, peak, total, mix, in_sems, out_sems,
):
    length, width = query.shape
    steps = length // BLOCK
    heads = range(HEADS)

    def loads(step):
        part = pl.ds(pl.multiple_of(step * BLOCK, BLOCK), BLOCK)
        return [
            pltpu.make_async_copy(query_in.at[part], query.at[part], in_sems.at[0, step]),
            pltpu.make_async_copy(key_in.at[part], key.at[part], in_sems.at[1, step]),
            pltpu.make_async_copy(value_t_in.at[:, part], value_t.at[:, part], in_sems.at[2, step]),
        ]

    def store(step):
        part = pl.ds(pl.multiple_of(step * BLOCK, BLOCK), BLOCK)
        return pltpu.make_async_copy(mixed.at[part], mixed_out.at[part], out_sems.at[step])

    for step in range(steps):
        for copy in loads(step):
            copy.start()
    masked_query[...] = jnp.zeros(masked_query.shape, BF)
    pair = lambda head: pl.ds(head // 2 * 128, 128)
    own = lambda head: pl.ds(head * HEAD_DIM, HEAD_DIM)

    def of_queries(step, _):
        for copy in loads(step):
            copy.wait()
        here = pl.ds(pl.multiple_of(step * BLOCK, BLOCK), BLOCK)
        keep_heads(query.at[here], masked_query)
        peak[...] = jnp.full(peak.shape, -1e30, F32)
        total[...] = jnp.zeros(total.shape, F32)
        mix[...] = jnp.zeros(mix.shape, F32)
        seen = segment_row[:, here]

        def visit(block, _):
            bias = bias_of(seen, block, step)
            rows = pl.ds(pl.multiple_of(block * BLOCK, BLOCK), BLOCK)
            scores = [dot_t(key[rows, pair(h)], masked_query[h]) + bias for h in heads]
            old = [peak[h : h + 1, :] for h in heads]
            new = [jnp.maximum(o, jnp.max(s, axis=0, keepdims=True)) for o, s in zip(old, scores)]
            power = [jnp.exp(s - n) for s, n in zip(scores, new)]
            fade = [jnp.exp(o - n) for o, n in zip(old, new)]
            added = [jnp.sum(p, axis=0, keepdims=True) for p in power]
            high = [p.astype(BF) for p in power]
            rest = [(p - x.astype(F32)).astype(BF) for p, x in zip(power, high)]
            mixes = [
                mix[own(h), :] * fade[h] + dot(value_t[own(h), rows], high[h]) + dot(value_t[own(h), rows], rest[h])
                for h in heads
            ]
            for h in heads:
                peak[h : h + 1, :] = new[h]
                total[h : h + 1, :] = total[h : h + 1, :] * fade[h] + added[h]
                mix[own(h), :] = mixes[h]
            return 0

        first = lax.div(segment[step * BLOCK], BLOCK)
        lax.fori_loop(first, step + 1, visit, 0)
        log_total[:, here] = peak[...] + jnp.log(total[...])
        for head in heads:
            mix[own(head), :] = mix[own(head), :] / total[head : head + 1, :]
        mixed[here, :] = mix[...].T
        store(step).start()
        return 0

    lax.fori_loop(0, steps, of_queries, 0)
    for step in range(steps):
        store(step).wait()


def attend(segment, segment_row, query, key, value_t):
    length, width = query.shape
    steps = length // BLOCK
    smem = pl.BlockSpec(memory_space=pltpu.SMEM)
    vmem = pl.BlockSpec(memory_space=pltpu.VMEM)
    rows = pltpu.VMEM((length, width), BF)
    return pl.pallas_call(
        attend_kernel,
        in_specs=[smem, vmem, ANYWHERE, ANYWHERE, ANYWHERE],
        out_specs=[ANYWHERE, vmem],
        out_shape=[
            jax.ShapeDtypeStruct((length, width), F32),
            jax.ShapeDtypeStruct((HEADS, length), F32),
        ],
        scratch_shapes=[
            rows,
            rows,
            pltpu.VMEM((width, length), BF),
            pltpu.VMEM((length, width), F32),
            pltpu.VMEM((HEADS, BLOCK, 128), BF),
            pltpu.VMEM((HEADS, BLOCK), F32),
            pltpu.VMEM((HEADS, BLOCK), F32),
            pltpu.VMEM((width, BLOCK), F32),
            pltpu.SemaphoreType.DMA((3, steps)),
            pltpu.SemaphoreType.DMA((steps,)),
        ],
        compiler_params=pltpu.CompilerParams(vmem_limit_bytes=VMEM),
        cost_estimate=pl.CostEstimate(
            flops=8 * length * length * width, bytes_accessed=6 * MIB, transcendentals=4 * length * length
        ),
        name="attend",
    )(segment, segment_row, query, key, value_t)


def attend_back_kernel(
    me, segment, segment_row, query_in, key_in, value_in, key_t_in, grad_in, log_total, inner_sum, normed_t_in, _after,
    grad_query, grad_key, grad_value, send, keep,
    query, key, value, grad_mixed, key_t, normed_t,
    masked_query, masked_grad, query_sum, key_sum, value_sum, low_query, low_key, low_value, staged,
    in_sems, out_sems, sems,
):
    length, width = query.shape
    steps = length // BLOCK
    heads = range(HEADS)
    by_rows = ((query_in, query), (key_in, key), (value_in, value), (grad_in, grad_mixed))

    def loads(step):
        part = pl.ds(pl.multiple_of(step * BLOCK, BLOCK), BLOCK)
        copies = [
            pltpu.make_async_copy(source.at[part], target.at[part], in_sems.at[k, step])
            for k, (source, target) in enumerate(by_rows)
        ]
        return copies + [
            pltpu.make_async_copy(key_t_in.at[:, part], key_t.at[:, part], in_sems.at[4, step])
        ]

    for step in range(steps):
        for copy in loads(step):
            copy.start()
    last_load = pltpu.make_async_copy(normed_t_in, normed_t, out_sems.at[3])
    last_load.start()
    key_sum[...] = jnp.zeros(key_sum.shape, F32)
    value_sum[...] = jnp.zeros(value_sum.shape, F32)
    masked_query[...] = jnp.zeros(masked_query.shape, BF)
    masked_grad[...] = jnp.zeros(masked_grad.shape, BF)
    pair = lambda head: pl.ds(head // 2 * 128, 128)
    own = lambda head: pl.ds(head * HEAD_DIM, HEAD_DIM)

    def of_queries(step, _):
        for copy in loads(step):
            copy.wait()
        here = pl.ds(pl.multiple_of(step * BLOCK, BLOCK), BLOCK)
        keep_heads(query.at[here], masked_query)
        keep_heads(grad_mixed.at[here], masked_grad)
        query_sum[...] = jnp.zeros(query_sum.shape, F32)
        seen = segment_row[:, here]

        def visit(block, _):
            bias = bias_of(seen, block, step)
            rows = pl.ds(pl.multiple_of(block * BLOCK, BLOCK), BLOCK)
            scores = [dot_t(key[rows, pair(h)], masked_query[h]) for h in heads]
            grad_probs = [dot_t(value[rows, pair(h)], masked_grad[h]) for h in heads]
            probs = [jnp.exp((scores[h] + bias) - log_total[h : h + 1, here]) for h in heads]
            grad_scores = [
                (probs[h] * (grad_probs[h] - inner_sum[h : h + 1, here])).astype(BF) for h in heads
            ]
            to_value = [dot(probs[h].astype(BF), masked_grad[h]) for h in heads]
            to_key = [dot(grad_scores[h], masked_query[h]) for h in heads]
            to_query = [dot(key_t[own(h), rows], grad_scores[h]) for h in heads]
            for h in heads[::2]:
                value_sum[rows, pair(h)] += to_value[h] + to_value[h + 1]
                key_sum[rows, pair(h)] += to_key[h] + to_key[h + 1]
            for h in heads:
                query_sum[own(h), :] += to_query[h]
            return 0

        first = lax.div(segment[step * BLOCK], BLOCK)
        lax.fori_loop(first, step + 1, visit, 0)
        low_query[here, :] = (query_sum[...] * HEAD_DIM**-0.5).astype(BF).T
        return 0

    lax.fori_loop(0, steps, of_queries, 0)
    low_key[...] = key_sum[...].astype(BF)
    low_value[...] = value_sum[...].astype(BF)
    results = ((low_query, grad_query), (low_key, grad_key), (low_value, grad_value))
    stores = [
        pltpu.make_async_copy(source, target, out_sems.at[k])
        for k, (source, target) in enumerate(results)
    ]
    for store in stores:
        store.start()
    last_load.wait()
    for k, (source, _) in enumerate(results):
        staged[:, k * width : (k + 1) * width] = dot(normed_t[...], source[...]).astype(BF)
    hand_out(
        me[0], lambda row: staged.at[pl.ds(row, ROWS)], lambda out, at: out.at[at], send, keep, sems
    )
    wait_out(send, keep, sems)
    for store in stores:
        store.wait()


def device_at(me, half, at):
    plane, line = at // 4, at % 4
    return jnp.bitwise_xor(me, (plane * 2 + half) * 4 + line)


def hand_out(me, source_at, target_at, send, keep, sems):
    for half, target in enumerate((keep, send)):
        for at in range(BLOCKS // 2):
            place = pl.multiple_of(device_at(me, half, at) * ROWS, ROWS)
            pltpu.make_async_copy(source_at(place), target_at(target, at), sems.at[half]).start()


def wait_out(send, keep, sems):
    for half, target in enumerate((keep, send)):
        pltpu.make_async_copy(target, target, sems.at[half]).wait()


def attend_back(
    me, segment, segment_row, query, key, value, key_t, grad_mixed, log_total, inner_sum, normed_t, after
):
    length, width = query.shape
    steps = length // BLOCK
    smem = pl.BlockSpec(memory_space=pltpu.SMEM)
    vmem = pl.BlockSpec(memory_space=pltpu.VMEM)
    flat = jax.ShapeDtypeStruct((length, width), BF)
    packet = jax.ShapeDtypeStruct((BLOCKS // 2, ROWS, 3 * width), BF)
    rows, columns = pltpu.VMEM((length, width), BF), pltpu.VMEM((width, length), BF)
    return pl.pallas_call(
        attend_back_kernel,
        in_specs=[smem, smem, vmem] + [ANYWHERE] * 5 + [vmem, vmem, ANYWHERE, ANYWHERE],
        out_specs=[ANYWHERE] * 5,
        out_shape=[flat, flat, flat, packet, packet],
        scratch_shapes=[rows] * 4 + [columns] * 2 + [
            pltpu.VMEM((HEADS, BLOCK, 128), BF),
            pltpu.VMEM((HEADS, BLOCK, 128), BF),
            pltpu.VMEM((width, BLOCK), F32),
            pltpu.VMEM((length, width), F32),
            pltpu.VMEM((length, width), F32),
        ] + [rows] * 3 + [
            pltpu.VMEM((width, 3 * width), BF),
            pltpu.SemaphoreType.DMA((5, steps)),
            pltpu.SemaphoreType.DMA((4,)),
            pltpu.SemaphoreType.DMA((2,)),
        ],
        compiler_params=pltpu.CompilerParams(vmem_limit_bytes=VMEM),
        cost_estimate=pl.CostEstimate(
            flops=20 * length * length * width, bytes_accessed=8 * MIB, transcendentals=4 * length * length
        ),
        name="attend_back",
    )(
        me, segment, segment_row, query, key, value, key_t, grad_mixed, log_total, inner_sum, normed_t, after
    )


def feed_kernel(
    me, order, tokens, normed, normed_t, mixed, out_grad, small, *refs
):
    pieces, refs = refs[:8], refs[8:]
    result, grad_middle, zeta_one_low, grad_mixed, inner_sum, gate_attn_out, send, keep, *refs = refs
    held, held_out, grads, staged, hidden, slope, sums, *refs = refs
    mix, second, grad_feed, zeta_two_low, grad_branch, grad_inner, sems, out_sems = refs
    step = pl.program_id(0)
    last = pl.num_programs(0) - 1
    features = tokens.shape[1]
    chunks = 4
    tile = lambda k: pl.ds(k * features, features)
    w_output, gate_attn, gate_ffn, *w_in = (held.at[:, tile(k)] for k in range(3 + chunks))
    w_out = [held_out.at[k] for k in range(chunks)]
    spans = (pl.ds(0, 3 * features), pl.ds(3 * features, chunks * features))

    @pl.when(step == 0)
    def _():
        for part in range(2 + chunks):
            for at in range(BLOCKS):
                place = pl.multiple_of(order[at] * ROWS, ROWS)
                source = pieces[at // 4].at[pl.ds(at % 4 * ROWS, ROWS)]
                here = pl.ds(place, ROWS)
                if part < 2:
                    copy = (source.at[:, spans[part]], held.at[here, spans[part]])
                else:
                    copy = (source.at[:, tile(3 + chunks + part - 2)], held_out.at[part - 2, here])
                pltpu.make_async_copy(*copy, sems.at[min(part, 2)]).start()
        sums[...] = jnp.zeros(sums.shape, F32)
        grads[...] = jnp.zeros(grads.shape, F32)
        pltpu.make_async_copy(held.at[:, spans[0]], held.at[:, spans[0]], sems.at[0]).wait()
        gate_attn_out[...] = gate_attn[...]

    gain, bias_one, bias_two = small[1:2, :], small[2:3, :], small[3:4, :]

    size = tokens.shape[0] // PARTS
    parts = range(PARTS)
    rows = [pl.ds(k * size, size) for k in parts]
    total = lambda vs: sum(jnp.sum(v, axis=0, keepdims=True) for v in vs)

    exact = [mixed[r, :] for r in rows]
    for k in parts:
        mix[rows[k], :] = exact[k].astype(BF)
    branch = [dot(mix[r, :], w_output[...]) for r in rows]
    gate_one = [sigmoid(dot(normed[r, :], gate_attn[...]) + bias_one) for r in rows]
    middle = [tokens[r, :].astype(F32) + g * b for r, g, b in zip(rows, gate_one, branch)]
    unit, scale = zip(*(normalise(m) for m in middle))
    for k in parts:
        second[rows[k], :] = (unit[k] * gain).astype(BF)
    gate_two = [sigmoid(dot(second[r, :], gate_ffn[...]) + bias_two) for r in rows]

    @pl.when(step == 0)
    def _():
        pltpu.make_async_copy(held.at[:, spans[1]], held.at[:, spans[1]], sems.at[1]).wait()
        pltpu.make_async_copy(held_out, held_out, sems.at[2]).wait()

    root = (2.0 / jnp.pi) ** 0.5
    feed = [jnp.zeros((size, features), F32) for _ in parts]
    for chunk in range(chunks):
        at = pl.ds(chunk * features, features)
        inner = [dot(second[r, :], w_in[chunk][...]) for r in rows]
        for k in parts:
            square = inner[k] * inner[k]
            turn = jnp.tanh(inner[k] * (root + (root * 0.044715) * square))
            rise = 0.5 + 0.5 * turn
            value = inner[k] * rise
            slope[rows[k], at] = rise + value * (1.0 - turn) * (
                root + (3.0 * root * 0.044715) * square
            )
            low = value.astype(BF)
            hidden[rows[k], at] = low
            feed[k] = feed[k] + dot(low, w_out[chunk][...])

    grad = [out_grad[r, :].astype(F32) for r in rows]
    zeta_two = []
    for k in parts:
        result[rows[k], :] = (middle[k] + gate_two[k] * feed[k]).astype(BF)
        gated = grad[k] * gate_two[k]
        grad_feed[rows[k], :] = gated.astype(BF)
        zeta_two.append(gated * feed[k] * (1.0 - gate_two[k]))
        zeta_two_low[rows[k], :] = zeta_two[k].astype(BF)
    second_t = second[...].T
    grad_second = [dot_t(zeta_two_low[r, :], gate_ffn[...]) for r in rows]
    grads[2] += dot(second_t, zeta_two_low[...])
    for chunk in range(chunks):
        at = pl.ds(chunk * features, features)
        for k in parts:
            grad_hidden = dot_t(grad_feed[rows[k], :], w_out[chunk][...])
            grad_inner[rows[k], :] = (slope[rows[k], at] * grad_hidden).astype(BF)
            grad_second[k] = grad_second[k] + dot_t(grad_inner[rows[k], :], w_in[chunk][...])
        grads[7 + chunk] += t_dot(hidden[:, at], grad_feed[...])
        grads[3 + chunk] += dot(second_t, grad_inner[...])

    @pl.when(step == last)
    def _():
        ready = pl.ds(2, TILES - 2)
        staged[ready] = grads[ready].astype(BF)
        hand_out(
            me[0], lambda row: staged.at[ready, pl.ds(row, ROWS)], lambda out, at: out.at[at, ready],
            send, keep, out_sems,
        )

    zeta_one = []
    for k in parts:
        grad_unit = grad_second[k] * gain
        grad_mid = grad[k] + scale[k] * (
            grad_unit - row_mean(grad_unit) - unit[k] * row_mean(grad_unit * unit[k])
        )
        grad_middle[rows[k], :] = grad_mid
        gated = grad_mid * gate_one[k]
        grad_branch[rows[k], :] = gated.astype(BF)
        zeta_one.append(gated * branch[k] * (1.0 - gate_one[k]))
        zeta_one_low[rows[k], :] = zeta_one[k].astype(BF)
    head_of = lax.broadcasted_iota(jnp.int32, (HEADS, features), 1) // HEAD_DIM
    own = (head_of == lax.broadcasted_iota(jnp.int32, (HEADS, features), 0)).astype(BF)
    for k in parts:
        back = dot_t(grad_branch[rows[k], :], w_output[...]).astype(BF)
        grad_mixed[rows[k], :] = back
        product = back.astype(F32) * exact[k]
        high = product.astype(BF)
        rest = (product - high.astype(F32)).astype(BF)
        inner_sum[:, rows[k]] = dot_t(own, high) + dot_t(own, rest)
    grads[0] += t_dot(mix[...], grad_branch[...])
    grads[1] += dot(normed_t[...], zeta_one_low[...])

    sums[0:1, :] += total(gate_one)
    sums[1:2, :] += total(g * g for g in gate_one)
    sums[2:3, :] += total(gate_two)
    sums[3:4, :] += total(g * g for g in gate_two)
    sums[4:5, :] += total(zeta_one)
    sums[5:6, :] += total(zeta_two)

    @pl.when(step == last)
    def _():
        sums_tile = write_sums(sums[0:6])
        for part, (first, count) in enumerate(((0, 2), (TILES, 1))):
            ready = pl.ds(first, count)
            if part == 0:
                staged[ready] = grads[ready].astype(BF)
            else:
                staged[TILES] = jnp.concatenate([sums_tile] * BLOCKS, axis=0)
            hand_out(
                me[0], lambda row: staged.at[ready, pl.ds(row, ROWS)], lambda out, at: out.at[at, ready],
                send, keep, out_sems,
            )
        wait_out(send, keep, out_sems)


def write_sums(sums):
    high = sums.astype(BF).astype(F32)
    rows = jnp.concatenate([high, sums - high, jnp.zeros((4, sums.shape[1]), F32)], axis=0)
    return rows.astype(BF)


def read_sums(tile):
    rows = tile.astype(F32)
    return rows[0:6] + rows[6:12]


def feed_forward(me, order, tokens, normed, normed_t, mixed, out_grad, small, pieces):
    length, width = tokens.shape
    hidden = 4 * width
    tile = 512
    by_rows = pl.BlockSpec((tile, width), lambda i: (i, 0))
    anywhere = pl.BlockSpec(memory_space=pl.ANY)
    rows = jax.ShapeDtypeStruct((length, width), BF)
    half = jax.ShapeDtypeStruct((BLOCKS // 2, TILES + 1, ROWS, width), BF)
    return pl.pallas_call(
        feed_kernel,
        grid=(length // tile,),
        in_specs=[
            pl.BlockSpec(memory_space=pltpu.SMEM),
            pl.BlockSpec(memory_space=pltpu.SMEM),
            by_rows, by_rows,
            pl.BlockSpec((width, tile), lambda i: (0, i)),
            by_rows, by_rows,
            pl.BlockSpec((4, width), lambda i: (0, 0)),
        ] + [anywhere] * 8,
        out_specs=[
            by_rows, by_rows, by_rows, by_rows,
            pl.BlockSpec((HEADS, tile), lambda i: (0, i)),
            pl.BlockSpec((width, width), lambda i: (0, 0)),
            anywhere, anywhere,
        ],
        out_shape=[
            rows,
            jax.ShapeDtypeStruct((length, width), F32),
            rows,
            rows,
            jax.ShapeDtypeStruct((HEADS, length), F32),
            jax.ShapeDtypeStruct((width, width), BF),
            half,
            half,
        ],
        scratch_shapes=[
            pltpu.VMEM((width, 7 * width), BF),
            pltpu.VMEM((4, width, width), BF),
            pltpu.VMEM((TILES, width, width), F32),
            pltpu.VMEM((TILES + 1, width, width), BF),
            pltpu.VMEM((tile, hidden), BF),
            pltpu.VMEM((tile, hidden), F32),
            pltpu.VMEM((8, width), F32),
        ] + [pltpu.VMEM((tile, width), BF)] * 6 + [
            pltpu.SemaphoreType.DMA((3,)),
            pltpu.SemaphoreType.DMA((2,)),
        ],
        compiler_params=pltpu.CompilerParams(vmem_limit_bytes=VMEM),
        cost_estimate=pl.CostEstimate(
            flops=6 * length * width * (3 * width + 2 * hidden), bytes_accessed=24 * MIB, transcendentals=length * hidden
        ),
        name="feed_forward",
    )(me, order, tokens, normed, normed_t, mixed, out_grad, small, *pieces)


def finish_kernel(tokens, zeta_one_low, grad_middle, weights, gate_attn, small, *refs):
    *grads, _after, token_grad, finished = refs
    finished[...] = jnp.zeros(finished.shape, F32)
    groups = len(grads) // 3
    width = tokens.shape[1]
    part = width // groups
    total = dot_t(zeta_one_low[...], gate_attn[...])
    for at, grad in enumerate(grads):
        which, group = at % 3, at // 3
        columns = pl.ds(which * width + group * part, part)
        total = total + dot_t(grad[...], weights[:, columns])
    unit, scale = normalise(tokens[...].astype(F32))
    grad_unit = total * small[0:1, :]
    token_grad[...] = grad_middle[...] + scale * (
        grad_unit - row_mean(grad_unit) - unit * row_mean(grad_unit * unit)
    )


def finish(tokens, zeta_one_low, grad_middle, weights, gate_attn, small, grads, after):
    length, width = tokens.shape
    tile = 512
    by_rows = pl.BlockSpec((tile, width), lambda i: (i, 0))
    return pl.pallas_call(
        finish_kernel,
        grid=(length // tile,),
        in_specs=[
            by_rows, by_rows, by_rows,
            pl.BlockSpec((width, 3 * width), lambda i: (0, 0)),
            pl.BlockSpec((width, width), lambda i: (0, 0)),
            pl.BlockSpec((4, width), lambda i: (0, 0)),
        ] + [pl.BlockSpec((tile, g.shape[1]), lambda i: (i, 0)) for g in grads]
        + [pl.BlockSpec(memory_space=pl.ANY)],
        out_specs=[by_rows, pl.BlockSpec((8, 128), lambda i: (0, 0))],
        out_shape=[
            jax.ShapeDtypeStruct((length, width), F32),
            jax.ShapeDtypeStruct((8, 128), F32),
        ],
        compiler_params=pltpu.CompilerParams(vmem_limit_bytes=VMEM),
        cost_estimate=pl.CostEstimate(
            flops=8 * length * width * width, bytes_accessed=16 * MIB, transcendentals=length
        ),
        name="finish",
    )(tokens, zeta_one_low, grad_middle, weights, gate_attn, small, *grads, after)


def row_sum(weight, grad):
    return jnp.sum(weight.astype(F32) * grad, axis=1, keepdims=True)


def in_order(features):
    unit = lax.broadcasted_iota(jnp.int32, (features, features), 0)
    column = lax.broadcasted_iota(jnp.int32, (features, features), 1)
    group, inside = column // 128, column % 128
    return (unit == inside // ROWS * 64 + group * ROWS + inside % ROWS).astype(BF)


def close_kernel(device, query, key, value, gate_attn, gate_ffn, w_in, gain_one, gain_two, *refs):
    late, early, refs = refs[:4], refs[4:8], refs[9:]
    *square_grads, grad_in, grad_out, norm_one, norm_two, bias_one, bias_two, stats = refs
    grad_query, grad_key, grad_value, grad_output, grad_gate_attn, grad_gate_ffn = square_grads
    width = query.shape[1]
    tile = lambda k: sum(p[pl.ds(k * ROWS, ROWS), :].astype(F32) for p in early)
    total = jnp.zeros((ROWS, 1), F32)
    for k, (weight, out) in enumerate(((query, grad_query), (key, grad_key), (value, grad_value))):
        grad = sum(p[:, pl.ds(k * width, width)].astype(F32) for p in late)
        out[...] = grad
        total = total + row_sum(weight[...], grad)
    grad_output[...] = tile(0)
    grad = tile(1)
    grad_gate_attn[...] = grad
    total = total + row_sum(gate_attn[...], grad)
    grad = tile(2)
    grad_gate_ffn[...] = grad
    other = row_sum(gate_ffn[...], grad)
    order = in_order(width)
    tiles = [tile(3 + k) for k in range(4)]
    for part in range(4):
        columns = pl.ds(part * width, width)
        grad = jnp.concatenate([t[:, part * 128 : (part + 1) * 128] for t in tiles], axis=1)
        high = grad.astype(BF)
        grad = dot_t(high, order) + dot_t((grad - high.astype(F32)).astype(BF), order)
        grad_in[:, columns] = grad
        other = other + row_sum(w_in[:, columns], grad)
    for group in range(4):
        grad_out[pl.ds(group * ROWS, ROWS), :] = tile(7 + group)

    def as_row(column, gain):
        eye = lax.broadcasted_iota(jnp.int32, (ROWS, ROWS), 0) == lax.broadcasted_iota(
            jnp.int32, (ROWS, ROWS), 1
        )
        return jnp.sum(jnp.where(eye, column, 0.0), axis=0, keepdims=True) / gain

    norm_one[...] = as_row(total, gain_one[...].astype(F32)[None, :])
    norm_two[...] = as_row(other, gain_two[...].astype(F32)[None, :])
    summed = sum(read_sums(p[pl.ds(TILES * ROWS, ROWS), :]) for p in early)
    mean = summed / device[1].astype(F32)
    stats[0:1, :] = mean[0:1]
    stats[1:2, :] = mean[1:2] - mean[0:1] * mean[0:1]
    stats[2:3, :] = mean[2:3]
    stats[3:4, :] = mean[3:4] - mean[2:3] * mean[2:3]
    both = jnp.concatenate([summed[4:6], jnp.zeros((6, width), F32)], axis=0)
    moved = pltpu.roll(both, lax.rem(width - device[0] * ROWS, width), 1)
    bias_one[...] = moved[0:1, :ROWS]
    bias_two[...] = moved[1:2, :ROWS]


def close(device, query, key, value, gate_attn, gate_ffn, w_in, gain_one, gain_two, late, early, after):
    width, wide = query.shape[1], w_in.shape[1]
    vmem = pl.BlockSpec(memory_space=pltpu.VMEM)
    square = jax.ShapeDtypeStruct((ROWS, width), F32)
    vector = jax.ShapeDtypeStruct((1, ROWS), F32)
    outs = [square] * 6 + [
        jax.ShapeDtypeStruct((ROWS, wide), F32),
        jax.ShapeDtypeStruct((4 * ROWS, width), F32),
    ] + [vector] * 4 + [jax.ShapeDtypeStruct((4, width), F32)]
    whole = lambda array: pl.BlockSpec(array.shape, lambda i: (0,) * len(array.shape))
    return pl.pallas_call(
        close_kernel,
        grid=(1,),
        in_specs=[pl.BlockSpec(memory_space=pltpu.SMEM)]
        + [whole(a) for a in (query, key, value, gate_attn, gate_ffn, w_in)]
        + [vmem] * 10
        + [ANYWHERE],
        out_specs=[whole(a) for a in outs],
        out_shape=outs,
        compiler_params=pltpu.CompilerParams(vmem_limit_bytes=VMEM),
        name="close",
    )(device, query, key, value, gate_attn, gate_ffn, w_in, gain_one, gain_two, *late, *early, after)


def swap(values, axis, bits):
    count = lax.axis_size(axis)
    return lax.ppermute(values, axis, [(i, i ^ bits) for i in range(count)])


def gather_pieces(values):
    line = jnp.concatenate([values] + [swap(values, "narrow", k) for k in (1, 2, 3)])
    return [line] + [swap(line, "wide", 2 * k) for k in (1, 2, 3)]


def both_cores(near):
    return list(near) + [swap(piece, "wide", 1) for piece in near]


def hold_kernel(*refs):
    pass


def hold(arrays, after):
    count = len(arrays)
    return pl.pallas_call(
        hold_kernel,
        in_specs=[ANYWHERE] * (count + len(after)),
        out_specs=[ANYWHERE] * count,
        out_shape=[jax.ShapeDtypeStruct(a.shape, a.dtype) for a in arrays],
        input_output_aliases={k: k for k in range(count)},
        name="hold",
    )(*arrays, *after)


def add_kernel(own, *refs, terms, sums):
    arrived, targets, (held, sems) = refs[: terms - 1], refs[terms : terms + 4], refs[terms + 4 :]
    each, rows, _ = targets[0].shape
    copies = []
    for part in range(4):
        here = pl.ds(part * each, each)
        copies.append(pltpu.make_async_copy(own.at[here], held.at[here], sems.at[part]))
        copies[-1].start()
    tile = pl.ds(rows - ROWS, ROWS)
    for part, target in enumerate(targets):
        copies[part].wait()
        for block in range(each):
            at = part * each + block
            target[block] = sum((a[at].astype(F32) for a in arrived), held[at].astype(F32)).astype(BF)
        if sums and part == 0:
            added = write_sums(sum((read_sums(a[0, tile, :]) for a in arrived), read_sums(held[0, tile, :])))
        if sums:
            for block in range(each):
                target[block, tile, :] = added


def add_split(own, arrived, sums, limit, after):
    blocks, rows, columns = own.shape
    vmem = pl.BlockSpec(memory_space=pltpu.VMEM)
    return pl.pallas_call(
        partial(add_kernel, terms=1 + len(arrived), sums=sums),
        in_specs=[ANYWHERE] + [vmem] * len(arrived) + [ANYWHERE],
        out_specs=[vmem] * 4,
        out_shape=[jax.ShapeDtypeStruct((blocks // 4, rows, columns), BF)] * 4,
        scratch_shapes=[pltpu.VMEM(own.shape, BF), pltpu.SemaphoreType.DMA((4,))],
        compiler_params=pltpu.CompilerParams(vmem_limit_bytes=int(limit * MIB)),
        name="add_split",
    )(own, *arrived, after)


def add_core(send, keep, sums, limit, after):
    return add_split(keep, [swap(send, "wide", 1)], sums, limit, after)


def swap_plane(plane):
    return [swap(plane[k], "wide", 2 * k) for k in (1, 2, 3)]


def along_line(line):
    return [line[0][0]] + [swap(line[k], "narrow", k)[0] for k in (1, 2, 3)]


def natural(send, keep):
    halves = jnp.stack([keep, send]).reshape(2, 4, 4, *keep.shape[1:])
    return halves.swapaxes(0, 1).reshape(BLOCKS, *keep.shape[1:])


def pack_first(device, vectors, shards, first):
    own = vectors[0].shape[0]
    column, row = lax.rem(device[0] * own, 128), lax.div(device[0] * own, 128)
    at = 0
    for shard in shards:
        first[:, at : at + shard.shape[1]] = shard[...]
        at += shard.shape[1]
    values = jnp.concatenate([v[...].astype(F32)[None, :] for v in vectors], axis=0)
    wide = pltpu.roll(jnp.concatenate([values, jnp.zeros((4, 128 - own), F32)], axis=1), column, 1)
    place = lax.broadcasted_iota(jnp.int32, (ROWS, 128), 0)
    tile = jnp.zeros((ROWS, 128), F32)
    for vector in range(4):
        tile = jnp.where(place == vector * 4 + row, wide[vector : vector + 1], tile)
    first[:, at:] = tile.astype(BF)


def pack_kernel(device, *refs):
    vectors, shards, (first, rest) = refs[:4], refs[4:-2], refs[-2:]
    pack_first(device, vectors, shards[:3], first)
    pack_rest(*shards[3:], rest)


def pack_rest(w_output, gate_attn, gate_ffn, w_in, w_out, rest):
    width = w_output.shape[1]
    tile = lambda k: pl.ds(k * width, width)
    for k, shard in enumerate((w_output, gate_attn, gate_ffn)):
        rest[:, tile(k)] = shard[...]
    order = in_order(width)
    for part in range(4):
        moved = dot(w_in[:, tile(part)], order).astype(BF)
        for group in range(4):
            rest[:, pl.ds((3 + group) * width + part * 128, 128)] = moved[:, group * 128 : (group + 1) * 128]
    for group in range(4):
        rest[:, tile(7 + group)] = w_out[group * ROWS : (group + 1) * ROWS, :]


def pack(device, vectors, *shards):
    vmem = pl.BlockSpec(memory_space=pltpu.VMEM)
    return pl.pallas_call(
        pack_kernel,
        in_specs=[pl.BlockSpec(memory_space=pltpu.SMEM)] + [vmem] * (4 + len(shards)),
        out_shape=[
            jax.ShapeDtypeStruct((ROWS, FIRST), BF),
            jax.ShapeDtypeStruct((ROWS, TILES * shards[0].shape[1]), BF),
        ],
        compiler_params=pltpu.CompilerParams(vmem_limit_bytes=VMEM),
        name="pack",
    )(device, *vectors, *shards)


def per_device(
    tokens, segment, w_query, w_key, w_value, w_output, gate_attn, gate_ffn, w_in, w_out,
    norm_attn, norm_ffn, bias_attn, bias_ffn, out_grad,
):
    wide, narrow = lax.axis_size("wide"), lax.axis_size("narrow")
    devices = wide * narrow
    length, width = tokens.shape
    hidden = w_in.shape[1]
    own_rows = w_query.shape[0]
    device = lax.axis_index("wide") * narrow + lax.axis_index("narrow")
    direct = wide == 8 and narrow == 4 and own_rows == ROWS
    vectors = (norm_attn, norm_ffn, bias_attn, bias_ffn)

    def gather(values):
        return lax.all_gather(values, AXES, axis=0, tiled=True)

    if direct:
        me = device.astype(jnp.int32).reshape(1)
        first, rest = pack(
            me, vectors, w_query, w_key, w_value, w_output, gate_attn, gate_ffn, w_in, w_out
        )
        pieces = both_cores(gather_pieces(first))
        rest_near = gather_pieces(rest)
        order = jnp.concatenate(
            [
                jnp.bitwise_xor(device, (jnp.arange(16) // 4 * 2 + half) * 4 + jnp.arange(16) % 4)
                for half in range(2)
            ]
        ).astype(jnp.int32)
    else:
        full = gather(jnp.stack(vectors, axis=1))
        tile = jnp.zeros((BLOCKS, ROWS, 128), BF).at[0].set(full.T.reshape(ROWS, 128))
        first = jnp.concatenate(
            [gather(w_query), gather(w_key), gather(w_value), tile.reshape(BLOCKS * ROWS, 128)], axis=1
        ).reshape(8, 4 * ROWS, FIRST)
        squares = [gather(w).reshape(BLOCKS, 1, ROWS, width) for w in (w_output, gate_attn, gate_ffn)]
        in_tiles = gather(w_in).reshape(BLOCKS, ROWS, BLOCKS, 4, ROWS).transpose(0, 3, 1, 2, 4)
        packet = jnp.concatenate(
            squares + [in_tiles.reshape(BLOCKS, 4, ROWS, width), gather(w_out).reshape(BLOCKS, 4, ROWS, width)],
            axis=1,
        ).swapaxes(1, 2).reshape(8, 4 * ROWS, TILES * width)
        pieces = [first[k] for k in range(8)]
        rest_pieces = [packet[k] for k in range(8)]
        me = jnp.zeros((1,), jnp.int32)
        order = jnp.arange(BLOCKS, dtype=jnp.int32)

    segment_row = segment.reshape(1, length)
    normed, normed_t, query, key, value, key_t, value_t, weights, small = project(order, tokens, pieces)
    mixed, log_total = attend(segment, segment_row, query, key, value_t)
    if direct:
        rest_pieces = both_cores(rest_near[:1] + list(hold(rest_near[1:], [log_total])))
    result, grad_middle, zeta_one_low, grad_mixed, inner_sum, whole_gate, send, keep = feed_forward(
        me, order, tokens, normed, normed_t, mixed, out_grad, small, rest_pieces
    )
    if direct:
        flat = lambda values: values.reshape(BLOCKS // 2, (TILES + 1) * ROWS, width)
        plane = add_core(flat(send), flat(keep), True, 12, me)
    else:
        plane = [me]
    *grads, late_send, late_keep = attend_back(
        me, segment, segment_row, query, key, value, key_t, grad_mixed, log_total, inner_sum,
        normed_t, plane[0],
    )
    if direct:
        received = swap_plane(plane)
        (late_send,) = hold([late_send], received)
        line = add_split(plane[0], received, True, 12, me)
        late_plane = add_core(late_send, late_keep, False, 12, line[0])
    else:
        late_plane = [me]
    token_grad, finished = finish(
        tokens, zeta_one_low, grad_middle, weights, whole_gate, small, grads, late_plane[0]
    )

    counted = length * devices
    if direct:
        early = along_line(line)
        late = along_line(add_split(late_plane[0], swap_plane(late_plane), False, 12, finished))
        device_and_count = jnp.stack([device, jnp.int32(counted)]).astype(jnp.int32)
        *owned, norm_one, norm_two, bias_one, bias_two, stats = close(
            device_and_count, w_query, w_key, w_value, gate_attn, gate_ffn, w_in, norm_attn, norm_ffn, late, early, finished
        )
        small_grads = [v.reshape(own_rows) for v in (norm_one, norm_two, bias_one, bias_two)]
        return (result, token_grad, *owned, *small_grads, stats)

    def scatter(values):
        return lax.psum_scatter(values, AXES, scatter_dimension=0, tiled=True)

    tile = keep[0, TILES].astype(F32)
    summed = lax.psum(tile[:6] + tile[6:12], AXES)
    whole = natural(send, keep).astype(F32)
    first = scatter(natural(late_send, late_keep).astype(F32).reshape(width, 3 * width))
    owned = [first[:, k * width : (k + 1) * width] for k in range(3)]
    owned += [scatter(whole[:, k].reshape(width, width)) for k in range(3)]
    in_tiles = whole[:, 3:7].reshape(BLOCKS, 4, ROWS, BLOCKS, ROWS).transpose(0, 2, 3, 1, 4)
    owned += [scatter(in_tiles.reshape(width, hidden)), scatter(whole[:, 7:11].reshape(hidden, width))]
    shards = (w_query, w_key, w_value, gate_attn)
    norm_one = sum(row_sum(w, g)[:, 0] for w, g in zip(shards, owned[:3] + owned[4:5]))
    norm_two = (row_sum(gate_ffn, owned[5]) + row_sum(w_in, owned[6]))[:, 0]
    mean = summed[:4] / counted
    gate_stats = jnp.stack([mean[0], mean[1] - mean[0] * mean[0], mean[2], mean[3] - mean[2] * mean[2]])
    own = lax.dynamic_slice(summed, (4, device * own_rows), (2, own_rows))
    return (
        result, token_grad, *owned, norm_one / norm_attn.astype(F32), norm_two / norm_ffn.astype(F32),
        own[0], own[1], gate_stats,
    )


def solution(mesh):
    rows = P(AXES, None)
    flat = P(AXES)
    in_specs = (rows, flat) + (rows,) * 8 + (flat,) * 4 + (rows,)
    out_specs = (rows,) * 10 + (flat,) * 4 + (P(),)
    return jax.shard_map(
        per_device, mesh=mesh, in_specs=in_specs, out_specs=out_specs, check_vma=False
    )
```

```python
from functools import partial

import jax
import jax.numpy as jnp
from jax import lax
from jax.experimental import pallas as pl
from jax.experimental.pallas import tpu as pltpu
from jax.sharding import PartitionSpec as P

HEADS = 8
HEAD_DIM = 64
EPSILON = 1e-05
MASKED = -1000000000.0
AXES = ("wide", "narrow")
BF = jnp.bfloat16
F32 = jnp.float32
MIB = 1 << 20
VMEM = 60 * MIB
ANYWHERE = pl.BlockSpec(memory_space=pl.ANY)
BLOCK = 256
ROWS = 16
BLOCKS = 32
FIRST = 1536 + 128
TILES = 11
PARTS = 1


def dot(left, right):
    return jnp.dot(left, right, preferred_element_type=F32)


def dot_t(left, right):
    return lax.dot_general(left, right, (((1,), (1,)), ((), ())), preferred_element_type=F32)


def t_dot(left, right):
    return lax.dot_general(left, right, (((0,), (0,)), ((), ())), preferred_element_type=F32)


def row_mean(values):
    return jnp.mean(values, axis=-1, keepdims=True)


def normalise(values):
    offset = values - row_mean(values)
    scale = lax.rsqrt(row_mean(offset * offset) + EPSILON)
    return offset * scale, scale


def sigmoid(values):
    return 0.5 + 0.5 * jnp.tanh(0.5 * values)


def project_kernel(
    order, tokens, *refs
):
    pieces, refs = refs[:8], refs[8:]
    normed, normed_t, query, key, value, key_t, value_t, weights, small, held, sem = refs
    step = pl.program_id(0)

    @pl.when(step == 0)
    def _():
        for at in range(BLOCKS):
            place = pl.multiple_of(order[at] * ROWS, ROWS)
            pltpu.make_async_copy(
                pieces[at // 4].at[pl.ds(at % 4 * ROWS, ROWS)], held.at[pl.ds(place, ROWS)], sem
            ).start()

    unit, _ = normalise(tokens[...].astype(F32))

    @pl.when(step == 0)
    def _():
        pltpu.make_async_copy(held, held, sem).wait()
        total = jnp.zeros((ROWS, 128), F32)
        for at in range(BLOCKS):
            total = total + held[pl.ds(at * ROWS, ROWS), 1536:FIRST].astype(F32)
        for vector in range(4):
            for part in range(4):
                small[vector : vector + 1, part * 128 : (part + 1) * 128] = total[
                    vector * 4 + part : vector * 4 + part + 1
                ]
        weights[...] = held[:, :1536]

    low = (unit * small[0:1, :]).astype(BF)
    normed[...] = low
    normed_t[...] = low.T
    query[...] = (dot(low, held[:, :512]).astype(BF).astype(F32) * HEAD_DIM**-0.5).astype(BF)
    keys = dot(low, held[:, 512:1024]).astype(BF)
    key[...] = keys
    key_t[...] = keys.T
    values = dot(low, held[:, 1024:1536]).astype(BF)
    value[...] = values
    value_t[...] = values.T


def project(order, tokens, pieces):
    length, width = tokens.shape
    tile = 512
    by_rows = pl.BlockSpec((tile, width), lambda i: (i, 0))
    by_columns = pl.BlockSpec((width, tile), lambda i: (0, i))
    whole = lambda *shape: pl.BlockSpec(shape, lambda i: (0,) * len(shape))
    rows = jax.ShapeDtypeStruct((length, width), BF)
    columns = jax.ShapeDtypeStruct((width, length), BF)
    return pl.pallas_call(
        project_kernel,
        grid=(length // tile,),
        in_specs=[
            pl.BlockSpec(memory_space=pltpu.SMEM),
            by_rows,
        ] + [pl.BlockSpec(memory_space=pl.ANY)] * 8,
        out_specs=[
            by_rows, by_columns, by_rows, by_rows, by_rows, by_columns, by_columns,
            whole(width, 1536), whole(4, width),
        ],
        out_shape=[
            rows, columns, rows, rows, rows, columns, columns,
            jax.ShapeDtypeStruct((width, 1536), BF),
            jax.ShapeDtypeStruct((4, width), F32),
        ],
        scratch_shapes=[pltpu.VMEM((width, FIRST), BF), pltpu.SemaphoreType.DMA],
        compiler_params=pltpu.CompilerParams(vmem_limit_bytes=VMEM),
        cost_estimate=pl.CostEstimate(
            flops=6 * length * width * width, bytes_accessed=12 * MIB, transcendentals=length
        ),
        name="project",
    )(order, tokens, *pieces)


def bias_of(segment_row, key_block, query_block):
    key_at = key_block * BLOCK + lax.broadcasted_iota(jnp.int32, (BLOCK, BLOCK), 0)
    query_at = query_block * BLOCK + lax.broadcasted_iota(jnp.int32, (BLOCK, BLOCK), 1)
    return jnp.where((key_at >= segment_row) & (key_at <= query_at), 0.0, MASKED)


def keep_heads(source, target):
    for head in range(target.shape[0]):
        target[head, :, pl.ds(head % 2 * HEAD_DIM, HEAD_DIM)] = source[:, pl.ds(head * HEAD_DIM, HEAD_DIM)]


def attend_kernel(
    segment, segment_row, query_in, key_in, value_t_in, mixed_out, log_total,
    query, key, value_t, mixed, masked_query, peak, total, mix, in_sems, out_sems,
):
    length, width = query.shape
    steps = length // BLOCK
    heads = range(HEADS)

    def loads(step):
        part = pl.ds(pl.multiple_of(step * BLOCK, BLOCK), BLOCK)
        return [
            pltpu.make_async_copy(query_in.at[part], query.at[part], in_sems.at[0, step]),
            pltpu.make_async_copy(key_in.at[part], key.at[part], in_sems.at[1, step]),
            pltpu.make_async_copy(value_t_in.at[:, part], value_t.at[:, part], in_sems.at[2, step]),
        ]

    def store(step):
        part = pl.ds(pl.multiple_of(step * BLOCK, BLOCK), BLOCK)
        return pltpu.make_async_copy(mixed.at[part], mixed_out.at[part], out_sems.at[step])

    for step in range(steps):
        for copy in loads(step):
            copy.start()
    masked_query[...] = jnp.zeros(masked_query.shape, BF)
    pair = lambda head: pl.ds(head // 2 * 128, 128)
    own = lambda head: pl.ds(head * HEAD_DIM, HEAD_DIM)

    def of_queries(step, _):
        for copy in loads(step):
            copy.wait()
        here = pl.ds(pl.multiple_of(step * BLOCK, BLOCK), BLOCK)
        keep_heads(query.at[here], masked_query)
        peak[...] = jnp.full(peak.shape, -1e30, F32)
        total[...] = jnp.zeros(total.shape, F32)
        mix[...] = jnp.zeros(mix.shape, F32)
        seen = segment_row[:, here]

        def visit(block, _):
            bias = bias_of(seen, block, step)
            rows = pl.ds(pl.multiple_of(block * BLOCK, BLOCK), BLOCK)
            scores = [dot_t(key[rows, pair(h)], masked_query[h]) + bias for h in heads]
            old = [peak[h : h + 1, :] for h in heads]
            new = [jnp.maximum(o, jnp.max(s, axis=0, keepdims=True)) for o, s in zip(old, scores)]
            power = [jnp.exp(s - n) for s, n in zip(scores, new)]
            fade = [jnp.exp(o - n) for o, n in zip(old, new)]
            added = [jnp.sum(p, axis=0, keepdims=True) for p in power]
            high = [p.astype(BF) for p in power]
            rest = [(p - x.astype(F32)).astype(BF) for p, x in zip(power, high)]
            mixes = [
                mix[own(h), :] * fade[h] + dot(value_t[own(h), rows], high[h]) + dot(value_t[own(h), rows], rest[h])
                for h in heads
            ]
            for h in heads:
                peak[h : h + 1, :] = new[h]
                total[h : h + 1, :] = total[h : h + 1, :] * fade[h] + added[h]
                mix[own(h), :] = mixes[h]
            return 0

        first = lax.div(segment[step * BLOCK], BLOCK)
        lax.fori_loop(first, step + 1, visit, 0)
        log_total[:, here] = peak[...] + jnp.log(total[...])
        for head in heads:
            mix[own(head), :] = mix[own(head), :] / total[head : head + 1, :]
        mixed[here, :] = mix[...].T
        store(step).start()
        return 0

    lax.fori_loop(0, steps, of_queries, 0)
    for step in range(steps):
        store(step).wait()


def attend(segment, segment_row, query, key, value_t):
    length, width = query.shape
    steps = length // BLOCK
    smem = pl.BlockSpec(memory_space=pltpu.SMEM)
    vmem = pl.BlockSpec(memory_space=pltpu.VMEM)
    rows = pltpu.VMEM((length, width), BF)
    return pl.pallas_call(
        attend_kernel,
        in_specs=[smem, vmem, ANYWHERE, ANYWHERE, ANYWHERE],
        out_specs=[ANYWHERE, vmem],
        out_shape=[
            jax.ShapeDtypeStruct((length, width), F32),
            jax.ShapeDtypeStruct((HEADS, length), F32),
        ],
        scratch_shapes=[
            rows,
            rows,
            pltpu.VMEM((width, length), BF),
            pltpu.VMEM((length, width), F32),
            pltpu.VMEM((HEADS, BLOCK, 128), BF),
            pltpu.VMEM((HEADS, BLOCK), F32),
            pltpu.VMEM((HEADS, BLOCK), F32),
            pltpu.VMEM((width, BLOCK), F32),
            pltpu.SemaphoreType.DMA((3, steps)),
            pltpu.SemaphoreType.DMA((steps,)),
        ],
        compiler_params=pltpu.CompilerParams(vmem_limit_bytes=VMEM),
        cost_estimate=pl.CostEstimate(
            flops=8 * length * length * width, bytes_accessed=6 * MIB, transcendentals=4 * length * length
        ),
        name="attend",
    )(segment, segment_row, query, key, value_t)


def attend_back_kernel(
    me, segment, segment_row, query_in, key_in, value_in, key_t_in, grad_in, log_total, inner_sum, normed_t_in, _after,
    grad_query, grad_key, grad_value, send, keep,
    query, key, value, grad_mixed, key_t, normed_t,
    masked_query, masked_grad, query_sum, key_sum, value_sum, low_query, low_key, low_value, staged,
    in_sems, out_sems, sems,
):
    length, width = query.shape
    steps = length // BLOCK
    heads = range(HEADS)
    by_rows = ((query_in, query), (key_in, key), (value_in, value), (grad_in, grad_mixed))

    def loads(step):
        part = pl.ds(pl.multiple_of(step * BLOCK, BLOCK), BLOCK)
        copies = [
            pltpu.make_async_copy(source.at[part], target.at[part], in_sems.at[k, step])
            for k, (source, target) in enumerate(by_rows)
        ]
        return copies + [
            pltpu.make_async_copy(key_t_in.at[:, part], key_t.at[:, part], in_sems.at[4, step])
        ]

    for step in range(steps):
        for copy in loads(step):
            copy.start()
    last_load = pltpu.make_async_copy(normed_t_in, normed_t, out_sems.at[3])
    last_load.start()
    key_sum[...] = jnp.zeros(key_sum.shape, F32)
    value_sum[...] = jnp.zeros(value_sum.shape, F32)
    masked_query[...] = jnp.zeros(masked_query.shape, BF)
    masked_grad[...] = jnp.zeros(masked_grad.shape, BF)
    pair = lambda head: pl.ds(head // 2 * 128, 128)
    own = lambda head: pl.ds(head * HEAD_DIM, HEAD_DIM)

    def of_queries(step, _):
        for copy in loads(step):
            copy.wait()
        here = pl.ds(pl.multiple_of(step * BLOCK, BLOCK), BLOCK)
        keep_heads(query.at[here], masked_query)
        keep_heads(grad_mixed.at[here], masked_grad)
        query_sum[...] = jnp.zeros(query_sum.shape, F32)
        seen = segment_row[:, here]

        def visit(block, _):
            bias = bias_of(seen, block, step)
            rows = pl.ds(pl.multiple_of(block * BLOCK, BLOCK), BLOCK)
            scores = [dot_t(key[rows, pair(h)], masked_query[h]) for h in heads]
            grad_probs = [dot_t(value[rows, pair(h)], masked_grad[h]) for h in heads]
            probs = [jnp.exp((scores[h] + bias) - log_total[h : h + 1, here]) for h in heads]
            grad_scores = [
                (probs[h] * (grad_probs[h] - inner_sum[h : h + 1, here])).astype(BF) for h in heads
            ]
            to_value = [dot(probs[h].astype(BF), masked_grad[h]) for h in heads]
            to_key = [dot(grad_scores[h], masked_query[h]) for h in heads]
            to_query = [dot(key_t[own(h), rows], grad_scores[h]) for h in heads]
            for h in heads[::2]:
                value_sum[rows, pair(h)] += to_value[h] + to_value[h + 1]
                key_sum[rows, pair(h)] += to_key[h] + to_key[h + 1]
            for h in heads:
                query_sum[own(h), :] += to_query[h]
            return 0

        first = lax.div(segment[step * BLOCK], BLOCK)
        lax.fori_loop(first, step + 1, visit, 0)
        low_query[here, :] = (query_sum[...] * HEAD_DIM**-0.5).astype(BF).T
        return 0

    lax.fori_loop(0, steps, of_queries, 0)
    low_key[...] = key_sum[...].astype(BF)
    low_value[...] = value_sum[...].astype(BF)
    results = ((low_query, grad_query), (low_key, grad_key), (low_value, grad_value))
    stores = [
        pltpu.make_async_copy(source, target, out_sems.at[k])
        for k, (source, target) in enumerate(results)
    ]
    for store in stores:
        store.start()
    last_load.wait()
    for k, (source, _) in enumerate(results):
        staged[:, k * width : (k + 1) * width] = dot(normed_t[...], source[...]).astype(BF)
    hand_out(
        me[0], lambda row: staged.at[pl.ds(row, ROWS)], lambda out, at: out.at[at], send, keep, sems
    )
    wait_out(send, keep, sems)
    for store in stores:
        store.wait()


def device_at(me, half, at):
    plane, line = at // 4, at % 4
    return jnp.bitwise_xor(me, (plane * 2 + half) * 4 + line)


def hand_out(me, source_at, target_at, send, keep, sems):
    for half, target in enumerate((keep, send)):
        for at in range(BLOCKS // 2):
            place = pl.multiple_of(device_at(me, half, at) * ROWS, ROWS)
            pltpu.make_async_copy(source_at(place), target_at(target, at), sems.at[half]).start()


def wait_out(send, keep, sems):
    for half, target in enumerate((keep, send)):
        pltpu.make_async_copy(target, target, sems.at[half]).wait()


def attend_back(
    me, segment, segment_row, query, key, value, key_t, grad_mixed, log_total, inner_sum, normed_t, after
):
    length, width = query.shape
    steps = length // BLOCK
    smem = pl.BlockSpec(memory_space=pltpu.SMEM)
    vmem = pl.BlockSpec(memory_space=pltpu.VMEM)
    flat = jax.ShapeDtypeStruct((length, width), BF)
    packet = jax.ShapeDtypeStruct((BLOCKS // 2, ROWS, 3 * width), BF)
    rows, columns = pltpu.VMEM((length, width), BF), pltpu.VMEM((width, length), BF)
    return pl.pallas_call(
        attend_back_kernel,
        in_specs=[smem, smem, vmem] + [ANYWHERE] * 5 + [vmem, vmem, ANYWHERE, ANYWHERE],
        out_specs=[ANYWHERE] * 5,
        out_shape=[flat, flat, flat, packet, packet],
        scratch_shapes=[rows] * 4 + [columns] * 2 + [
            pltpu.VMEM((HEADS, BLOCK, 128), BF),
            pltpu.VMEM((HEADS, BLOCK, 128), BF),
            pltpu.VMEM((width, BLOCK), F32),
            pltpu.VMEM((length, width), F32),
            pltpu.VMEM((length, width), F32),
        ] + [rows] * 3 + [
            pltpu.VMEM((width, 3 * width), BF),
            pltpu.SemaphoreType.DMA((5, steps)),
            pltpu.SemaphoreType.DMA((4,)),
            pltpu.SemaphoreType.DMA((2,)),
        ],
        compiler_params=pltpu.CompilerParams(vmem_limit_bytes=57 * MIB),
        cost_estimate=pl.CostEstimate(
            flops=20 * length * length * width, bytes_accessed=8 * MIB, transcendentals=4 * length * length
        ),
        name="attend_back",
    )(
        me, segment, segment_row, query, key, value, key_t, grad_mixed, log_total, inner_sum, normed_t, after
    )


def feed_kernel(
    me, order, tokens, normed, normed_t, mixed, out_grad, small, *refs
):
    pieces, refs = refs[:8], refs[8:]
    result, grad_middle, zeta_one_low, grad_mixed, inner_sum, gate_attn_out, send, keep, *refs = refs
    held, held_out, grads, staged, hidden, slope, sums, *refs = refs
    mix, second, grad_feed, zeta_two_low, grad_branch, grad_inner, sems, out_sems = refs
    step = pl.program_id(0)
    last = pl.num_programs(0) - 1
    features = tokens.shape[1]
    chunks = 4
    tile = lambda k: pl.ds(k * features, features)
    w_output, gate_attn, gate_ffn, *w_in = (held.at[:, tile(k)] for k in range(3 + chunks))
    w_out = [held_out.at[k] for k in range(chunks)]
    spans = (pl.ds(0, 3 * features), pl.ds(3 * features, chunks * features))

    @pl.when(step == 0)
    def _():
        for part in range(2 + chunks):
            for at in range(BLOCKS):
                place = pl.multiple_of(order[at] * ROWS, ROWS)
                source = pieces[at // 4].at[pl.ds(at % 4 * ROWS, ROWS)]
                here = pl.ds(place, ROWS)
                if part < 2:
                    copy = (source.at[:, spans[part]], held.at[here, spans[part]])
                else:
                    copy = (source.at[:, tile(3 + chunks + part - 2)], held_out.at[part - 2, here])
                pltpu.make_async_copy(*copy, sems.at[min(part, 2)]).start()
        sums[...] = jnp.zeros(sums.shape, F32)
        grads[...] = jnp.zeros(grads.shape, F32)
        pltpu.make_async_copy(held.at[:, spans[0]], held.at[:, spans[0]], sems.at[0]).wait()
        gate_attn_out[...] = gate_attn[...]

    gain, bias_one, bias_two = small[1:2, :], small[2:3, :], small[3:4, :]

    size = tokens.shape[0] // PARTS
    parts = range(PARTS)
    rows = [pl.ds(k * size, size) for k in parts]
    total = lambda vs: sum(jnp.sum(v, axis=0, keepdims=True) for v in vs)

    exact = [mixed[r, :] for r in rows]
    for k in parts:
        mix[rows[k], :] = exact[k].astype(BF)
    branch = [dot(mix[r, :], w_output[...]) for r in rows]
    gate_one = [sigmoid(dot(normed[r, :], gate_attn[...]) + bias_one) for r in rows]
    middle = [tokens[r, :].astype(F32) + g * b for r, g, b in zip(rows, gate_one, branch)]
    unit, scale = zip(*(normalise(m) for m in middle))
    for k in parts:
        second[rows[k], :] = (unit[k] * gain).astype(BF)
    gate_two = [sigmoid(dot(second[r, :], gate_ffn[...]) + bias_two) for r in rows]

    @pl.when(step == 0)
    def _():
        pltpu.make_async_copy(held.at[:, spans[1]], held.at[:, spans[1]], sems.at[1]).wait()
        pltpu.make_async_copy(held_out, held_out, sems.at[2]).wait()

    root = (2.0 / jnp.pi) ** 0.5
    feed = [jnp.zeros((size, features), F32) for _ in parts]
    for chunk in range(chunks):
        at = pl.ds(chunk * features, features)
        inner = [dot(second[r, :], w_in[chunk][...]) for r in rows]
        for k in parts:
            square = inner[k] * inner[k]
            turn = jnp.tanh(inner[k] * (root + (root * 0.044715) * square))
            rise = 0.5 + 0.5 * turn
            value = inner[k] * rise
            slope[rows[k], at] = rise + value * (1.0 - turn) * (
                root + (3.0 * root * 0.044715) * square
            )
            low = value.astype(BF)
            hidden[rows[k], at] = low
            feed[k] = feed[k] + dot(low, w_out[chunk][...])

    grad = [out_grad[r, :].astype(F32) for r in rows]
    zeta_two = []
    for k in parts:
        result[rows[k], :] = (middle[k] + gate_two[k] * feed[k]).astype(BF)
        gated = grad[k] * gate_two[k]
        grad_feed[rows[k], :] = gated.astype(BF)
        zeta_two.append(gated * feed[k] * (1.0 - gate_two[k]))
        zeta_two_low[rows[k], :] = zeta_two[k].astype(BF)
    second_t = second[...].T
    grad_second = [dot_t(zeta_two_low[r, :], gate_ffn[...]) for r in rows]
    grads[2] += dot(second_t, zeta_two_low[...])
    for chunk in range(chunks):
        at = pl.ds(chunk * features, features)
        for k in parts:
            grad_hidden = dot_t(grad_feed[rows[k], :], w_out[chunk][...])
            grad_inner[rows[k], :] = (slope[rows[k], at] * grad_hidden).astype(BF)
            grad_second[k] = grad_second[k] + dot_t(grad_inner[rows[k], :], w_in[chunk][...])
        grads[7 + chunk] += t_dot(hidden[:, at], grad_feed[...])
        grads[3 + chunk] += dot(second_t, grad_inner[...])

    @pl.when(step == last)
    def _():
        ready = pl.ds(2, TILES - 2)
        staged[ready] = grads[ready].astype(BF)
        hand_out(
            me[0], lambda row: staged.at[ready, pl.ds(row, ROWS)], lambda out, at: out.at[at, ready],
            send, keep, out_sems,
        )

    zeta_one = []
    for k in parts:
        grad_unit = grad_second[k] * gain
        grad_mid = grad[k] + scale[k] * (
            grad_unit - row_mean(grad_unit) - unit[k] * row_mean(grad_unit * unit[k])
        )
        grad_middle[rows[k], :] = grad_mid
        gated = grad_mid * gate_one[k]
        grad_branch[rows[k], :] = gated.astype(BF)
        zeta_one.append(gated * branch[k] * (1.0 - gate_one[k]))
        zeta_one_low[rows[k], :] = zeta_one[k].astype(BF)
    head_of = lax.broadcasted_iota(jnp.int32, (HEADS, features), 1) // HEAD_DIM
    own = (head_of == lax.broadcasted_iota(jnp.int32, (HEADS, features), 0)).astype(BF)
    for k in parts:
        back = dot_t(grad_branch[rows[k], :], w_output[...]).astype(BF)
        grad_mixed[rows[k], :] = back
        product = back.astype(F32) * exact[k]
        high = product.astype(BF)
        rest = (product - high.astype(F32)).astype(BF)
        inner_sum[:, rows[k]] = dot_t(own, high) + dot_t(own, rest)
    grads[0] += t_dot(mix[...], grad_branch[...])
    grads[1] += dot(normed_t[...], zeta_one_low[...])

    sums[0:1, :] += total(gate_one)
    sums[1:2, :] += total(g * g for g in gate_one)
    sums[2:3, :] += total(gate_two)
    sums[3:4, :] += total(g * g for g in gate_two)
    sums[4:5, :] += total(zeta_one)
    sums[5:6, :] += total(zeta_two)

    @pl.when(step == last)
    def _():
        sums_tile = write_sums(sums[0:6])
        for part, (first, count) in enumerate(((0, 2), (TILES, 1))):
            ready = pl.ds(first, count)
            if part == 0:
                staged[ready] = grads[ready].astype(BF)
            else:
                staged[TILES] = jnp.concatenate([sums_tile] * BLOCKS, axis=0)
            hand_out(
                me[0], lambda row: staged.at[ready, pl.ds(row, ROWS)], lambda out, at: out.at[at, ready],
                send, keep, out_sems,
            )
        wait_out(send, keep, out_sems)


def write_sums(sums):
    high = sums.astype(BF).astype(F32)
    rows = jnp.concatenate([high, sums - high, jnp.zeros((4, sums.shape[1]), F32)], axis=0)
    return rows.astype(BF)


def read_sums(tile):
    rows = tile.astype(F32)
    return rows[0:6] + rows[6:12]


def feed_forward(me, order, tokens, normed, normed_t, mixed, out_grad, small, pieces):
    length, width = tokens.shape
    hidden = 4 * width
    tile = 512
    by_rows = pl.BlockSpec((tile, width), lambda i: (i, 0))
    anywhere = pl.BlockSpec(memory_space=pl.ANY)
    rows = jax.ShapeDtypeStruct((length, width), BF)
    half = jax.ShapeDtypeStruct((BLOCKS // 2, TILES + 1, ROWS, width), BF)
    return pl.pallas_call(
        feed_kernel,
        grid=(length // tile,),
        in_specs=[
            pl.BlockSpec(memory_space=pltpu.SMEM),
            pl.BlockSpec(memory_space=pltpu.SMEM),
            by_rows, by_rows,
            pl.BlockSpec((width, tile), lambda i: (0, i)),
            by_rows, by_rows,
            pl.BlockSpec((4, width), lambda i: (0, 0)),
        ] + [anywhere] * 8,
        out_specs=[
            by_rows, by_rows, by_rows, by_rows,
            pl.BlockSpec((HEADS, tile), lambda i: (0, i)),
            pl.BlockSpec((width, width), lambda i: (0, 0)),
            anywhere, anywhere,
        ],
        out_shape=[
            rows,
            jax.ShapeDtypeStruct((length, width), F32),
            rows,
            rows,
            jax.ShapeDtypeStruct((HEADS, length), F32),
            jax.ShapeDtypeStruct((width, width), BF),
            half,
            half,
        ],
        scratch_shapes=[
            pltpu.VMEM((width, 7 * width), BF),
            pltpu.VMEM((4, width, width), BF),
            pltpu.VMEM((TILES, width, width), F32),
            pltpu.VMEM((TILES + 1, width, width), BF),
            pltpu.VMEM((tile, hidden), BF),
            pltpu.VMEM((tile, hidden), F32),
            pltpu.VMEM((8, width), F32),
        ] + [pltpu.VMEM((tile, width), BF)] * 6 + [
            pltpu.SemaphoreType.DMA((3,)),
            pltpu.SemaphoreType.DMA((2,)),
        ],
        compiler_params=pltpu.CompilerParams(vmem_limit_bytes=VMEM),
        cost_estimate=pl.CostEstimate(
            flops=6 * length * width * (3 * width + 2 * hidden), bytes_accessed=24 * MIB, transcendentals=length * hidden
        ),
        name="feed_forward",
    )(me, order, tokens, normed, normed_t, mixed, out_grad, small, *pieces)


def finish_kernel(tokens, zeta_one_low, grad_middle, weights, gate_attn, small, *refs):
    grads, (token_grad, finished) = refs[:3], refs[-2:]
    finished[...] = jnp.zeros(finished.shape, F32)
    width = tokens.shape[1]
    total = dot_t(zeta_one_low[...], gate_attn[...])
    for which, grad in enumerate(grads):
        total = total + dot_t(grad[...], weights[:, which * width : (which + 1) * width])
    unit, scale = normalise(tokens[...].astype(F32))
    grad_unit = total * small[0:1, :]
    token_grad[...] = grad_middle[...] + scale * (
        grad_unit - row_mean(grad_unit) - unit * row_mean(grad_unit * unit)
    )


def finish(tokens, zeta_one_low, grad_middle, weights, gate_attn, small, grads, after, first, count, before=()):
    length, width = tokens.shape
    tile = 512
    by_rows = pl.BlockSpec((tile, width), lambda i: (i + first, 0))
    whole = lambda *shape: pl.BlockSpec(shape, lambda i: (0, 0))
    return pl.pallas_call(
        finish_kernel,
        grid=(count,),
        in_specs=[by_rows] * 3 + [whole(width, 3 * width), whole(width, width), whole(4, width)]
        + [by_rows] * 3
        + [ANYWHERE] * (1 + len(before)),
        out_specs=[by_rows, whole(8, 128)],
        out_shape=[
            jax.ShapeDtypeStruct((length, width), F32),
            jax.ShapeDtypeStruct((8, 128), F32),
        ],
        input_output_aliases={10: 0} if before else {},
        compiler_params=pltpu.CompilerParams(vmem_limit_bytes=VMEM),
        cost_estimate=pl.CostEstimate(
            flops=8 * tile * count * width * width, bytes_accessed=5 * MIB * count, transcendentals=tile
        ),
        name="finish",
    )(tokens, zeta_one_low, grad_middle, weights, gate_attn, small, *grads, after, *before)


def row_sum(weight, grad):
    return jnp.sum(weight.astype(F32) * grad, axis=1, keepdims=True)


def in_order(features):
    unit = lax.broadcasted_iota(jnp.int32, (features, features), 0)
    column = lax.broadcasted_iota(jnp.int32, (features, features), 1)
    group, inside = column // 128, column % 128
    return (unit == inside // ROWS * 64 + group * ROWS + inside % ROWS).astype(BF)


def close_kernel(device, query, key, value, gate_attn, gate_ffn, w_in, gain_one, gain_two, *refs):
    late, early, refs = refs[:4], refs[4:8], refs[9:]
    *square_grads, grad_in, grad_out, norm_one, norm_two, bias_one, bias_two, stats = refs
    grad_query, grad_key, grad_value, grad_output, grad_gate_attn, grad_gate_ffn = square_grads
    width = query.shape[1]
    tile = lambda k: sum(p[pl.ds(k * ROWS, ROWS), :].astype(F32) for p in early)
    total = jnp.zeros((ROWS, 1), F32)
    for k, (weight, out) in enumerate(((query, grad_query), (key, grad_key), (value, grad_value))):
        grad = sum(p[:, pl.ds(k * width, width)].astype(F32) for p in late)
        out[...] = grad
        total = total + row_sum(weight[...], grad)
    grad_output[...] = tile(0)
    grad = tile(1)
    grad_gate_attn[...] = grad
    total = total + row_sum(gate_attn[...], grad)
    grad = tile(2)
    grad_gate_ffn[...] = grad
    other = row_sum(gate_ffn[...], grad)
    order = in_order(width)
    tiles = [tile(3 + k) for k in range(4)]
    for part in range(4):
        columns = pl.ds(part * width, width)
        grad = jnp.concatenate([t[:, part * 128 : (part + 1) * 128] for t in tiles], axis=1)
        high = grad.astype(BF)
        grad = dot_t(high, order) + dot_t((grad - high.astype(F32)).astype(BF), order)
        grad_in[:, columns] = grad
        other = other + row_sum(w_in[:, columns], grad)
    for group in range(4):
        grad_out[pl.ds(group * ROWS, ROWS), :] = tile(7 + group)

    def as_row(column, gain):
        eye = lax.broadcasted_iota(jnp.int32, (ROWS, ROWS), 0) == lax.broadcasted_iota(
            jnp.int32, (ROWS, ROWS), 1
        )
        return jnp.sum(jnp.where(eye, column, 0.0), axis=0, keepdims=True) / gain

    norm_one[...] = as_row(total, gain_one[...].astype(F32)[None, :])
    norm_two[...] = as_row(other, gain_two[...].astype(F32)[None, :])
    summed = sum(read_sums(p[pl.ds(TILES * ROWS, ROWS), :]) for p in early)
    mean = summed / device[1].astype(F32)
    stats[0:1, :] = mean[0:1]
    stats[1:2, :] = mean[1:2] - mean[0:1] * mean[0:1]
    stats[2:3, :] = mean[2:3]
    stats[3:4, :] = mean[3:4] - mean[2:3] * mean[2:3]
    both = jnp.concatenate([summed[4:6], jnp.zeros((6, width), F32)], axis=0)
    moved = pltpu.roll(both, lax.rem(width - device[0] * ROWS, width), 1)
    bias_one[...] = moved[0:1, :ROWS]
    bias_two[...] = moved[1:2, :ROWS]


def close(device, query, key, value, gate_attn, gate_ffn, w_in, gain_one, gain_two, late, early, after):
    width, wide = query.shape[1], w_in.shape[1]
    vmem = pl.BlockSpec(memory_space=pltpu.VMEM)
    square = jax.ShapeDtypeStruct((ROWS, width), F32)
    vector = jax.ShapeDtypeStruct((1, ROWS), F32)
    outs = [square] * 6 + [
        jax.ShapeDtypeStruct((ROWS, wide), F32),
        jax.ShapeDtypeStruct((4 * ROWS, width), F32),
    ] + [vector] * 4 + [jax.ShapeDtypeStruct((4, width), F32)]
    whole = lambda array: pl.BlockSpec(array.shape, lambda i: (0,) * len(array.shape))
    return pl.pallas_call(
        close_kernel,
        grid=(1,),
        in_specs=[pl.BlockSpec(memory_space=pltpu.SMEM)]
        + [whole(a) for a in (query, key, value, gate_attn, gate_ffn, w_in)]
        + [vmem] * 10
        + [ANYWHERE],
        out_specs=[whole(a) for a in outs],
        out_shape=outs,
        compiler_params=pltpu.CompilerParams(vmem_limit_bytes=VMEM),
        name="close",
    )(device, query, key, value, gate_attn, gate_ffn, w_in, gain_one, gain_two, *late, *early, after)


def swap(values, axis, bits):
    count = lax.axis_size(axis)
    return lax.ppermute(values, axis, [(i, i ^ bits) for i in range(count)])


def gather_pieces(values):
    line = jnp.concatenate([values] + [swap(values, "narrow", k) for k in (1, 2, 3)])
    return [line] + [swap(line, "wide", 2 * k) for k in (1, 2, 3)]


def both_cores(near):
    return list(near) + [swap(piece, "wide", 1) for piece in near]


def hold_kernel(*refs):
    pass


def hold(arrays, after):
    count = len(arrays)
    return pl.pallas_call(
        hold_kernel,
        in_specs=[ANYWHERE] * (count + len(after)),
        out_specs=[ANYWHERE] * count,
        out_shape=[jax.ShapeDtypeStruct(a.shape, a.dtype) for a in arrays],
        input_output_aliases={k: k for k in range(count)},
        compiler_params=pltpu.CompilerParams(vmem_limit_bytes=4 * MIB),
        name="hold",
    )(*arrays, *after)


def add_kernel(own, *refs, terms, sums):
    arrived, targets, (held, sems) = refs[: terms - 1], refs[terms : terms + 4], refs[terms + 4 :]
    each, rows, _ = targets[0].shape
    copies = []
    for part in range(4):
        here = pl.ds(part * each, each)
        copies.append(pltpu.make_async_copy(own.at[here], held.at[here], sems.at[part]))
        copies[-1].start()
    tile = pl.ds(rows - ROWS, ROWS)
    for part, target in enumerate(targets):
        copies[part].wait()
        for block in range(each):
            at = part * each + block
            target[block] = sum((a[at].astype(F32) for a in arrived), held[at].astype(F32)).astype(BF)
        if sums and part == 0:
            added = write_sums(sum((read_sums(a[0, tile, :]) for a in arrived), read_sums(held[0, tile, :])))
        if sums:
            for block in range(each):
                target[block, tile, :] = added


def add_split(own, arrived, sums, limit, after):
    blocks, rows, columns = own.shape
    vmem = pl.BlockSpec(memory_space=pltpu.VMEM)
    return pl.pallas_call(
        partial(add_kernel, terms=1 + len(arrived), sums=sums),
        in_specs=[ANYWHERE] + [vmem] * len(arrived) + [ANYWHERE],
        out_specs=[vmem] * 4,
        out_shape=[jax.ShapeDtypeStruct((blocks // 4, rows, columns), BF)] * 4,
        scratch_shapes=[pltpu.VMEM(own.shape, BF), pltpu.SemaphoreType.DMA((4,))],
        compiler_params=pltpu.CompilerParams(vmem_limit_bytes=int(limit * MIB)),
        name="add_split",
    )(own, *arrived, after)


def add_core(send, keep, sums, limit, after):
    return add_split(keep, [swap(send, "wide", 1)], sums, limit, after)


def swap_plane(plane):
    return [swap(plane[k], "wide", 2 * k) for k in (1, 2, 3)]


def along_line(line):
    return [line[0][0]] + [swap(line[k], "narrow", k)[0] for k in (1, 2, 3)]


def natural(send, keep):
    halves = jnp.stack([keep, send]).reshape(2, 4, 4, *keep.shape[1:])
    return halves.swapaxes(0, 1).reshape(BLOCKS, *keep.shape[1:])


def pack_first(device, vectors, shards, first):
    own = vectors[0].shape[0]
    column, row = lax.rem(device[0] * own, 128), lax.div(device[0] * own, 128)
    at = 0
    for shard in shards:
        first[:, at : at + shard.shape[1]] = shard[...]
        at += shard.shape[1]
    values = jnp.concatenate([v[...].astype(F32)[None, :] for v in vectors], axis=0)
    wide = pltpu.roll(jnp.concatenate([values, jnp.zeros((4, 128 - own), F32)], axis=1), column, 1)
    place = lax.broadcasted_iota(jnp.int32, (ROWS, 128), 0)
    tile = jnp.zeros((ROWS, 128), F32)
    for vector in range(4):
        tile = jnp.where(place == vector * 4 + row, wide[vector : vector + 1], tile)
    first[:, at:] = tile.astype(BF)


def pack_kernel(device, *refs):
    vectors, shards, (first, rest) = refs[:4], refs[4:-2], refs[-2:]
    pack_first(device, vectors, shards[:3], first)
    pack_rest(*shards[3:], rest)


def pack_rest(w_output, gate_attn, gate_ffn, w_in, w_out, rest):
    width = w_output.shape[1]
    tile = lambda k: pl.ds(k * width, width)
    for k, shard in enumerate((w_output, gate_attn, gate_ffn)):
        rest[:, tile(k)] = shard[...]
    order = in_order(width)
    for part in range(4):
        moved = dot(w_in[:, tile(part)], order).astype(BF)
        for group in range(4):
            rest[:, pl.ds((3 + group) * width + part * 128, 128)] = moved[:, group * 128 : (group + 1) * 128]
    for group in range(4):
        rest[:, tile(7 + group)] = w_out[group * ROWS : (group + 1) * ROWS, :]


def pack(device, vectors, *shards):
    vmem = pl.BlockSpec(memory_space=pltpu.VMEM)
    return pl.pallas_call(
        pack_kernel,
        in_specs=[pl.BlockSpec(memory_space=pltpu.SMEM)] + [vmem] * (4 + len(shards)),
        out_shape=[
            jax.ShapeDtypeStruct((ROWS, FIRST), BF),
            jax.ShapeDtypeStruct((ROWS, TILES * shards[0].shape[1]), BF),
        ],
        compiler_params=pltpu.CompilerParams(vmem_limit_bytes=VMEM),
        name="pack",
    )(device, *vectors, *shards)


def per_device(
    tokens, segment, w_query, w_key, w_value, w_output, gate_attn, gate_ffn, w_in, w_out,
    norm_attn, norm_ffn, bias_attn, bias_ffn, out_grad,
):
    wide, narrow = lax.axis_size("wide"), lax.axis_size("narrow")
    devices = wide * narrow
    length, width = tokens.shape
    hidden = w_in.shape[1]
    own_rows = w_query.shape[0]
    device = lax.axis_index("wide") * narrow + lax.axis_index("narrow")
    direct = wide == 8 and narrow == 4 and own_rows == ROWS
    vectors = (norm_attn, norm_ffn, bias_attn, bias_ffn)

    def gather(values):
        return lax.all_gather(values, AXES, axis=0, tiled=True)

    if direct:
        me = device.astype(jnp.int32).reshape(1)
        first, rest = pack(
            me, vectors, w_query, w_key, w_value, w_output, gate_attn, gate_ffn, w_in, w_out
        )
        pieces = both_cores(gather_pieces(first))
        rest_near = gather_pieces(rest)
        order = jnp.concatenate(
            [
                jnp.bitwise_xor(device, (jnp.arange(16) // 4 * 2 + half) * 4 + jnp.arange(16) % 4)
                for half in range(2)
            ]
        ).astype(jnp.int32)
    else:
        full = gather(jnp.stack(vectors, axis=1))
        tile = jnp.zeros((BLOCKS, ROWS, 128), BF).at[0].set(full.T.reshape(ROWS, 128))
        first = jnp.concatenate(
            [gather(w_query), gather(w_key), gather(w_value), tile.reshape(BLOCKS * ROWS, 128)], axis=1
        ).reshape(8, 4 * ROWS, FIRST)
        squares = [gather(w).reshape(BLOCKS, 1, ROWS, width) for w in (w_output, gate_attn, gate_ffn)]
        in_tiles = gather(w_in).reshape(BLOCKS, ROWS, BLOCKS, 4, ROWS).transpose(0, 3, 1, 2, 4)
        packet = jnp.concatenate(
            squares + [in_tiles.reshape(BLOCKS, 4, ROWS, width), gather(w_out).reshape(BLOCKS, 4, ROWS, width)],
            axis=1,
        ).swapaxes(1, 2).reshape(8, 4 * ROWS, TILES * width)
        pieces = [first[k] for k in range(8)]
        rest_pieces = [packet[k] for k in range(8)]
        me = jnp.zeros((1,), jnp.int32)
        order = jnp.arange(BLOCKS, dtype=jnp.int32)

    segment_row = segment.reshape(1, length)
    normed, normed_t, query, key, value, key_t, value_t, weights, small = project(order, tokens, pieces)
    mixed, log_total = attend(segment, segment_row, query, key, value_t)
    if direct:
        rest_pieces = both_cores(rest_near[:1] + list(hold(rest_near[1:], [log_total])))
    result, grad_middle, zeta_one_low, grad_mixed, inner_sum, whole_gate, send, keep = feed_forward(
        me, order, tokens, normed, normed_t, mixed, out_grad, small, rest_pieces
    )
    if direct:
        flat = lambda values: values.reshape(BLOCKS // 2, (TILES + 1) * ROWS, width)
        plane = add_core(flat(send), flat(keep), True, 12, me)
    else:
        plane = [me]
    *grads, late_send, late_keep = attend_back(
        me, segment, segment_row, query, key, value, key_t, grad_mixed, log_total, inner_sum,
        normed_t, plane[0],
    )
    if direct:
        received = swap_plane(plane)
        (late_send,) = hold([late_send], received)
        line = add_split(plane[0], received, True, 12, me)
        late_plane = add_core(late_send, late_keep, False, 12, line[0])
    else:
        late_plane = [me]
    to_finish = (tokens, zeta_one_low, grad_middle, weights, whole_gate, small, grads)
    tiles = length // 512
    token_grad, finished = finish(*to_finish, late_plane[0], 0, tiles - 1)
    if direct:
        late_line = add_split(late_plane[0], swap_plane(late_plane), False, 12, finished)
    else:
        late_line = [me]
    token_grad, finished = finish(*to_finish, late_line[0], tiles - 1, 1, (token_grad,))

    counted = length * devices
    if direct:
        early = along_line(line)
        late = along_line(late_line)
        device_and_count = jnp.stack([device, jnp.int32(counted)]).astype(jnp.int32)
        *owned, norm_one, norm_two, bias_one, bias_two, stats = close(
            device_and_count, w_query, w_key, w_value, gate_attn, gate_ffn, w_in, norm_attn, norm_ffn, late, early, finished
        )
        small_grads = [v.reshape(own_rows) for v in (norm_one, norm_two, bias_one, bias_two)]
        return (result, token_grad, *owned, *small_grads, stats)

    def scatter(values):
        return lax.psum_scatter(values, AXES, scatter_dimension=0, tiled=True)

    tile = keep[0, TILES].astype(F32)
    summed = lax.psum(tile[:6] + tile[6:12], AXES)
    whole = natural(send, keep).astype(F32)
    first = scatter(natural(late_send, late_keep).astype(F32).reshape(width, 3 * width))
    owned = [first[:, k * width : (k + 1) * width] for k in range(3)]
    owned += [scatter(whole[:, k].reshape(width, width)) for k in range(3)]
    in_tiles = whole[:, 3:7].reshape(BLOCKS, 4, ROWS, BLOCKS, ROWS).transpose(0, 2, 3, 1, 4)
    owned += [scatter(in_tiles.reshape(width, hidden)), scatter(whole[:, 7:11].reshape(hidden, width))]
    shards = (w_query, w_key, w_value, gate_attn)
    norm_one = sum(row_sum(w, g)[:, 0] for w, g in zip(shards, owned[:3] + owned[4:5]))
    norm_two = (row_sum(gate_ffn, owned[5]) + row_sum(w_in, owned[6]))[:, 0]
    mean = summed[:4] / counted
    gate_stats = jnp.stack([mean[0], mean[1] - mean[0] * mean[0], mean[2], mean[3] - mean[2] * mean[2]])
    own = lax.dynamic_slice(summed, (4, device * own_rows), (2, own_rows))
    return (
        result, token_grad, *owned, norm_one / norm_attn.astype(F32), norm_two / norm_ffn.astype(F32),
        own[0], own[1], gate_stats,
    )


def solution(mesh):
    rows = P(AXES, None)
    flat = P(AXES)
    in_specs = (rows, flat) + (rows,) * 8 + (flat,) * 4 + (rows,)
    out_specs = (rows,) * 10 + (flat,) * 4 + (P(),)
    return jax.shard_map(
        per_device, mesh=mesh, in_specs=in_specs, out_specs=out_specs, check_vma=False
    )
```

```python
from functools import partial

import jax
import jax.numpy as jnp
from jax import lax
from jax.experimental import pallas as pl
from jax.experimental.pallas import tpu as pltpu
from jax.sharding import PartitionSpec as P

HEADS = 8
HEAD_DIM = 64
EPSILON = 1e-05
MASKED = -1000000000.0
AXES = ("wide", "narrow")
BF = jnp.bfloat16
F32 = jnp.float32
MIB = 1 << 20
VMEM = 60 * MIB
ANYWHERE = pl.BlockSpec(memory_space=pl.ANY)
BLOCK = 256
ROWS = 16
BLOCKS = 32
FIRST = 1536 + 128
TILES = 11
PARTS = 1


def dot(left, right):
    return jnp.dot(left, right, preferred_element_type=F32)


def dot_t(left, right):
    return lax.dot_general(left, right, (((1,), (1,)), ((), ())), preferred_element_type=F32)


def t_dot(left, right):
    return lax.dot_general(left, right, (((0,), (0,)), ((), ())), preferred_element_type=F32)


def row_mean(values):
    return jnp.mean(values, axis=-1, keepdims=True)


def normalise(values):
    offset = values - row_mean(values)
    scale = lax.rsqrt(row_mean(offset * offset) + EPSILON)
    return offset * scale, scale


def sigmoid(values):
    return 0.5 + 0.5 * jnp.tanh(0.5 * values)


def project_kernel(
    order, tokens, *refs
):
    pieces, refs = refs[:8], refs[8:]
    normed, normed_t, query, key, value, key_t, value_t, weights, small, held, sem = refs
    step = pl.program_id(0)

    @pl.when(step == 0)
    def _():
        for at in range(BLOCKS):
            place = pl.multiple_of(order[at] * ROWS, ROWS)
            pltpu.make_async_copy(
                pieces[at // 4].at[pl.ds(at % 4 * ROWS, ROWS)], held.at[pl.ds(place, ROWS)], sem
            ).start()

    unit, _ = normalise(tokens[...].astype(F32))

    @pl.when(step == 0)
    def _():
        pltpu.make_async_copy(held, held, sem).wait()
        total = jnp.zeros((ROWS, 128), F32)
        for at in range(BLOCKS):
            total = total + held[pl.ds(at * ROWS, ROWS), 1536:FIRST].astype(F32)
        for vector in range(4):
            for part in range(4):
                small[vector : vector + 1, part * 128 : (part + 1) * 128] = total[
                    vector * 4 + part : vector * 4 + part + 1
                ]
        weights[...] = held[:, :1536]

    low = (unit * small[0:1, :]).astype(BF)
    normed[...] = low
    normed_t[...] = low.T
    query[...] = (dot(low, held[:, :512]).astype(BF).astype(F32) * HEAD_DIM**-0.5).astype(BF)
    keys = dot(low, held[:, 512:1024]).astype(BF)
    key[...] = keys
    key_t[...] = keys.T
    values = dot(low, held[:, 1024:1536]).astype(BF)
    value[...] = values
    value_t[...] = values.T


def project(order, tokens, pieces):
    length, width = tokens.shape
    tile = 512
    by_rows = pl.BlockSpec((tile, width), lambda i: (i, 0))
    by_columns = pl.BlockSpec((width, tile), lambda i: (0, i))
    whole = lambda *shape: pl.BlockSpec(shape, lambda i: (0,) * len(shape))
    rows = jax.ShapeDtypeStruct((length, width), BF)
    columns = jax.ShapeDtypeStruct((width, length), BF)
    return pl.pallas_call(
        project_kernel,
        grid=(length // tile,),
        in_specs=[
            pl.BlockSpec(memory_space=pltpu.SMEM),
            by_rows,
        ] + [pl.BlockSpec(memory_space=pl.ANY)] * 8,
        out_specs=[
            by_rows, by_columns, by_rows, by_rows, by_rows, by_columns, by_columns,
            whole(width, 1536), whole(4, width),
        ],
        out_shape=[
            rows, columns, rows, rows, rows, columns, columns,
            jax.ShapeDtypeStruct((width, 1536), BF),
            jax.ShapeDtypeStruct((4, width), F32),
        ],
        scratch_shapes=[pltpu.VMEM((width, FIRST), BF), pltpu.SemaphoreType.DMA],
        compiler_params=pltpu.CompilerParams(vmem_limit_bytes=VMEM),
        cost_estimate=pl.CostEstimate(
            flops=6 * length * width * width, bytes_accessed=12 * MIB, transcendentals=length
        ),
        name="project",
    )(order, tokens, *pieces)


def bias_of(segment_row, first_key, first_query, keys):
    shape = (keys, segment_row.shape[1])
    key_at = first_key + lax.broadcasted_iota(jnp.int32, shape, 0)
    query_at = first_query + lax.broadcasted_iota(jnp.int32, shape, 1)
    return jnp.where((key_at >= segment_row) & (key_at <= query_at), 0.0, MASKED)


def parts_of(block, step):
    start = block * BLOCK
    half = BLOCK // 2
    if block is step:
        return [(start, half, 0), (start + half, half, half)]
    return [(start, BLOCK, 0)]


def keep_heads(source, target):
    for head in range(target.shape[0]):
        target[head, :, pl.ds(head % 2 * HEAD_DIM, HEAD_DIM)] = source[:, pl.ds(head * HEAD_DIM, HEAD_DIM)]


def attend_kernel(
    segment, segment_row, query_in, key_in, value_t_in, mixed_out, log_total,
    query, key, value_t, mixed, masked_query, peak, total, mix, in_sems, out_sems,
):
    length, width = query.shape
    steps = length // BLOCK
    heads = range(HEADS)

    def loads(step):
        part = pl.ds(pl.multiple_of(step * BLOCK, BLOCK), BLOCK)
        return [
            pltpu.make_async_copy(query_in.at[part], query.at[part], in_sems.at[0, step]),
            pltpu.make_async_copy(key_in.at[part], key.at[part], in_sems.at[1, step]),
            pltpu.make_async_copy(value_t_in.at[:, part], value_t.at[:, part], in_sems.at[2, step]),
        ]

    def store(step):
        part = pl.ds(pl.multiple_of(step * BLOCK, BLOCK), BLOCK)
        return pltpu.make_async_copy(mixed.at[part], mixed_out.at[part], out_sems.at[step])

    for step in range(steps):
        for copy in loads(step):
            copy.start()
    masked_query[...] = jnp.zeros(masked_query.shape, BF)
    pair = lambda head: pl.ds(head // 2 * 128, 128)
    own = lambda head: pl.ds(head * HEAD_DIM, HEAD_DIM)

    def of_queries(step, _):
        for copy in loads(step):
            copy.wait()
        here = pl.ds(pl.multiple_of(step * BLOCK, BLOCK), BLOCK)
        keep_heads(query.at[here], masked_query)
        peak[...] = jnp.full(peak.shape, -1e30, F32)
        total[...] = jnp.zeros(total.shape, F32)
        mix[...] = jnp.zeros(mix.shape, F32)
        seen = segment_row[:, here]

        def visit(block, _):
            parts = parts_of(block, step)
            rows = [pl.ds(pl.multiple_of(start, keys), keys) for start, keys, _ in parts]
            bias = [
                bias_of(seen[:, low:], start, step * BLOCK + low, keys) for start, keys, low in parts
            ]

            def widen(value, part, fill):
                low = parts[part][2]
                return jnp.concatenate([jnp.full((value.shape[0], low), fill, F32), value], axis=1) if low else value

            each = [(h, p) for h in heads for p in range(len(parts))]
            scores = {
                (h, p): dot_t(key[rows[p], pair(h)], masked_query[h, parts[p][2] :]) + bias[p] for h, p in each
            }
            old = [peak[h : h + 1, :] for h in heads]
            new = list(old)
            for h, p in each:
                highest = jnp.max(scores[h, p], axis=0, keepdims=True)
                new[h] = jnp.maximum(new[h], widen(highest, p, -1e30))
            power = {(h, p): jnp.exp(scores[h, p] - new[h][:, parts[p][2] :]) for h, p in each}
            fade = [jnp.exp(o - n) for o, n in zip(old, new)]
            high = {at: power[at].astype(BF) for at in each}
            rest = {at: (power[at] - high[at].astype(F32)).astype(BF) for at in each}
            mixes = [mix[own(h), :] * fade[h] for h in heads]
            added = [total[h : h + 1, :] * fade[h] for h in heads]
            for h, p in each:
                values = value_t[own(h), rows[p]]
                mixes[h] = mixes[h] + widen(dot(values, high[h, p]) + dot(values, rest[h, p]), p, 0.0)
                added[h] = added[h] + widen(jnp.sum(power[h, p], axis=0, keepdims=True), p, 0.0)
            for h in heads:
                peak[h : h + 1, :] = new[h]
                total[h : h + 1, :] = added[h]
                mix[own(h), :] = mixes[h]
            return 0

        first = lax.div(segment[step * BLOCK], BLOCK)
        lax.fori_loop(first, step, visit, 0)
        visit(step, 0)
        log_total[:, here] = peak[...] + jnp.log(total[...])
        for head in heads:
            mix[own(head), :] = mix[own(head), :] / total[head : head + 1, :]
        mixed[here, :] = mix[...].T
        store(step).start()
        return 0

    lax.fori_loop(0, steps, of_queries, 0)
    for step in range(steps):
        store(step).wait()


def attend(segment, segment_row, query, key, value_t):
    length, width = query.shape
    steps = length // BLOCK
    smem = pl.BlockSpec(memory_space=pltpu.SMEM)
    vmem = pl.BlockSpec(memory_space=pltpu.VMEM)
    rows = pltpu.VMEM((length, width), BF)
    return pl.pallas_call(
        attend_kernel,
        in_specs=[smem, vmem, ANYWHERE, ANYWHERE, ANYWHERE],
        out_specs=[ANYWHERE, vmem],
        out_shape=[
            jax.ShapeDtypeStruct((length, width), F32),
            jax.ShapeDtypeStruct((HEADS, length), F32),
        ],
        scratch_shapes=[
            rows,
            rows,
            pltpu.VMEM((width, length), BF),
            pltpu.VMEM((length, width), F32),
            pltpu.VMEM((HEADS, BLOCK, 128), BF),
            pltpu.VMEM((HEADS, BLOCK), F32),
            pltpu.VMEM((HEADS, BLOCK), F32),
            pltpu.VMEM((width, BLOCK), F32),
            pltpu.SemaphoreType.DMA((3, steps)),
            pltpu.SemaphoreType.DMA((steps,)),
        ],
        compiler_params=pltpu.CompilerParams(vmem_limit_bytes=VMEM),
        cost_estimate=pl.CostEstimate(
            flops=8 * length * length * width, bytes_accessed=6 * MIB, transcendentals=4 * length * length
        ),
        name="attend",
    )(segment, segment_row, query, key, value_t)


def attend_back_kernel(
    me, segment, segment_row, query_in, key_in, value_in, key_t_in, grad_in, log_total, inner_sum, normed_t_in, _after,
    grad_query, grad_key, grad_value, send, keep,
    query, key, value, grad_mixed, key_t, normed_t,
    masked_query, masked_grad, query_sum, key_sum, value_sum, low_query, low_key, low_value, staged,
    in_sems, out_sems, sems,
):
    length, width = query.shape
    steps = length // BLOCK
    heads = range(HEADS)
    by_rows = ((query_in, query), (key_in, key), (value_in, value), (grad_in, grad_mixed))

    def loads(step):
        part = pl.ds(pl.multiple_of(step * BLOCK, BLOCK), BLOCK)
        copies = [
            pltpu.make_async_copy(source.at[part], target.at[part], in_sems.at[k, step])
            for k, (source, target) in enumerate(by_rows)
        ]
        return copies + [
            pltpu.make_async_copy(key_t_in.at[:, part], key_t.at[:, part], in_sems.at[4, step])
        ]

    for step in range(steps):
        for copy in loads(step):
            copy.start()
    last_load = pltpu.make_async_copy(normed_t_in, normed_t, out_sems.at[3])
    last_load.start()
    key_sum[...] = jnp.zeros(key_sum.shape, F32)
    value_sum[...] = jnp.zeros(value_sum.shape, F32)
    masked_query[...] = jnp.zeros(masked_query.shape, BF)
    masked_grad[...] = jnp.zeros(masked_grad.shape, BF)
    pair = lambda head: pl.ds(head // 2 * 128, 128)
    own = lambda head: pl.ds(head * HEAD_DIM, HEAD_DIM)

    def of_queries(step, _):
        for copy in loads(step):
            copy.wait()
        here = pl.ds(pl.multiple_of(step * BLOCK, BLOCK), BLOCK)
        keep_heads(query.at[here], masked_query)
        keep_heads(grad_mixed.at[here], masked_grad)
        query_sum[...] = jnp.zeros(query_sum.shape, F32)
        seen = segment_row[:, here]

        def visit(block, _):
            parts = parts_of(block, step)
            rows = [pl.ds(pl.multiple_of(start, keys), keys) for start, keys, _ in parts]
            bias = [
                bias_of(seen[:, low:], start, step * BLOCK + low, keys) for start, keys, low in parts
            ]
            lows = [low for _, _, low in parts]
            each = [(h, p) for h in heads for p in range(len(parts))]
            queries = {(h, p): masked_query[h, lows[p] :] for h, p in each}
            grads = {(h, p): masked_grad[h, lows[p] :] for h, p in each}
            logs = [log_total[h : h + 1, here] for h in heads]
            inner = [inner_sum[h : h + 1, here] for h in heads]
            scores = {(h, p): dot_t(key[rows[p], pair(h)], queries[h, p]) for h, p in each}
            grad_probs = {(h, p): dot_t(value[rows[p], pair(h)], grads[h, p]) for h, p in each}
            probs = {
                (h, p): jnp.exp((scores[h, p] + bias[p]) - logs[h][:, lows[p] :]) for h, p in each
            }
            grad_scores = {
                (h, p): (probs[h, p] * (grad_probs[h, p] - inner[h][:, lows[p] :])).astype(BF)
                for h, p in each
            }
            to_value = {at: dot(probs[at].astype(BF), grads[at]) for at in each}
            to_key = {at: dot(grad_scores[at], queries[at]) for at in each}
            to_query = {(h, p): dot(key_t[own(h), rows[p]], grad_scores[h, p]) for h, p in each}
            for p in range(len(parts)):
                for h in heads[::2]:
                    value_sum[rows[p], pair(h)] += to_value[h, p] + to_value[h + 1, p]
                    key_sum[rows[p], pair(h)] += to_key[h, p] + to_key[h + 1, p]
                for h in heads:
                    query_sum[own(h), lows[p] :] += to_query[h, p]
            return 0

        first = lax.div(segment[step * BLOCK], BLOCK)
        lax.fori_loop(first, step, visit, 0)
        visit(step, 0)
        low_query[here, :] = (query_sum[...] * HEAD_DIM**-0.5).astype(BF).T
        return 0

    lax.fori_loop(0, steps, of_queries, 0)
    low_key[...] = key_sum[...].astype(BF)
    low_value[...] = value_sum[...].astype(BF)
    results = ((low_query, grad_query), (low_key, grad_key), (low_value, grad_value))
    stores = [
        pltpu.make_async_copy(source, target, out_sems.at[k])
        for k, (source, target) in enumerate(results)
    ]
    for store in stores:
        store.start()
    last_load.wait()
    for k, (source, _) in enumerate(results):
        staged[:, k * width : (k + 1) * width] = dot(normed_t[...], source[...]).astype(BF)
    hand_out(
        me[0], lambda row: staged.at[pl.ds(row, ROWS)], lambda out, at: out.at[at], send, keep, sems
    )
    wait_out(send, keep, sems)
    for store in stores:
        store.wait()


def device_at(me, half, at):
    plane, line = at // 4, at % 4
    return jnp.bitwise_xor(me, (plane * 2 + half) * 4 + line)


def hand_out(me, source_at, target_at, send, keep, sems):
    for half, target in enumerate((keep, send)):
        for at in range(BLOCKS // 2):
            place = pl.multiple_of(device_at(me, half, at) * ROWS, ROWS)
            pltpu.make_async_copy(source_at(place), target_at(target, at), sems.at[half]).start()


def wait_out(send, keep, sems):
    for half, target in enumerate((keep, send)):
        pltpu.make_async_copy(target, target, sems.at[half]).wait()


def attend_back(
    me, segment, segment_row, query, key, value, key_t, grad_mixed, log_total, inner_sum, normed_t, after
):
    length, width = query.shape
    steps = length // BLOCK
    smem = pl.BlockSpec(memory_space=pltpu.SMEM)
    vmem = pl.BlockSpec(memory_space=pltpu.VMEM)
    flat = jax.ShapeDtypeStruct((length, width), BF)
    packet = jax.ShapeDtypeStruct((BLOCKS // 2, ROWS, 3 * width), BF)
    rows, columns = pltpu.VMEM((length, width), BF), pltpu.VMEM((width, length), BF)
    return pl.pallas_call(
        attend_back_kernel,
        in_specs=[smem, smem, vmem] + [ANYWHERE] * 5 + [vmem, vmem, ANYWHERE, ANYWHERE],
        out_specs=[ANYWHERE] * 5,
        out_shape=[flat, flat, flat, packet, packet],
        scratch_shapes=[rows] * 4 + [columns] * 2 + [
            pltpu.VMEM((HEADS, BLOCK, 128), BF),
            pltpu.VMEM((HEADS, BLOCK, 128), BF),
            pltpu.VMEM((width, BLOCK), F32),
            pltpu.VMEM((length, width), F32),
            pltpu.VMEM((length, width), F32),
        ] + [rows] * 3 + [
            pltpu.VMEM((width, 3 * width), BF),
            pltpu.SemaphoreType.DMA((5, steps)),
            pltpu.SemaphoreType.DMA((4,)),
            pltpu.SemaphoreType.DMA((2,)),
        ],
        compiler_params=pltpu.CompilerParams(vmem_limit_bytes=57 * MIB),
        cost_estimate=pl.CostEstimate(
            flops=20 * length * length * width, bytes_accessed=8 * MIB, transcendentals=4 * length * length
        ),
        name="attend_back",
    )(
        me, segment, segment_row, query, key, value, key_t, grad_mixed, log_total, inner_sum, normed_t, after
    )


def feed_kernel(
    me, order, tokens, normed, normed_t, mixed, out_grad, small, *refs
):
    pieces, refs = refs[:8], refs[8:]
    result, grad_middle, zeta_one_low, grad_mixed, inner_sum, gate_attn_out, send, keep, *refs = refs
    held, held_out, grads, staged, hidden, slope, sums, *refs = refs
    mix, second, grad_feed, zeta_two_low, grad_branch, grad_inner, sems, out_sems = refs
    step = pl.program_id(0)
    last = pl.num_programs(0) - 1
    features = tokens.shape[1]
    chunks = 4
    tile = lambda k: pl.ds(k * features, features)
    w_output, gate_attn, gate_ffn, *w_in = (held.at[:, tile(k)] for k in range(3 + chunks))
    w_out = [held_out.at[k] for k in range(chunks)]
    spans = (pl.ds(0, 3 * features), pl.ds(3 * features, chunks * features))

    @pl.when(step == 0)
    def _():
        for part in range(2 + chunks):
            for at in range(BLOCKS):
                place = pl.multiple_of(order[at] * ROWS, ROWS)
                source = pieces[at // 4].at[pl.ds(at % 4 * ROWS, ROWS)]
                here = pl.ds(place, ROWS)
                if part < 2:
                    copy = (source.at[:, spans[part]], held.at[here, spans[part]])
                else:
                    copy = (source.at[:, tile(3 + chunks + part - 2)], held_out.at[part - 2, here])
                pltpu.make_async_copy(*copy, sems.at[min(part, 2)]).start()
        sums[...] = jnp.zeros(sums.shape, F32)
        grads[...] = jnp.zeros(grads.shape, F32)
        pltpu.make_async_copy(held.at[:, spans[0]], held.at[:, spans[0]], sems.at[0]).wait()
        gate_attn_out[...] = gate_attn[...]

    gain, bias_one, bias_two = small[1:2, :], small[2:3, :], small[3:4, :]

    size = tokens.shape[0] // PARTS
    parts = range(PARTS)
    rows = [pl.ds(k * size, size) for k in parts]
    total = lambda vs: sum(jnp.sum(v, axis=0, keepdims=True) for v in vs)

    exact = [mixed[r, :] for r in rows]
    for k in parts:
        mix[rows[k], :] = exact[k].astype(BF)
    branch = [dot(mix[r, :], w_output[...]) for r in rows]
    gate_one = [sigmoid(dot(normed[r, :], gate_attn[...]) + bias_one) for r in rows]
    middle = [tokens[r, :].astype(F32) + g * b for r, g, b in zip(rows, gate_one, branch)]
    unit, scale = zip(*(normalise(m) for m in middle))
    for k in parts:
        second[rows[k], :] = (unit[k] * gain).astype(BF)
    gate_two = [sigmoid(dot(second[r, :], gate_ffn[...]) + bias_two) for r in rows]

    @pl.when(step == 0)
    def _():
        pltpu.make_async_copy(held.at[:, spans[1]], held.at[:, spans[1]], sems.at[1]).wait()
        pltpu.make_async_copy(held_out, held_out, sems.at[2]).wait()

    root = (2.0 / jnp.pi) ** 0.5
    feed = [jnp.zeros((size, features), F32) for _ in parts]
    for chunk in range(chunks):
        at = pl.ds(chunk * features, features)
        inner = [dot(second[r, :], w_in[chunk][...]) for r in rows]
        for k in parts:
            square = inner[k] * inner[k]
            turn = jnp.tanh(inner[k] * (root + (root * 0.044715) * square))
            rise = 0.5 + 0.5 * turn
            value = inner[k] * rise
            slope[rows[k], at] = rise + value * (1.0 - turn) * (
                root + (3.0 * root * 0.044715) * square
            )
            low = value.astype(BF)
            hidden[rows[k], at] = low
            feed[k] = feed[k] + dot(low, w_out[chunk][...])

    grad = [out_grad[r, :].astype(F32) for r in rows]
    zeta_two = []
    for k in parts:
        result[rows[k], :] = (middle[k] + gate_two[k] * feed[k]).astype(BF)
        gated = grad[k] * gate_two[k]
        grad_feed[rows[k], :] = gated.astype(BF)
        zeta_two.append(gated * feed[k] * (1.0 - gate_two[k]))
        zeta_two_low[rows[k], :] = zeta_two[k].astype(BF)
    second_t = second[...].T
    grad_second = [dot_t(zeta_two_low[r, :], gate_ffn[...]) for r in rows]
    grads[2] += dot(second_t, zeta_two_low[...])
    for chunk in range(chunks):
        at = pl.ds(chunk * features, features)
        for k in parts:
            grad_hidden = dot_t(grad_feed[rows[k], :], w_out[chunk][...])
            grad_inner[rows[k], :] = (slope[rows[k], at] * grad_hidden).astype(BF)
            grad_second[k] = grad_second[k] + dot_t(grad_inner[rows[k], :], w_in[chunk][...])
        grads[7 + chunk] += t_dot(hidden[:, at], grad_feed[...])
        grads[3 + chunk] += dot(second_t, grad_inner[...])

    @pl.when(step == last)
    def _():
        ready = pl.ds(2, TILES - 2)
        staged[ready] = grads[ready].astype(BF)
        hand_out(
            me[0], lambda row: staged.at[ready, pl.ds(row, ROWS)], lambda out, at: out.at[at, ready],
            send, keep, out_sems,
        )

    zeta_one = []
    for k in parts:
        grad_unit = grad_second[k] * gain
        grad_mid = grad[k] + scale[k] * (
            grad_unit - row_mean(grad_unit) - unit[k] * row_mean(grad_unit * unit[k])
        )
        grad_middle[rows[k], :] = grad_mid
        gated = grad_mid * gate_one[k]
        grad_branch[rows[k], :] = gated.astype(BF)
        zeta_one.append(gated * branch[k] * (1.0 - gate_one[k]))
        zeta_one_low[rows[k], :] = zeta_one[k].astype(BF)
    head_of = lax.broadcasted_iota(jnp.int32, (HEADS, features), 1) // HEAD_DIM
    own = (head_of == lax.broadcasted_iota(jnp.int32, (HEADS, features), 0)).astype(BF)
    for k in parts:
        back = dot_t(grad_branch[rows[k], :], w_output[...]).astype(BF)
        grad_mixed[rows[k], :] = back
        product = back.astype(F32) * exact[k]
        high = product.astype(BF)
        rest = (product - high.astype(F32)).astype(BF)
        inner_sum[:, rows[k]] = dot_t(own, high) + dot_t(own, rest)
    grads[0] += t_dot(mix[...], grad_branch[...])
    grads[1] += dot(normed_t[...], zeta_one_low[...])

    sums[0:1, :] += total(gate_one)
    sums[1:2, :] += total(g * g for g in gate_one)
    sums[2:3, :] += total(gate_two)
    sums[3:4, :] += total(g * g for g in gate_two)
    sums[4:5, :] += total(zeta_one)
    sums[5:6, :] += total(zeta_two)

    @pl.when(step == last)
    def _():
        sums_tile = write_sums(sums[0:6])
        for part, (first, count) in enumerate(((0, 2), (TILES, 1))):
            ready = pl.ds(first, count)
            if part == 0:
                staged[ready] = grads[ready].astype(BF)
            else:
                staged[TILES] = jnp.concatenate([sums_tile] * BLOCKS, axis=0)
            hand_out(
                me[0], lambda row: staged.at[ready, pl.ds(row, ROWS)], lambda out, at: out.at[at, ready],
                send, keep, out_sems,
            )
        wait_out(send, keep, out_sems)


def write_sums(sums):
    high = sums.astype(BF).astype(F32)
    rows = jnp.concatenate([high, sums - high, jnp.zeros((4, sums.shape[1]), F32)], axis=0)
    return rows.astype(BF)


def read_sums(tile):
    rows = tile.astype(F32)
    return rows[0:6] + rows[6:12]


def feed_forward(me, order, tokens, normed, normed_t, mixed, out_grad, small, pieces):
    length, width = tokens.shape
    hidden = 4 * width
    tile = 512
    by_rows = pl.BlockSpec((tile, width), lambda i: (i, 0))
    anywhere = pl.BlockSpec(memory_space=pl.ANY)
    rows = jax.ShapeDtypeStruct((length, width), BF)
    half = jax.ShapeDtypeStruct((BLOCKS // 2, TILES + 1, ROWS, width), BF)
    return pl.pallas_call(
        feed_kernel,
        grid=(length // tile,),
        in_specs=[
            pl.BlockSpec(memory_space=pltpu.SMEM),
            pl.BlockSpec(memory_space=pltpu.SMEM),
            by_rows, by_rows,
            pl.BlockSpec((width, tile), lambda i: (0, i)),
            by_rows, by_rows,
            pl.BlockSpec((4, width), lambda i: (0, 0)),
        ] + [anywhere] * 8,
        out_specs=[
            by_rows, by_rows, by_rows, by_rows,
            pl.BlockSpec((HEADS, tile), lambda i: (0, i)),
            pl.BlockSpec((width, width), lambda i: (0, 0)),
            anywhere, anywhere,
        ],
        out_shape=[
            rows,
            jax.ShapeDtypeStruct((length, width), F32),
            rows,
            rows,
            jax.ShapeDtypeStruct((HEADS, length), F32),
            jax.ShapeDtypeStruct((width, width), BF),
            half,
            half,
        ],
        scratch_shapes=[
            pltpu.VMEM((width, 7 * width), BF),
            pltpu.VMEM((4, width, width), BF),
            pltpu.VMEM((TILES, width, width), F32),
            pltpu.VMEM((TILES + 1, width, width), BF),
            pltpu.VMEM((tile, hidden), BF),
            pltpu.VMEM((tile, hidden), F32),
            pltpu.VMEM((8, width), F32),
        ] + [pltpu.VMEM((tile, width), BF)] * 6 + [
            pltpu.SemaphoreType.DMA((3,)),
            pltpu.SemaphoreType.DMA((2,)),
        ],
        compiler_params=pltpu.CompilerParams(vmem_limit_bytes=VMEM),
        cost_estimate=pl.CostEstimate(
            flops=6 * length * width * (3 * width + 2 * hidden), bytes_accessed=24 * MIB, transcendentals=length * hidden
        ),
        name="feed_forward",
    )(me, order, tokens, normed, normed_t, mixed, out_grad, small, *pieces)


def finish_kernel(tokens, zeta_one_low, grad_middle, weights, gate_attn, small, *refs):
    grads, (token_grad, finished) = refs[:3], refs[-2:]
    finished[...] = jnp.zeros(finished.shape, F32)
    width = tokens.shape[1]
    total = dot_t(zeta_one_low[...], gate_attn[...])
    for which, grad in enumerate(grads):
        total = total + dot_t(grad[...], weights[:, which * width : (which + 1) * width])
    unit, scale = normalise(tokens[...].astype(F32))
    grad_unit = total * small[0:1, :]
    token_grad[...] = grad_middle[...] + scale * (
        grad_unit - row_mean(grad_unit) - unit * row_mean(grad_unit * unit)
    )


def finish(tokens, zeta_one_low, grad_middle, weights, gate_attn, small, grads, after, first, count, before=()):
    length, width = tokens.shape
    tile = 512
    by_rows = pl.BlockSpec((tile, width), lambda i: (i + first, 0))
    whole = lambda *shape: pl.BlockSpec(shape, lambda i: (0, 0))
    return pl.pallas_call(
        finish_kernel,
        grid=(count,),
        in_specs=[by_rows] * 3 + [whole(width, 3 * width), whole(width, width), whole(4, width)]
        + [by_rows] * 3
        + [ANYWHERE] * (1 + len(before)),
        out_specs=[by_rows, whole(8, 128)],
        out_shape=[
            jax.ShapeDtypeStruct((length, width), F32),
            jax.ShapeDtypeStruct((8, 128), F32),
        ],
        input_output_aliases={10: 0} if before else {},
        compiler_params=pltpu.CompilerParams(vmem_limit_bytes=VMEM),
        cost_estimate=pl.CostEstimate(
            flops=8 * tile * count * width * width, bytes_accessed=5 * MIB * count, transcendentals=tile
        ),
        name="finish",
    )(tokens, zeta_one_low, grad_middle, weights, gate_attn, small, *grads, after, *before)


def row_sum(weight, grad):
    return jnp.sum(weight.astype(F32) * grad, axis=1, keepdims=True)


def in_order(features):
    unit = lax.broadcasted_iota(jnp.int32, (features, features), 0)
    column = lax.broadcasted_iota(jnp.int32, (features, features), 1)
    group, inside = column // 128, column % 128
    return (unit == inside // ROWS * 64 + group * ROWS + inside % ROWS).astype(BF)


def close_kernel(device, query, key, value, gate_attn, gate_ffn, w_in, gain_one, gain_two, *refs):
    late, early, refs = refs[:4], refs[4:8], refs[9:]
    *square_grads, grad_in, grad_out, norm_one, norm_two, bias_one, bias_two, stats = refs
    grad_query, grad_key, grad_value, grad_output, grad_gate_attn, grad_gate_ffn = square_grads
    width = query.shape[1]
    tile = lambda k: sum(p[pl.ds(k * ROWS, ROWS), :].astype(F32) for p in early)
    total = jnp.zeros((ROWS, 1), F32)
    for k, (weight, out) in enumerate(((query, grad_query), (key, grad_key), (value, grad_value))):
        grad = sum(p[:, pl.ds(k * width, width)].astype(F32) for p in late)
        out[...] = grad
        total = total + row_sum(weight[...], grad)
    grad_output[...] = tile(0)
    grad = tile(1)
    grad_gate_attn[...] = grad
    total = total + row_sum(gate_attn[...], grad)
    grad = tile(2)
    grad_gate_ffn[...] = grad
    other = row_sum(gate_ffn[...], grad)
    order = in_order(width)
    tiles = [tile(3 + k) for k in range(4)]
    for part in range(4):
        columns = pl.ds(part * width, width)
        grad = jnp.concatenate([t[:, part * 128 : (part + 1) * 128] for t in tiles], axis=1)
        high = grad.astype(BF)
        grad = dot_t(high, order) + dot_t((grad - high.astype(F32)).astype(BF), order)
        grad_in[:, columns] = grad
        other = other + row_sum(w_in[:, columns], grad)
    for group in range(4):
        grad_out[pl.ds(group * ROWS, ROWS), :] = tile(7 + group)

    def as_row(column, gain):
        eye = lax.broadcasted_iota(jnp.int32, (ROWS, ROWS), 0) == lax.broadcasted_iota(
            jnp.int32, (ROWS, ROWS), 1
        )
        return jnp.sum(jnp.where(eye, column, 0.0), axis=0, keepdims=True) / gain

    norm_one[...] = as_row(total, gain_one[...].astype(F32)[None, :])
    norm_two[...] = as_row(other, gain_two[...].astype(F32)[None, :])
    summed = sum(read_sums(p[pl.ds(TILES * ROWS, ROWS), :]) for p in early)
    mean = summed / device[1].astype(F32)
    stats[0:1, :] = mean[0:1]
    stats[1:2, :] = mean[1:2] - mean[0:1] * mean[0:1]
    stats[2:3, :] = mean[2:3]
    stats[3:4, :] = mean[3:4] - mean[2:3] * mean[2:3]
    both = jnp.concatenate([summed[4:6], jnp.zeros((6, width), F32)], axis=0)
    moved = pltpu.roll(both, lax.rem(width - device[0] * ROWS, width), 1)
    bias_one[...] = moved[0:1, :ROWS]
    bias_two[...] = moved[1:2, :ROWS]


def close(device, query, key, value, gate_attn, gate_ffn, w_in, gain_one, gain_two, late, early, after):
    width, wide = query.shape[1], w_in.shape[1]
    vmem = pl.BlockSpec(memory_space=pltpu.VMEM)
    square = jax.ShapeDtypeStruct((ROWS, width), F32)
    vector = jax.ShapeDtypeStruct((1, ROWS), F32)
    outs = [square] * 6 + [
        jax.ShapeDtypeStruct((ROWS, wide), F32),
        jax.ShapeDtypeStruct((4 * ROWS, width), F32),
    ] + [vector] * 4 + [jax.ShapeDtypeStruct((4, width), F32)]
    whole = lambda array: pl.BlockSpec(array.shape, lambda i: (0,) * len(array.shape))
    return pl.pallas_call(
        close_kernel,
        grid=(1,),
        in_specs=[pl.BlockSpec(memory_space=pltpu.SMEM)]
        + [whole(a) for a in (query, key, value, gate_attn, gate_ffn, w_in)]
        + [vmem] * 10
        + [ANYWHERE],
        out_specs=[whole(a) for a in outs],
        out_shape=outs,
        compiler_params=pltpu.CompilerParams(vmem_limit_bytes=VMEM),
        name="close",
    )(device, query, key, value, gate_attn, gate_ffn, w_in, gain_one, gain_two, *late, *early, after)


def swap(values, axis, bits):
    count = lax.axis_size(axis)
    return lax.ppermute(values, axis, [(i, i ^ bits) for i in range(count)])


def gather_pieces(values):
    line = jnp.concatenate([values] + [swap(values, "narrow", k) for k in (1, 2, 3)])
    return [line] + [swap(line, "wide", 2 * k) for k in (1, 2, 3)]


def both_cores(near):
    return list(near) + [swap(piece, "wide", 1) for piece in near]


def hold_kernel(*refs):
    pass


def hold(arrays, after):
    count = len(arrays)
    return pl.pallas_call(
        hold_kernel,
        in_specs=[ANYWHERE] * (count + len(after)),
        out_specs=[ANYWHERE] * count,
        out_shape=[jax.ShapeDtypeStruct(a.shape, a.dtype) for a in arrays],
        input_output_aliases={k: k for k in range(count)},
        compiler_params=pltpu.CompilerParams(vmem_limit_bytes=4 * MIB),
        name="hold",
    )(*arrays, *after)


def add_kernel(own, *refs, terms, sums):
    arrived, targets, (held, sems) = refs[: terms - 1], refs[terms : terms + 4], refs[terms + 4 :]
    each, rows, _ = targets[0].shape
    copies = []
    for part in range(4):
        here = pl.ds(part * each, each)
        copies.append(pltpu.make_async_copy(own.at[here], held.at[here], sems.at[part]))
        copies[-1].start()
    tile = pl.ds(rows - ROWS, ROWS)
    for part, target in enumerate(targets):
        copies[part].wait()
        for block in range(each):
            at = part * each + block
            target[block] = sum((a[at].astype(F32) for a in arrived), held[at].astype(F32)).astype(BF)
        if sums and part == 0:
            added = write_sums(sum((read_sums(a[0, tile, :]) for a in arrived), read_sums(held[0, tile, :])))
        if sums:
            for block in range(each):
                target[block, tile, :] = added


def add_split(own, arrived, sums, limit, after):
    blocks, rows, columns = own.shape
    vmem = pl.BlockSpec(memory_space=pltpu.VMEM)
    return pl.pallas_call(
        partial(add_kernel, terms=1 + len(arrived), sums=sums),
        in_specs=[ANYWHERE] + [vmem] * len(arrived) + [ANYWHERE],
        out_specs=[vmem] * 4,
        out_shape=[jax.ShapeDtypeStruct((blocks // 4, rows, columns), BF)] * 4,
        scratch_shapes=[pltpu.VMEM(own.shape, BF), pltpu.SemaphoreType.DMA((4,))],
        compiler_params=pltpu.CompilerParams(vmem_limit_bytes=int(limit * MIB)),
        name="add_split",
    )(own, *arrived, after)


def add_core(send, keep, sums, limit, after):
    return add_split(keep, [swap(send, "wide", 1)], sums, limit, after)


def swap_plane(plane):
    return [swap(plane[k], "wide", 2 * k) for k in (1, 2, 3)]


def along_line(line):
    return [line[0][0]] + [swap(line[k], "narrow", k)[0] for k in (1, 2, 3)]


def natural(send, keep):
    halves = jnp.stack([keep, send]).reshape(2, 4, 4, *keep.shape[1:])
    return halves.swapaxes(0, 1).reshape(BLOCKS, *keep.shape[1:])


def pack_first(device, vectors, shards, first):
    own = vectors[0].shape[0]
    column, row = lax.rem(device[0] * own, 128), lax.div(device[0] * own, 128)
    at = 0
    for shard in shards:
        first[:, at : at + shard.shape[1]] = shard[...]
        at += shard.shape[1]
    values = jnp.concatenate([v[...].astype(F32)[None, :] for v in vectors], axis=0)
    wide = pltpu.roll(jnp.concatenate([values, jnp.zeros((4, 128 - own), F32)], axis=1), column, 1)
    place = lax.broadcasted_iota(jnp.int32, (ROWS, 128), 0)
    tile = jnp.zeros((ROWS, 128), F32)
    for vector in range(4):
        tile = jnp.where(place == vector * 4 + row, wide[vector : vector + 1], tile)
    first[:, at:] = tile.astype(BF)


def pack_kernel(device, *refs):
    vectors, shards, (first, rest) = refs[:4], refs[4:-2], refs[-2:]
    pack_first(device, vectors, shards[:3], first)
    pack_rest(*shards[3:], rest)


def pack_rest(w_output, gate_attn, gate_ffn, w_in, w_out, rest):
    width = w_output.shape[1]
    tile = lambda k: pl.ds(k * width, width)
    for k, shard in enumerate((w_output, gate_attn, gate_ffn)):
        rest[:, tile(k)] = shard[...]
    order = in_order(width)
    for part in range(4):
        moved = dot(w_in[:, tile(part)], order).astype(BF)
        for group in range(4):
            rest[:, pl.ds((3 + group) * width + part * 128, 128)] = moved[:, group * 128 : (group + 1) * 128]
    for group in range(4):
        rest[:, tile(7 + group)] = w_out[group * ROWS : (group + 1) * ROWS, :]


def pack(device, vectors, *shards):
    vmem = pl.BlockSpec(memory_space=pltpu.VMEM)
    return pl.pallas_call(
        pack_kernel,
        in_specs=[pl.BlockSpec(memory_space=pltpu.SMEM)] + [vmem] * (4 + len(shards)),
        out_shape=[
            jax.ShapeDtypeStruct((ROWS, FIRST), BF),
            jax.ShapeDtypeStruct((ROWS, TILES * shards[0].shape[1]), BF),
        ],
        compiler_params=pltpu.CompilerParams(vmem_limit_bytes=VMEM),
        name="pack",
    )(device, *vectors, *shards)


def per_device(
    tokens, segment, w_query, w_key, w_value, w_output, gate_attn, gate_ffn, w_in, w_out,
    norm_attn, norm_ffn, bias_attn, bias_ffn, out_grad,
):
    wide, narrow = lax.axis_size("wide"), lax.axis_size("narrow")
    devices = wide * narrow
    length, width = tokens.shape
    hidden = w_in.shape[1]
    own_rows = w_query.shape[0]
    device = lax.axis_index("wide") * narrow + lax.axis_index("narrow")
    direct = wide == 8 and narrow == 4 and own_rows == ROWS
    vectors = (norm_attn, norm_ffn, bias_attn, bias_ffn)

    def gather(values):
        return lax.all_gather(values, AXES, axis=0, tiled=True)

    if direct:
        me = device.astype(jnp.int32).reshape(1)
        first, rest = pack(
            me, vectors, w_query, w_key, w_value, w_output, gate_attn, gate_ffn, w_in, w_out
        )
        pieces = both_cores(gather_pieces(first))
        rest_near = gather_pieces(rest)
        order = jnp.concatenate(
            [
                jnp.bitwise_xor(device, (jnp.arange(16) // 4 * 2 + half) * 4 + jnp.arange(16) % 4)
                for half in range(2)
            ]
        ).astype(jnp.int32)
    else:
        full = gather(jnp.stack(vectors, axis=1))
        tile = jnp.zeros((BLOCKS, ROWS, 128), BF).at[0].set(full.T.reshape(ROWS, 128))
        first = jnp.concatenate(
            [gather(w_query), gather(w_key), gather(w_value), tile.reshape(BLOCKS * ROWS, 128)], axis=1
        ).reshape(8, 4 * ROWS, FIRST)
        squares = [gather(w).reshape(BLOCKS, 1, ROWS, width) for w in (w_output, gate_attn, gate_ffn)]
        in_tiles = gather(w_in).reshape(BLOCKS, ROWS, BLOCKS, 4, ROWS).transpose(0, 3, 1, 2, 4)
        packet = jnp.concatenate(
            squares + [in_tiles.reshape(BLOCKS, 4, ROWS, width), gather(w_out).reshape(BLOCKS, 4, ROWS, width)],
            axis=1,
        ).swapaxes(1, 2).reshape(8, 4 * ROWS, TILES * width)
        pieces = [first[k] for k in range(8)]
        rest_pieces = [packet[k] for k in range(8)]
        me = jnp.zeros((1,), jnp.int32)
        order = jnp.arange(BLOCKS, dtype=jnp.int32)

    segment_row = segment.reshape(1, length)
    normed, normed_t, query, key, value, key_t, value_t, weights, small = project(order, tokens, pieces)
    mixed, log_total = attend(segment, segment_row, query, key, value_t)
    if direct:
        rest_pieces = both_cores(rest_near[:1] + list(hold(rest_near[1:], [log_total])))
    result, grad_middle, zeta_one_low, grad_mixed, inner_sum, whole_gate, send, keep = feed_forward(
        me, order, tokens, normed, normed_t, mixed, out_grad, small, rest_pieces
    )
    if direct:
        flat = lambda values: values.reshape(BLOCKS // 2, (TILES + 1) * ROWS, width)
        plane = add_core(flat(send), flat(keep), True, 12, me)
    else:
        plane = [me]
    *grads, late_send, late_keep = attend_back(
        me, segment, segment_row, query, key, value, key_t, grad_mixed, log_total, inner_sum,
        normed_t, plane[0],
    )
    if direct:
        received = swap_plane(plane)
        (late_send,) = hold([late_send], received)
        line = add_split(plane[0], received, True, 12, me)
        late_plane = add_core(late_send, late_keep, False, 12, line[0])
    else:
        late_plane = [me]
    to_finish = (tokens, zeta_one_low, grad_middle, weights, whole_gate, small, grads)
    tiles = length // 512
    token_grad, finished = finish(*to_finish, late_plane[0], 0, tiles - 1)
    if direct:
        late_line = add_split(late_plane[0], swap_plane(late_plane), False, 12, finished)
    else:
        late_line = [me]
    token_grad, finished = finish(*to_finish, late_line[0], tiles - 1, 1, (token_grad,))

    counted = length * devices
    if direct:
        early = along_line(line)
        late = along_line(late_line)
        device_and_count = jnp.stack([device, jnp.int32(counted)]).astype(jnp.int32)
        *owned, norm_one, norm_two, bias_one, bias_two, stats = close(
            device_and_count, w_query, w_key, w_value, gate_attn, gate_ffn, w_in, norm_attn, norm_ffn, late, early, finished
        )
        small_grads = [v.reshape(own_rows) for v in (norm_one, norm_two, bias_one, bias_two)]
        return (result, token_grad, *owned, *small_grads, stats)

    def scatter(values):
        return lax.psum_scatter(values, AXES, scatter_dimension=0, tiled=True)

    tile = keep[0, TILES].astype(F32)
    summed = lax.psum(tile[:6] + tile[6:12], AXES)
    whole = natural(send, keep).astype(F32)
    first = scatter(natural(late_send, late_keep).astype(F32).reshape(width, 3 * width))
    owned = [first[:, k * width : (k + 1) * width] for k in range(3)]
    owned += [scatter(whole[:, k].reshape(width, width)) for k in range(3)]
    in_tiles = whole[:, 3:7].reshape(BLOCKS, 4, ROWS, BLOCKS, ROWS).transpose(0, 2, 3, 1, 4)
    owned += [scatter(in_tiles.reshape(width, hidden)), scatter(whole[:, 7:11].reshape(hidden, width))]
    shards = (w_query, w_key, w_value, gate_attn)
    norm_one = sum(row_sum(w, g)[:, 0] for w, g in zip(shards, owned[:3] + owned[4:5]))
    norm_two = (row_sum(gate_ffn, owned[5]) + row_sum(w_in, owned[6]))[:, 0]
    mean = summed[:4] / counted
    gate_stats = jnp.stack([mean[0], mean[1] - mean[0] * mean[0], mean[2], mean[3] - mean[2] * mean[2]])
    own = lax.dynamic_slice(summed, (4, device * own_rows), (2, own_rows))
    return (
        result, token_grad, *owned, norm_one / norm_attn.astype(F32), norm_two / norm_ffn.astype(F32),
        own[0], own[1], gate_stats,
    )


def solution(mesh):
    rows = P(AXES, None)
    flat = P(AXES)
    in_specs = (rows, flat) + (rows,) * 8 + (flat,) * 4 + (rows,)
    out_specs = (rows,) * 10 + (flat,) * 4 + (P(),)
    return jax.shard_map(
        per_device, mesh=mesh, in_specs=in_specs, out_specs=out_specs, check_vma=False
    )
```

```python
from functools import partial

import jax
import jax.numpy as jnp
from jax import lax
from jax.experimental import pallas as pl
from jax.experimental.pallas import tpu as pltpu
from jax.sharding import PartitionSpec as P

HEADS = 8
HEAD_DIM = 64
EPSILON = 1e-05
MASKED = -1000000000.0
AXES = ("wide", "narrow")
BF = jnp.bfloat16
F32 = jnp.float32
MIB = 1 << 20
VMEM = 60 * MIB
ANYWHERE = pl.BlockSpec(memory_space=pl.ANY)
BLOCK = 256
ROWS = 16
BLOCKS = 32
FIRST = 1536 + 128
TILES = 11
PARTS = 1


def dot(left, right):
    return jnp.dot(left, right, preferred_element_type=F32)


def dot_t(left, right):
    return lax.dot_general(left, right, (((1,), (1,)), ((), ())), preferred_element_type=F32)


def t_dot(left, right):
    return lax.dot_general(left, right, (((0,), (0,)), ((), ())), preferred_element_type=F32)


def row_mean(values):
    return jnp.mean(values, axis=-1, keepdims=True)


def normalise(values):
    offset = values - row_mean(values)
    scale = lax.rsqrt(row_mean(offset * offset) + EPSILON)
    return offset * scale, scale


def sigmoid(values):
    return 0.5 + 0.5 * jnp.tanh(0.5 * values)


def project_kernel(
    order, tokens, *refs
):
    pieces, refs = refs[:8], refs[8:]
    normed, normed_t, query, key, value, key_t, value_t, weights, small, held, sem = refs
    step = pl.program_id(0)

    @pl.when(step == 0)
    def _():
        for at in range(BLOCKS):
            place = pl.multiple_of(order[at] * ROWS, ROWS)
            pltpu.make_async_copy(
                pieces[at // 4].at[pl.ds(at % 4 * ROWS, ROWS)], held.at[pl.ds(place, ROWS)], sem
            ).start()

    unit, _ = normalise(tokens[...].astype(F32))

    @pl.when(step == 0)
    def _():
        pltpu.make_async_copy(held, held, sem).wait()
        total = jnp.zeros((ROWS, 128), F32)
        for at in range(BLOCKS):
            total = total + held[pl.ds(at * ROWS, ROWS), 1536:FIRST].astype(F32)
        for vector in range(4):
            for part in range(4):
                small[vector : vector + 1, part * 128 : (part + 1) * 128] = total[
                    vector * 4 + part : vector * 4 + part + 1
                ]
        weights[...] = held[:, :1536]

    low = (unit * small[0:1, :]).astype(BF)
    normed[...] = low
    normed_t[...] = low.T
    query[...] = (dot(low, held[:, :512]).astype(BF).astype(F32) * HEAD_DIM**-0.5).astype(BF)
    keys = dot(low, held[:, 512:1024]).astype(BF)
    key[...] = keys
    key_t[...] = keys.T
    values = dot(low, held[:, 1024:1536]).astype(BF)
    value[...] = values
    value_t[...] = values.T


def project(order, tokens, pieces):
    length, width = tokens.shape
    tile = 512
    by_rows = pl.BlockSpec((tile, width), lambda i: (i, 0))
    by_columns = pl.BlockSpec((width, tile), lambda i: (0, i))
    whole = lambda *shape: pl.BlockSpec(shape, lambda i: (0,) * len(shape))
    rows = jax.ShapeDtypeStruct((length, width), BF)
    columns = jax.ShapeDtypeStruct((width, length), BF)
    return pl.pallas_call(
        project_kernel,
        grid=(length // tile,),
        in_specs=[
            pl.BlockSpec(memory_space=pltpu.SMEM),
            by_rows,
        ] + [pl.BlockSpec(memory_space=pl.ANY)] * 8,
        out_specs=[
            by_rows, by_columns, by_rows, by_rows, by_rows, by_columns, by_columns,
            whole(width, 1536), whole(4, width),
        ],
        out_shape=[
            rows, columns, rows, rows, rows, columns, columns,
            jax.ShapeDtypeStruct((width, 1536), BF),
            jax.ShapeDtypeStruct((4, width), F32),
        ],
        scratch_shapes=[pltpu.VMEM((width, FIRST), BF), pltpu.SemaphoreType.DMA],
        compiler_params=pltpu.CompilerParams(vmem_limit_bytes=VMEM),
        cost_estimate=pl.CostEstimate(
            flops=6 * length * width * width, bytes_accessed=12 * MIB, transcendentals=length
        ),
        name="project",
    )(order, tokens, *pieces)


def bias_of(segment_row, first_key, first_query, keys):
    shape = (keys, segment_row.shape[1])
    key_at = first_key + lax.broadcasted_iota(jnp.int32, shape, 0)
    query_at = first_query + lax.broadcasted_iota(jnp.int32, shape, 1)
    return jnp.where((key_at >= segment_row) & (key_at <= query_at), 0.0, MASKED)


def parts_of(block, step):
    start = block * BLOCK
    half = BLOCK // 2
    if block is step:
        return [(start, half, 0), (start + half, half, half)]
    return [(start, BLOCK, 0)]


def keep_heads(source, target):
    for head in range(target.shape[0]):
        target[head, :, pl.ds(head % 2 * HEAD_DIM, HEAD_DIM)] = source[:, pl.ds(head * HEAD_DIM, HEAD_DIM)]


def attend_kernel(
    segment, segment_row, query_in, key_in, value_t_in, mixed_out, log_total,
    query, key, value_t, mixed, masked_query, peak, total, mix, in_sems, out_sems,
):
    length, width = query.shape
    steps = length // BLOCK
    heads = range(HEADS)

    def loads(step):
        part = pl.ds(pl.multiple_of(step * BLOCK, BLOCK), BLOCK)
        return [
            pltpu.make_async_copy(query_in.at[part], query.at[part], in_sems.at[0, step]),
            pltpu.make_async_copy(key_in.at[part], key.at[part], in_sems.at[1, step]),
            pltpu.make_async_copy(value_t_in.at[:, part], value_t.at[:, part], in_sems.at[2, step]),
        ]

    def store(step):
        part = pl.ds(pl.multiple_of(step * BLOCK, BLOCK), BLOCK)
        return pltpu.make_async_copy(mixed.at[part], mixed_out.at[part], out_sems.at[step])

    for step in range(steps):
        for copy in loads(step):
            copy.start()
    masked_query[...] = jnp.zeros(masked_query.shape, BF)
    pair = lambda head: pl.ds(head // 2 * 128, 128)
    own = lambda head: pl.ds(head * HEAD_DIM, HEAD_DIM)

    def of_queries(step, _):
        for copy in loads(step):
            copy.wait()
        here = pl.ds(pl.multiple_of(step * BLOCK, BLOCK), BLOCK)
        keep_heads(query.at[here], masked_query)
        peak[...] = jnp.full(peak.shape, -1e30, F32)
        total[...] = jnp.zeros(total.shape, F32)
        mix[...] = jnp.zeros(mix.shape, F32)
        seen = segment_row[:, here]

        def visit(block, _):
            parts = parts_of(block, step)
            rows = [pl.ds(pl.multiple_of(start, keys), keys) for start, keys, _ in parts]
            bias = [
                bias_of(seen[:, low:], start, step * BLOCK + low, keys) for start, keys, low in parts
            ]

            def widen(value, part, fill):
                low = parts[part][2]
                return jnp.concatenate([jnp.full((value.shape[0], low), fill, F32), value], axis=1) if low else value

            each = [(h, p) for h in heads for p in range(len(parts))]
            scores = {
                (h, p): dot_t(key[rows[p], pair(h)], masked_query[h, parts[p][2] :]) + bias[p] for h, p in each
            }
            old = [peak[h : h + 1, :] for h in heads]
            new = list(old)
            for h, p in each:
                highest = jnp.max(scores[h, p], axis=0, keepdims=True)
                new[h] = jnp.maximum(new[h], widen(highest, p, -1e30))
            power = {(h, p): jnp.exp(scores[h, p] - new[h][:, parts[p][2] :]) for h, p in each}
            fade = [jnp.exp(o - n) for o, n in zip(old, new)]
            high = {at: power[at].astype(BF) for at in each}
            rest = {at: (power[at] - high[at].astype(F32)).astype(BF) for at in each}
            mixes = [mix[own(h), :] * fade[h] for h in heads]
            added = [total[h : h + 1, :] * fade[h] for h in heads]
            for h, p in each:
                values = value_t[own(h), rows[p]]
                mixes[h] = mixes[h] + widen(dot(values, high[h, p]) + dot(values, rest[h, p]), p, 0.0)
                added[h] = added[h] + widen(jnp.sum(power[h, p], axis=0, keepdims=True), p, 0.0)
            for h in heads:
                peak[h : h + 1, :] = new[h]
                total[h : h + 1, :] = added[h]
                mix[own(h), :] = mixes[h]
            return 0

        first = lax.div(segment[step * BLOCK], BLOCK)
        lax.fori_loop(first, step, visit, 0)
        visit(step, 0)
        log_total[:, here] = peak[...] + jnp.log(total[...])
        for head in heads:
            mix[own(head), :] = mix[own(head), :] / total[head : head + 1, :]
        mixed[here, :] = mix[...].T
        store(step).start()
        return 0

    lax.fori_loop(0, steps, of_queries, 0)
    for step in range(steps):
        store(step).wait()


def attend(segment, segment_row, query, key, value_t):
    length, width = query.shape
    steps = length // BLOCK
    smem = pl.BlockSpec(memory_space=pltpu.SMEM)
    vmem = pl.BlockSpec(memory_space=pltpu.VMEM)
    rows = pltpu.VMEM((length, width), BF)
    return pl.pallas_call(
        attend_kernel,
        in_specs=[smem, vmem, ANYWHERE, ANYWHERE, ANYWHERE],
        out_specs=[ANYWHERE, vmem],
        out_shape=[
            jax.ShapeDtypeStruct((length, width), F32),
            jax.ShapeDtypeStruct((HEADS, length), F32),
        ],
        scratch_shapes=[
            rows,
            rows,
            pltpu.VMEM((width, length), BF),
            pltpu.VMEM((length, width), F32),
            pltpu.VMEM((HEADS, BLOCK, 128), BF),
            pltpu.VMEM((HEADS, BLOCK), F32),
            pltpu.VMEM((HEADS, BLOCK), F32),
            pltpu.VMEM((width, BLOCK), F32),
            pltpu.SemaphoreType.DMA((3, steps)),
            pltpu.SemaphoreType.DMA((steps,)),
        ],
        compiler_params=pltpu.CompilerParams(vmem_limit_bytes=VMEM),
        cost_estimate=pl.CostEstimate(
            flops=8 * length * length * width, bytes_accessed=6 * MIB, transcendentals=4 * length * length
        ),
        name="attend",
    )(segment, segment_row, query, key, value_t)


def attend_back_kernel(
    me, segment, segment_row, query_in, key_in, value_in, key_t_in, grad_in, log_total, inner_sum, normed_t_in, _after,
    grad_query, grad_key, grad_value, send, keep,
    query, key, value, grad_mixed, key_t, normed_t,
    masked_query, masked_grad, query_sum, key_sum, value_sum, low_query, low_key, low_value, staged,
    in_sems, out_sems, sems,
):
    length, width = query.shape
    steps = length // BLOCK
    heads = range(HEADS)
    by_rows = ((query_in, query), (key_in, key), (value_in, value), (grad_in, grad_mixed))

    def loads(step):
        part = pl.ds(pl.multiple_of(step * BLOCK, BLOCK), BLOCK)
        copies = [
            pltpu.make_async_copy(source.at[part], target.at[part], in_sems.at[k, step])
            for k, (source, target) in enumerate(by_rows)
        ]
        return copies + [
            pltpu.make_async_copy(key_t_in.at[:, part], key_t.at[:, part], in_sems.at[4, step])
        ]

    for step in range(steps):
        for copy in loads(step):
            copy.start()
    last_load = pltpu.make_async_copy(normed_t_in, normed_t, out_sems.at[3])
    last_load.start()
    key_sum[...] = jnp.zeros(key_sum.shape, F32)
    value_sum[...] = jnp.zeros(value_sum.shape, F32)
    masked_query[...] = jnp.zeros(masked_query.shape, BF)
    masked_grad[...] = jnp.zeros(masked_grad.shape, BF)
    pair = lambda head: pl.ds(head // 2 * 128, 128)
    own = lambda head: pl.ds(head * HEAD_DIM, HEAD_DIM)

    def of_queries(step, _):
        for copy in loads(step):
            copy.wait()
        here = pl.ds(pl.multiple_of(step * BLOCK, BLOCK), BLOCK)
        keep_heads(query.at[here], masked_query)
        keep_heads(grad_mixed.at[here], masked_grad)
        query_sum[...] = jnp.zeros(query_sum.shape, F32)
        seen = segment_row[:, here]

        def visit(block, _):
            parts = parts_of(block, step)
            rows = [pl.ds(pl.multiple_of(start, keys), keys) for start, keys, _ in parts]
            bias = [
                bias_of(seen[:, low:], start, step * BLOCK + low, keys) for start, keys, low in parts
            ]
            lows = [low for _, _, low in parts]
            each = [(h, p) for h in heads for p in range(len(parts))]
            queries = {(h, p): masked_query[h, lows[p] :] for h, p in each}
            grads = {(h, p): masked_grad[h, lows[p] :] for h, p in each}
            logs = [log_total[h : h + 1, here] for h in heads]
            inner = [inner_sum[h : h + 1, here] for h in heads]
            scores = {(h, p): dot_t(key[rows[p], pair(h)], queries[h, p]) for h, p in each}
            grad_probs = {(h, p): dot_t(value[rows[p], pair(h)], grads[h, p]) for h, p in each}
            probs = {
                (h, p): jnp.exp((scores[h, p] + bias[p]) - logs[h][:, lows[p] :]) for h, p in each
            }
            grad_scores = {
                (h, p): (probs[h, p] * (grad_probs[h, p] - inner[h][:, lows[p] :])).astype(BF)
                for h, p in each
            }
            to_value = {at: dot(probs[at].astype(BF), grads[at]) for at in each}
            to_key = {at: dot(grad_scores[at], queries[at]) for at in each}
            to_query = {(h, p): dot(key_t[own(h), rows[p]], grad_scores[h, p]) for h, p in each}
            for p in range(len(parts)):
                for h in heads[::2]:
                    value_sum[rows[p], pair(h)] += to_value[h, p] + to_value[h + 1, p]
                    key_sum[rows[p], pair(h)] += to_key[h, p] + to_key[h + 1, p]
                for h in heads:
                    query_sum[own(h), lows[p] :] += to_query[h, p]
            return 0

        first = lax.div(segment[step * BLOCK], BLOCK)
        lax.fori_loop(first, step, visit, 0)
        visit(step, 0)
        low_query[here, :] = (query_sum[...] * HEAD_DIM**-0.5).astype(BF).T
        return 0

    lax.fori_loop(0, steps, of_queries, 0)
    low_key[...] = key_sum[...].astype(BF)
    low_value[...] = value_sum[...].astype(BF)
    results = ((low_query, grad_query), (low_key, grad_key), (low_value, grad_value))
    stores = [
        pltpu.make_async_copy(source, target, out_sems.at[k])
        for k, (source, target) in enumerate(results)
    ]
    for store in stores:
        store.start()
    last_load.wait()
    for k, (source, _) in enumerate(results):
        staged[:, k * width : (k + 1) * width] = dot(normed_t[...], source[...]).astype(BF)
    hand_out(
        me[0], lambda row: staged.at[pl.ds(row, ROWS)], lambda out, at: out.at[at], send, keep, sems
    )
    wait_out(send, keep, sems)
    for store in stores:
        store.wait()


def device_at(me, half, at):
    plane, line = at // 4, at % 4
    return jnp.bitwise_xor(me, (plane * 2 + half) * 4 + line)


def hand_out(me, source_at, target_at, send, keep, sems):
    for half, target in enumerate((keep, send)):
        for at in range(BLOCKS // 2):
            place = pl.multiple_of(device_at(me, half, at) * ROWS, ROWS)
            pltpu.make_async_copy(source_at(place), target_at(target, at), sems.at[half]).start()


def wait_out(send, keep, sems):
    for half, target in enumerate((keep, send)):
        pltpu.make_async_copy(target, target, sems.at[half]).wait()


def attend_back(
    me, segment, segment_row, query, key, value, key_t, grad_mixed, log_total, inner_sum, normed_t, after
):
    length, width = query.shape
    steps = length // BLOCK
    smem = pl.BlockSpec(memory_space=pltpu.SMEM)
    vmem = pl.BlockSpec(memory_space=pltpu.VMEM)
    flat = jax.ShapeDtypeStruct((length, width), BF)
    packet = jax.ShapeDtypeStruct((BLOCKS // 2, ROWS, 3 * width), BF)
    rows, columns = pltpu.VMEM((length, width), BF), pltpu.VMEM((width, length), BF)
    return pl.pallas_call(
        attend_back_kernel,
        in_specs=[smem, smem, vmem] + [ANYWHERE] * 5 + [vmem, vmem, ANYWHERE, ANYWHERE],
        out_specs=[ANYWHERE] * 5,
        out_shape=[flat, flat, flat, packet, packet],
        scratch_shapes=[rows] * 4 + [columns] * 2 + [
            pltpu.VMEM((HEADS, BLOCK, 128), BF),
            pltpu.VMEM((HEADS, BLOCK, 128), BF),
            pltpu.VMEM((width, BLOCK), F32),
            pltpu.VMEM((length, width), F32),
            pltpu.VMEM((length, width), F32),
        ] + [rows] * 3 + [
            pltpu.VMEM((width, 3 * width), BF),
            pltpu.SemaphoreType.DMA((5, steps)),
            pltpu.SemaphoreType.DMA((4,)),
            pltpu.SemaphoreType.DMA((2,)),
        ],
        compiler_params=pltpu.CompilerParams(vmem_limit_bytes=57 * MIB),
        cost_estimate=pl.CostEstimate(
            flops=20 * length * length * width, bytes_accessed=8 * MIB, transcendentals=4 * length * length
        ),
        name="attend_back",
    )(
        me, segment, segment_row, query, key, value, key_t, grad_mixed, log_total, inner_sum, normed_t, after
    )


def feed_kernel(
    me, order, tokens, normed, normed_t, mixed, out_grad, small, *refs
):
    pieces, refs = refs[:8], refs[8:]
    result, grad_middle, zeta_one_low, grad_mixed, inner_sum, gate_attn_out, send, keep, *refs = refs
    held, held_out, grads, staged, hidden, slope, sums, *refs = refs
    mix, second, grad_feed, zeta_two_low, grad_branch, grad_inner, sems, out_sems = refs
    step = pl.program_id(0)
    last = pl.num_programs(0) - 1
    features = tokens.shape[1]
    chunks = 4
    tile = lambda k: pl.ds(k * features, features)
    w_output, gate_attn, gate_ffn, *w_in = (held.at[:, tile(k)] for k in range(3 + chunks))
    w_out = [held_out.at[k] for k in range(chunks)]
    spans = (pl.ds(0, 3 * features), pl.ds(3 * features, chunks * features))

    @pl.when(step == 0)
    def _():
        for part in range(2 + chunks):
            for at in range(BLOCKS):
                place = pl.multiple_of(order[at] * ROWS, ROWS)
                source = pieces[at // 4].at[pl.ds(at % 4 * ROWS, ROWS)]
                here = pl.ds(place, ROWS)
                if part < 2:
                    copy = (source.at[:, spans[part]], held.at[here, spans[part]])
                else:
                    copy = (source.at[:, tile(3 + chunks + part - 2)], held_out.at[part - 2, here])
                pltpu.make_async_copy(*copy, sems.at[min(part, 2)]).start()
        sums[...] = jnp.zeros(sums.shape, F32)
        grads[...] = jnp.zeros(grads.shape, F32)
        pltpu.make_async_copy(held.at[:, spans[0]], held.at[:, spans[0]], sems.at[0]).wait()
        gate_attn_out[...] = gate_attn[...]

    gain, bias_one, bias_two = small[1:2, :], small[2:3, :], small[3:4, :]

    size = tokens.shape[0] // PARTS
    parts = range(PARTS)
    rows = [pl.ds(k * size, size) for k in parts]
    total = lambda vs: sum(jnp.sum(v, axis=0, keepdims=True) for v in vs)

    exact = [mixed[r, :] for r in rows]
    for k in parts:
        mix[rows[k], :] = exact[k].astype(BF)
    branch = [dot(mix[r, :], w_output[...]) for r in rows]
    gate_one = [sigmoid(dot(normed[r, :], gate_attn[...]) + bias_one) for r in rows]
    middle = [tokens[r, :].astype(F32) + g * b for r, g, b in zip(rows, gate_one, branch)]
    unit, scale = zip(*(normalise(m) for m in middle))
    for k in parts:
        second[rows[k], :] = (unit[k] * gain).astype(BF)
    gate_two = [sigmoid(dot(second[r, :], gate_ffn[...]) + bias_two) for r in rows]

    @pl.when(step == 0)
    def _():
        pltpu.make_async_copy(held.at[:, spans[1]], held.at[:, spans[1]], sems.at[1]).wait()
        pltpu.make_async_copy(held_out, held_out, sems.at[2]).wait()

    root = (2.0 / jnp.pi) ** 0.5
    feed = [jnp.zeros((size, features), F32) for _ in parts]
    for chunk in range(chunks):
        at = pl.ds(chunk * features, features)
        inner = [dot(second[r, :], w_in[chunk][...]) for r in rows]
        for k in parts:
            square = inner[k] * inner[k]
            turn = jnp.tanh(inner[k] * (root + (root * 0.044715) * square))
            rise = 0.5 + 0.5 * turn
            value = inner[k] * rise
            slope[rows[k], at] = rise + value * (1.0 - turn) * (
                root + (3.0 * root * 0.044715) * square
            )
            low = value.astype(BF)
            hidden[rows[k], at] = low
            feed[k] = feed[k] + dot(low, w_out[chunk][...])

    grad = [out_grad[r, :].astype(F32) for r in rows]
    zeta_two = []
    for k in parts:
        result[rows[k], :] = (middle[k] + gate_two[k] * feed[k]).astype(BF)
        gated = grad[k] * gate_two[k]
        grad_feed[rows[k], :] = gated.astype(BF)
        zeta_two.append(gated * feed[k] * (1.0 - gate_two[k]))
        zeta_two_low[rows[k], :] = zeta_two[k].astype(BF)
    second_t = second[...].T
    grad_second = [dot_t(zeta_two_low[r, :], gate_ffn[...]) for r in rows]
    grads[2] += dot(second_t, zeta_two_low[...])
    for chunk in range(chunks):
        at = pl.ds(chunk * features, features)
        for k in parts:
            grad_hidden = dot_t(grad_feed[rows[k], :], w_out[chunk][...])
            grad_inner[rows[k], :] = (slope[rows[k], at] * grad_hidden).astype(BF)
            grad_second[k] = grad_second[k] + dot_t(grad_inner[rows[k], :], w_in[chunk][...])
        grads[7 + chunk] += t_dot(hidden[:, at], grad_feed[...])
        grads[3 + chunk] += dot(second_t, grad_inner[...])

    @pl.when(step == last)
    def _():
        ready = pl.ds(2, TILES - 2)
        staged[ready] = grads[ready].astype(BF)
        hand_out(
            me[0], lambda row: staged.at[ready, pl.ds(row, ROWS)], lambda out, at: out.at[at, ready],
            send, keep, out_sems,
        )

    zeta_one = []
    for k in parts:
        grad_unit = grad_second[k] * gain
        grad_mid = grad[k] + scale[k] * (
            grad_unit - row_mean(grad_unit) - unit[k] * row_mean(grad_unit * unit[k])
        )
        grad_middle[rows[k], :] = grad_mid
        gated = grad_mid * gate_one[k]
        grad_branch[rows[k], :] = gated.astype(BF)
        zeta_one.append(gated * branch[k] * (1.0 - gate_one[k]))
        zeta_one_low[rows[k], :] = zeta_one[k].astype(BF)
    head_of = lax.broadcasted_iota(jnp.int32, (HEADS, features), 1) // HEAD_DIM
    own = (head_of == lax.broadcasted_iota(jnp.int32, (HEADS, features), 0)).astype(BF)
    for k in parts:
        back = dot_t(grad_branch[rows[k], :], w_output[...]).astype(BF)
        grad_mixed[rows[k], :] = back
        product = back.astype(F32) * exact[k]
        high = product.astype(BF)
        rest = (product - high.astype(F32)).astype(BF)
        inner_sum[:, rows[k]] = dot_t(own, high) + dot_t(own, rest)
    grads[0] += t_dot(mix[...], grad_branch[...])
    grads[1] += dot(normed_t[...], zeta_one_low[...])

    sums[0:1, :] += total(gate_one)
    sums[1:2, :] += total(g * g for g in gate_one)
    sums[2:3, :] += total(gate_two)
    sums[3:4, :] += total(g * g for g in gate_two)
    sums[4:5, :] += total(zeta_one)
    sums[5:6, :] += total(zeta_two)

    @pl.when(step == last)
    def _():
        sums_tile = write_sums(sums[0:6])
        for part, (first, count) in enumerate(((0, 2), (TILES, 1))):
            ready = pl.ds(first, count)
            if part == 0:
                staged[ready] = grads[ready].astype(BF)
            else:
                staged[TILES] = jnp.concatenate([sums_tile] * BLOCKS, axis=0)
            hand_out(
                me[0], lambda row: staged.at[ready, pl.ds(row, ROWS)], lambda out, at: out.at[at, ready],
                send, keep, out_sems,
            )
        wait_out(send, keep, out_sems)


def write_sums(sums):
    high = sums.astype(BF).astype(F32)
    rows = jnp.concatenate([high, sums - high, jnp.zeros((4, sums.shape[1]), F32)], axis=0)
    return rows.astype(BF)


def read_sums(tile):
    rows = tile.astype(F32)
    return rows[0:6] + rows[6:12]


def feed_forward(me, order, tokens, normed, normed_t, mixed, out_grad, small, pieces):
    length, width = tokens.shape
    hidden = 4 * width
    tile = 512
    by_rows = pl.BlockSpec((tile, width), lambda i: (i, 0))
    anywhere = pl.BlockSpec(memory_space=pl.ANY)
    rows = jax.ShapeDtypeStruct((length, width), BF)
    half = jax.ShapeDtypeStruct((BLOCKS // 2, TILES + 1, ROWS, width), BF)
    return pl.pallas_call(
        feed_kernel,
        grid=(length // tile,),
        in_specs=[
            pl.BlockSpec(memory_space=pltpu.SMEM),
            pl.BlockSpec(memory_space=pltpu.SMEM),
            by_rows, by_rows,
            pl.BlockSpec((width, tile), lambda i: (0, i)),
            by_rows, by_rows,
            pl.BlockSpec((4, width), lambda i: (0, 0)),
        ] + [anywhere] * 8,
        out_specs=[
            by_rows, by_rows, by_rows, by_rows,
            pl.BlockSpec((HEADS, tile), lambda i: (0, i)),
            pl.BlockSpec((width, width), lambda i: (0, 0)),
            anywhere, anywhere,
        ],
        out_shape=[
            rows,
            jax.ShapeDtypeStruct((length, width), F32),
            rows,
            rows,
            jax.ShapeDtypeStruct((HEADS, length), F32),
            jax.ShapeDtypeStruct((width, width), BF),
            half,
            half,
        ],
        scratch_shapes=[
            pltpu.VMEM((width, 7 * width), BF),
            pltpu.VMEM((4, width, width), BF),
            pltpu.VMEM((TILES, width, width), F32),
            pltpu.VMEM((TILES + 1, width, width), BF),
            pltpu.VMEM((tile, hidden), BF),
            pltpu.VMEM((tile, hidden), F32),
            pltpu.VMEM((8, width), F32),
        ] + [pltpu.VMEM((tile, width), BF)] * 6 + [
            pltpu.SemaphoreType.DMA((3,)),
            pltpu.SemaphoreType.DMA((2,)),
        ],
        compiler_params=pltpu.CompilerParams(vmem_limit_bytes=VMEM),
        cost_estimate=pl.CostEstimate(
            flops=6 * length * width * (3 * width + 2 * hidden), bytes_accessed=24 * MIB, transcendentals=length * hidden
        ),
        name="feed_forward",
    )(me, order, tokens, normed, normed_t, mixed, out_grad, small, *pieces)


def finish_kernel(tokens, zeta_one_low, grad_middle, weights, gate_attn, small, *refs):
    grads, (token_grad, finished) = refs[:3], refs[-2:]
    finished[...] = jnp.zeros(finished.shape, F32)
    width = tokens.shape[1]
    total = dot_t(zeta_one_low[...], gate_attn[...])
    for which, grad in enumerate(grads):
        total = total + dot_t(grad[...], weights[:, which * width : (which + 1) * width])
    unit, scale = normalise(tokens[...].astype(F32))
    grad_unit = total * small[0:1, :]
    token_grad[...] = grad_middle[...] + scale * (
        grad_unit - row_mean(grad_unit) - unit * row_mean(grad_unit * unit)
    )


def finish(tokens, zeta_one_low, grad_middle, weights, gate_attn, small, grads, after, first, count, before=()):
    length, width = tokens.shape
    tile = 512
    by_rows = pl.BlockSpec((tile, width), lambda i: (i + first, 0))
    whole = lambda *shape: pl.BlockSpec(shape, lambda i: (0, 0))
    return pl.pallas_call(
        finish_kernel,
        grid=(count,),
        in_specs=[by_rows] * 3 + [whole(width, 3 * width), whole(width, width), whole(4, width)]
        + [by_rows] * 3
        + [ANYWHERE] * (1 + len(before)),
        out_specs=[by_rows, whole(8, 128)],
        out_shape=[
            jax.ShapeDtypeStruct((length, width), F32),
            jax.ShapeDtypeStruct((8, 128), F32),
        ],
        input_output_aliases={10: 0} if before else {},
        compiler_params=pltpu.CompilerParams(vmem_limit_bytes=VMEM),
        cost_estimate=pl.CostEstimate(
            flops=8 * tile * count * width * width, bytes_accessed=5 * MIB * count, transcendentals=tile
        ),
        name="finish",
    )(tokens, zeta_one_low, grad_middle, weights, gate_attn, small, *grads, after, *before)


def row_sum(weight, grad):
    return jnp.sum(weight.astype(F32) * grad, axis=1, keepdims=True)


def in_order(features):
    unit = lax.broadcasted_iota(jnp.int32, (features, features), 0)
    column = lax.broadcasted_iota(jnp.int32, (features, features), 1)
    group, inside = column // 128, column % 128
    return (unit == inside // ROWS * 64 + group * ROWS + inside % ROWS).astype(BF)


def close_kernel(device, query, key, value, gate_attn, gate_ffn, w_in, gain_one, gain_two, *refs):
    late, early, refs = refs[:4], refs[4:8], refs[9:]
    *square_grads, grad_in, grad_out, norm_one, norm_two, bias_one, bias_two, stats = refs
    grad_query, grad_key, grad_value, grad_output, grad_gate_attn, grad_gate_ffn = square_grads
    width = query.shape[1]
    tile = lambda k: sum(p[pl.ds(k * ROWS, ROWS), :].astype(F32) for p in early)
    total = jnp.zeros((ROWS, 1), F32)
    for k, (weight, out) in enumerate(((query, grad_query), (key, grad_key), (value, grad_value))):
        grad = sum(p[:, pl.ds(k * width, width)].astype(F32) for p in late)
        out[...] = grad
        total = total + row_sum(weight[...], grad)
    grad_output[...] = tile(0)
    grad = tile(1)
    grad_gate_attn[...] = grad
    total = total + row_sum(gate_attn[...], grad)
    grad = tile(2)
    grad_gate_ffn[...] = grad
    other = row_sum(gate_ffn[...], grad)
    tiles = [tile(3 + k) for k in range(4)]
    spread = jnp.concatenate(
        [
            jnp.concatenate([t[:, part * 128 : (part + 1) * 128] for t in tiles], axis=1)
            for part in range(4)
        ],
        axis=0,
    )
    high = spread.astype(BF)
    low = (spread - high.astype(F32)).astype(BF)
    moved = dot_t(jnp.concatenate([high, low], axis=0), in_order(width))
    moved = moved[: 4 * ROWS] + moved[4 * ROWS :]
    for part in range(4):
        columns = pl.ds(part * width, width)
        grad = moved[part * ROWS : (part + 1) * ROWS]
        grad_in[:, columns] = grad
        other = other + row_sum(w_in[:, columns], grad)
    for group in range(4):
        grad_out[pl.ds(group * ROWS, ROWS), :] = tile(7 + group)

    def as_row(column, gain):
        eye = lax.broadcasted_iota(jnp.int32, (ROWS, ROWS), 0) == lax.broadcasted_iota(
            jnp.int32, (ROWS, ROWS), 1
        )
        return jnp.sum(jnp.where(eye, column, 0.0), axis=0, keepdims=True) / gain

    norm_one[...] = as_row(total, gain_one[...].astype(F32)[None, :])
    norm_two[...] = as_row(other, gain_two[...].astype(F32)[None, :])
    summed = sum(read_sums(p[pl.ds(TILES * ROWS, ROWS), :]) for p in early)
    mean = summed / device[1].astype(F32)
    stats[0:1, :] = mean[0:1]
    stats[1:2, :] = mean[1:2] - mean[0:1] * mean[0:1]
    stats[2:3, :] = mean[2:3]
    stats[3:4, :] = mean[3:4] - mean[2:3] * mean[2:3]
    both = jnp.concatenate([summed[4:6], jnp.zeros((6, width), F32)], axis=0)
    moved = pltpu.roll(both, lax.rem(width - device[0] * ROWS, width), 1)
    bias_one[...] = moved[0:1, :ROWS]
    bias_two[...] = moved[1:2, :ROWS]


def close(device, query, key, value, gate_attn, gate_ffn, w_in, gain_one, gain_two, late, early, after):
    width, wide = query.shape[1], w_in.shape[1]
    vmem = pl.BlockSpec(memory_space=pltpu.VMEM)
    square = jax.ShapeDtypeStruct((ROWS, width), F32)
    vector = jax.ShapeDtypeStruct((1, ROWS), F32)
    outs = [square] * 6 + [
        jax.ShapeDtypeStruct((ROWS, wide), F32),
        jax.ShapeDtypeStruct((4 * ROWS, width), F32),
    ] + [vector] * 4 + [jax.ShapeDtypeStruct((4, width), F32)]
    whole = lambda array: pl.BlockSpec(array.shape, lambda i: (0,) * len(array.shape))
    return pl.pallas_call(
        close_kernel,
        grid=(1,),
        in_specs=[pl.BlockSpec(memory_space=pltpu.SMEM)]
        + [whole(a) for a in (query, key, value, gate_attn, gate_ffn, w_in)]
        + [vmem] * 10
        + [ANYWHERE],
        out_specs=[whole(a) for a in outs],
        out_shape=outs,
        compiler_params=pltpu.CompilerParams(vmem_limit_bytes=VMEM),
        name="close",
    )(device, query, key, value, gate_attn, gate_ffn, w_in, gain_one, gain_two, *late, *early, after)


def swap(values, axis, bits):
    count = lax.axis_size(axis)
    return lax.ppermute(values, axis, [(i, i ^ bits) for i in range(count)])


def gather_pieces(values):
    line = jnp.concatenate([values] + [swap(values, "narrow", k) for k in (1, 2, 3)])
    return [line] + [swap(line, "wide", 2 * k) for k in (1, 2, 3)]


def both_cores(near):
    return list(near) + [swap(piece, "wide", 1) for piece in near]


def hold_kernel(*refs):
    pass


def hold(arrays, after):
    count = len(arrays)
    return pl.pallas_call(
        hold_kernel,
        in_specs=[ANYWHERE] * (count + len(after)),
        out_specs=[ANYWHERE] * count,
        out_shape=[jax.ShapeDtypeStruct(a.shape, a.dtype) for a in arrays],
        input_output_aliases={k: k for k in range(count)},
        compiler_params=pltpu.CompilerParams(vmem_limit_bytes=4 * MIB),
        name="hold",
    )(*arrays, *after)


def add_kernel(own, *refs, terms, sums):
    arrived, targets, (held, sems) = refs[: terms - 1], refs[terms : terms + 4], refs[terms + 4 :]
    each, rows, _ = targets[0].shape
    copies = []
    for part in range(4):
        here = pl.ds(part * each, each)
        copies.append(pltpu.make_async_copy(own.at[here], held.at[here], sems.at[part]))
        copies[-1].start()
    tile = pl.ds(rows - ROWS, ROWS)
    for part, target in enumerate(targets):
        copies[part].wait()
        for block in range(each):
            at = part * each + block
            target[block] = sum((a[at].astype(F32) for a in arrived), held[at].astype(F32)).astype(BF)
        if sums and part == 0:
            added = write_sums(sum((read_sums(a[0, tile, :]) for a in arrived), read_sums(held[0, tile, :])))
        if sums:
            for block in range(each):
                target[block, tile, :] = added


def add_split(own, arrived, sums, limit, after):
    blocks, rows, columns = own.shape
    vmem = pl.BlockSpec(memory_space=pltpu.VMEM)
    return pl.pallas_call(
        partial(add_kernel, terms=1 + len(arrived), sums=sums),
        in_specs=[ANYWHERE] + [vmem] * len(arrived) + [ANYWHERE],
        out_specs=[vmem] * 4,
        out_shape=[jax.ShapeDtypeStruct((blocks // 4, rows, columns), BF)] * 4,
        scratch_shapes=[pltpu.VMEM(own.shape, BF), pltpu.SemaphoreType.DMA((4,))],
        compiler_params=pltpu.CompilerParams(vmem_limit_bytes=int(limit * MIB)),
        name="add_split",
    )(own, *arrived, after)


def add_core(send, keep, sums, limit, after):
    return add_split(keep, [swap(send, "wide", 1)], sums, limit, after)


def swap_plane(plane):
    return [swap(plane[k], "wide", 2 * k) for k in (1, 2, 3)]


def along_line(line):
    return [line[0][0]] + [swap(line[k], "narrow", k)[0] for k in (1, 2, 3)]


def natural(send, keep):
    halves = jnp.stack([keep, send]).reshape(2, 4, 4, *keep.shape[1:])
    return halves.swapaxes(0, 1).reshape(BLOCKS, *keep.shape[1:])


def pack_first(device, vectors, shards, first):
    own = vectors[0].shape[0]
    column, row = lax.rem(device[0] * own, 128), lax.div(device[0] * own, 128)
    at = 0
    for shard in shards:
        first[:, at : at + shard.shape[1]] = shard[...]
        at += shard.shape[1]
    values = jnp.concatenate([v[...].astype(F32)[None, :] for v in vectors], axis=0)
    wide = pltpu.roll(jnp.concatenate([values, jnp.zeros((4, 128 - own), F32)], axis=1), column, 1)
    place = lax.broadcasted_iota(jnp.int32, (ROWS, 128), 0)
    tile = jnp.zeros((ROWS, 128), F32)
    for vector in range(4):
        tile = jnp.where(place == vector * 4 + row, wide[vector : vector + 1], tile)
    first[:, at:] = tile.astype(BF)


def pack_kernel(device, *refs):
    vectors, shards, (first, rest) = refs[:4], refs[4:-2], refs[-2:]
    pack_first(device, vectors, shards[:3], first)
    pack_rest(*shards[3:], rest)


def pack_rest(w_output, gate_attn, gate_ffn, w_in, w_out, rest):
    width = w_output.shape[1]
    tile = lambda k: pl.ds(k * width, width)
    for k, shard in enumerate((w_output, gate_attn, gate_ffn)):
        rest[:, tile(k)] = shard[...]
    moved = dot(jnp.concatenate([w_in[:, tile(part)] for part in range(4)], axis=0), in_order(width))
    moved = moved.astype(BF)
    for part in range(4):
        for group in range(4):
            rest[:, pl.ds((3 + group) * width + part * 128, 128)] = moved[
                part * ROWS : (part + 1) * ROWS, group * 128 : (group + 1) * 128
            ]
    for group in range(4):
        rest[:, tile(7 + group)] = w_out[group * ROWS : (group + 1) * ROWS, :]


def pack(device, vectors, *shards):
    vmem = pl.BlockSpec(memory_space=pltpu.VMEM)
    return pl.pallas_call(
        pack_kernel,
        in_specs=[pl.BlockSpec(memory_space=pltpu.SMEM)] + [vmem] * (4 + len(shards)),
        out_shape=[
            jax.ShapeDtypeStruct((ROWS, FIRST), BF),
            jax.ShapeDtypeStruct((ROWS, TILES * shards[0].shape[1]), BF),
        ],
        compiler_params=pltpu.CompilerParams(vmem_limit_bytes=VMEM),
        name="pack",
    )(device, *vectors, *shards)


def per_device(
    tokens, segment, w_query, w_key, w_value, w_output, gate_attn, gate_ffn, w_in, w_out,
    norm_attn, norm_ffn, bias_attn, bias_ffn, out_grad,
):
    wide, narrow = lax.axis_size("wide"), lax.axis_size("narrow")
    devices = wide * narrow
    length, width = tokens.shape
    hidden = w_in.shape[1]
    own_rows = w_query.shape[0]
    device = lax.axis_index("wide") * narrow + lax.axis_index("narrow")
    direct = wide == 8 and narrow == 4 and own_rows == ROWS
    vectors = (norm_attn, norm_ffn, bias_attn, bias_ffn)

    def gather(values):
        return lax.all_gather(values, AXES, axis=0, tiled=True)

    if direct:
        me = device.astype(jnp.int32).reshape(1)
        first, rest = pack(
            me, vectors, w_query, w_key, w_value, w_output, gate_attn, gate_ffn, w_in, w_out
        )
        pieces = both_cores(gather_pieces(first))
        rest_near = gather_pieces(rest)
        order = jnp.concatenate(
            [
                jnp.bitwise_xor(device, (jnp.arange(16) // 4 * 2 + half) * 4 + jnp.arange(16) % 4)
                for half in range(2)
            ]
        ).astype(jnp.int32)
    else:
        full = gather(jnp.stack(vectors, axis=1))
        tile = jnp.zeros((BLOCKS, ROWS, 128), BF).at[0].set(full.T.reshape(ROWS, 128))
        first = jnp.concatenate(
            [gather(w_query), gather(w_key), gather(w_value), tile.reshape(BLOCKS * ROWS, 128)], axis=1
        ).reshape(8, 4 * ROWS, FIRST)
        squares = [gather(w).reshape(BLOCKS, 1, ROWS, width) for w in (w_output, gate_attn, gate_ffn)]
        in_tiles = gather(w_in).reshape(BLOCKS, ROWS, BLOCKS, 4, ROWS).transpose(0, 3, 1, 2, 4)
        packet = jnp.concatenate(
            squares + [in_tiles.reshape(BLOCKS, 4, ROWS, width), gather(w_out).reshape(BLOCKS, 4, ROWS, width)],
            axis=1,
        ).swapaxes(1, 2).reshape(8, 4 * ROWS, TILES * width)
        pieces = [first[k] for k in range(8)]
        rest_pieces = [packet[k] for k in range(8)]
        me = jnp.zeros((1,), jnp.int32)
        order = jnp.arange(BLOCKS, dtype=jnp.int32)

    segment_row = segment.reshape(1, length)
    normed, normed_t, query, key, value, key_t, value_t, weights, small = project(order, tokens, pieces)
    mixed, log_total = attend(segment, segment_row, query, key, value_t)
    if direct:
        rest_pieces = both_cores(rest_near[:1] + list(hold(rest_near[1:], [log_total])))
    result, grad_middle, zeta_one_low, grad_mixed, inner_sum, whole_gate, send, keep = feed_forward(
        me, order, tokens, normed, normed_t, mixed, out_grad, small, rest_pieces
    )
    if direct:
        flat = lambda values: values.reshape(BLOCKS // 2, (TILES + 1) * ROWS, width)
        plane = add_core(flat(send), flat(keep), True, 12, me)
    else:
        plane = [me]
    *grads, late_send, late_keep = attend_back(
        me, segment, segment_row, query, key, value, key_t, grad_mixed, log_total, inner_sum,
        normed_t, plane[0],
    )
    if direct:
        received = swap_plane(plane)
        (late_send,) = hold([late_send], received)
        line = add_split(plane[0], received, True, 12, me)
        late_plane = add_core(late_send, late_keep, False, 12, line[0])
    else:
        late_plane = [me]
    to_finish = (tokens, zeta_one_low, grad_middle, weights, whole_gate, small, grads)
    tiles = length // 512
    token_grad, finished = finish(*to_finish, late_plane[0], 0, tiles - 1)
    if direct:
        late_line = add_split(late_plane[0], swap_plane(late_plane), False, 12, finished)
    else:
        late_line = [me]
    token_grad, finished = finish(*to_finish, late_line[0], tiles - 1, 1, (token_grad,))

    counted = length * devices
    if direct:
        early = along_line(line)
        late = along_line(late_line)
        device_and_count = jnp.stack([device, jnp.int32(counted)]).astype(jnp.int32)
        *owned, norm_one, norm_two, bias_one, bias_two, stats = close(
            device_and_count, w_query, w_key, w_value, gate_attn, gate_ffn, w_in, norm_attn, norm_ffn, late, early, finished
        )
        small_grads = [v.reshape(own_rows) for v in (norm_one, norm_two, bias_one, bias_two)]
        return (result, token_grad, *owned, *small_grads, stats)

    def scatter(values):
        return lax.psum_scatter(values, AXES, scatter_dimension=0, tiled=True)

    tile = keep[0, TILES].astype(F32)
    summed = lax.psum(tile[:6] + tile[6:12], AXES)
    whole = natural(send, keep).astype(F32)
    first = scatter(natural(late_send, late_keep).astype(F32).reshape(width, 3 * width))
    owned = [first[:, k * width : (k + 1) * width] for k in range(3)]
    owned += [scatter(whole[:, k].reshape(width, width)) for k in range(3)]
    in_tiles = whole[:, 3:7].reshape(BLOCKS, 4, ROWS, BLOCKS, ROWS).transpose(0, 2, 3, 1, 4)
    owned += [scatter(in_tiles.reshape(width, hidden)), scatter(whole[:, 7:11].reshape(hidden, width))]
    shards = (w_query, w_key, w_value, gate_attn)
    norm_one = sum(row_sum(w, g)[:, 0] for w, g in zip(shards, owned[:3] + owned[4:5]))
    norm_two = (row_sum(gate_ffn, owned[5]) + row_sum(w_in, owned[6]))[:, 0]
    mean = summed[:4] / counted
    gate_stats = jnp.stack([mean[0], mean[1] - mean[0] * mean[0], mean[2], mean[3] - mean[2] * mean[2]])
    own = lax.dynamic_slice(summed, (4, device * own_rows), (2, own_rows))
    return (
        result, token_grad, *owned, norm_one / norm_attn.astype(F32), norm_two / norm_ffn.astype(F32),
        own[0], own[1], gate_stats,
    )


def solution(mesh):
    rows = P(AXES, None)
    flat = P(AXES)
    in_specs = (rows, flat) + (rows,) * 8 + (flat,) * 4 + (rows,)
    out_specs = (rows,) * 10 + (flat,) * 4 + (P(),)
    return jax.shard_map(
        per_device, mesh=mesh, in_specs=in_specs, out_specs=out_specs, check_vma=False
    )
```
